32 devices in a mesh: expert: 8 (over z, x), shard: 4 (over y, core).
Axes of the slice: x: 2, y: 2, z: 4, core: 2. Of those that a mesh axis runs over, the one named last changes fastest.
Arguments:
- tokens: int32 [8192], replicated, may hold values from 0 to 50303
- prefix: int32 [32], P(('expert', 'shard')), may hold values from 1 to 256
- routes: int32 [8192, 4], P(('expert', 'shard')), may hold values from 0 to 7, all different within a row; in each aligned block of 256 rows (0 to 255, 256 to 511, ...) at most 144 rows name the same one
- picked: int32 [256], P(('expert', 'shard')), may hold values from 0 to 255, as said below
- loss_ids: int32 [256, 65], replicated, may hold values from 0 to 50303, as said below
- teacher_logits: float32 [256, 64], replicated, may hold values from -8 to 8
- embedding: float32 [50304, 1024], P(None, ('expert', 'shard')), may hold values from -6 to 6
- embedding_mean: float32 [50304, 1024], P(None, ('expert', 'shard')), may hold values from -4.5776367e-05 to 4.5776367e-05
- embedding_square: float32 [50304, 1024], P(None, ('expert', 'shard')), may hold values from 9.313226e-10 to 9.313226e-08
- attention: float32 [2, 1024, 4096], P(None, ('expert', 'shard'))
- attention_mean: float32 [2, 1024, 4096], P(None, ('expert', 'shard')), may hold values from -0.01171875 to 0.01171875
- attention_square: float32 [2, 1024, 4096], P(None, ('expert', 'shard')), may hold values from 2.3841858e-07 to 2.3841858e-05
- router: float32 [2, 1024, 8], P(None, ('expert', 'shard')), may hold values from -0.375 to 0.375
- router_mean: float32 [2, 1024, 8], P(None, ('expert', 'shard')), may hold values from -0.01171875 to 0.01171875
- router_square: float32 [2, 1024, 8], P(None, ('expert', 'shard')), may hold values from 3.8146973e-06 to 0.00038146973
- norm_gains: float32 [9, 1024], P(None, ('expert', 'shard')), may hold values from 0.5 to 1.5
- gains_mean: float32 [9, 1024], P(None, ('expert', 'shard')), may hold values from -0.01171875 to 0.01171875
- gains_square: float32 [9, 1024], P(None, ('expert', 'shard')), may hold values from 3.8146973e-06 to 0.00038146973
- expert_up: float32 [8, 2, 1024, 1024], P('expert', None, 'shard'), may hold values from -0.1875 to 0.1875
- upward_mean: float32 [8, 2, 1024, 1024], P('expert', None, 'shard'), may hold values from -0.0014648438 to 0.0014648438
- upward_square: float32 [8, 2, 1024, 1024], P('expert', None, 'shard'), may hold values from 2.9802322e-08 to 2.9802322e-06
- expert_down: float32 [8, 2, 512, 1024], P('expert', None, None, 'shard'), may hold values from -2 to 2
- downward_mean: float32 [8, 2, 512, 1024], P('expert', None, None, 'shard'), may hold values from -9.1552734e-05 to 9.1552734e-05
- downward_square: float32 [8, 2, 512, 1024], P('expert', None, None, 'shard'), may hold values from 2.3283064e-10 to 2.3283064e-08
- output_table: float32 [50304, 1024], P(('expert', 'shard')), may hold values from -0.375 to 0.375
- table_mean: float32 [50304, 1024], P(('expert', 'shard')), may hold values from -1.4909351e-05 to 1.4909351e-05
- table_square: float32 [50304, 1024], P(('expert', 'shard')), may hold values from 6.1746875e-12 to 6.1746874e-10
Outputs:
- loss_value: float32 [], replicated
- embedding_mean_next: float32 [50304, 1024], P(None, ('expert', 'shard'))
- embedding_square_next: float32 [50304, 1024], P(None, ('expert', 'shard'))
- embedding_update: float32 [50304, 1024], P(None, ('expert', 'shard'))
- attention_mean_next: float32 [2, 1024, 4096], P(None, ('expert', 'shard'))
- attention_square_next: float32 [2, 1024, 4096], P(None, ('expert', 'shard'))
- attention_update: float32 [2, 1024, 4096], P(None, ('expert', 'shard'))
- router_mean_next: float32 [2, 1024, 8], P(None, ('expert', 'shard'))
- router_square_next: float32 [2, 1024, 8], P(None, ('expert', 'shard'))
- router_update: float32 [2, 1024, 8], P(None, ('expert', 'shard'))
- gains_mean_next: float32 [9, 1024], P(None, ('expert', 'shard'))
- gains_square_next: float32 [9, 1024], P(None, ('expert', 'shard'))
- gains_update: float32 [9, 1024], P(None, ('expert', 'shard'))
- upward_mean_next: float32 [8, 2, 1024, 1024], P('expert', None, 'shard')
- upward_square_next: float32 [8, 2, 1024, 1024], P('expert', None, 'shard')
- upward_update: float32 [8, 2, 1024, 1024], P('expert', None, 'shard')
- downward_mean_next: float32 [8, 2, 512, 1024], P('expert', None, None, 'shard')
- downward_square_next: float32 [8, 2, 512, 1024], P('expert', None, None, 'shard')
- downward_update: float32 [8, 2, 512, 1024], P('expert', None, None, 'shard')
- table_mean_next: float32 [50304, 1024], P(('expert', 'shard'))
- table_square_next: float32 [50304, 1024], P(('expert', 'shard'))
- table_update: float32 [50304, 1024], P(('expert', 'shard'))
The draws below stay inside these ranges and needn't reach their ends.
Inputs may be any that keep to these rules, and one draw needn't show every extreme that they name: `routes`: each row names 4 different experts. Within the 256 rows of one sequence no expert is named more than 144 times, a bound that some block reaches. `picked`: the 8 entries of one sequence are distinct positions of that sequence. `loss_ids`: column 0 holds a position's target token, columns 1 to 64 the teacher's 64 distinct candidate tokens.
All inputs are finite; a program needn't handle non-finite values.
Results may differ from the reference program's by a relative error of at most 0.023.
The reference program's roundings to bfloat16 on the way count: a program that leaves them out, or rounds other values in their place, can miss the bound.
Values may be sent and summed in bfloat16 or wider, within the bound.
A program may use at most 384 MiB of HBM per device.

```python
import math
from functools import partial
import jax
import jax.numpy as jnp
import numpy as np
from jax import lax

D = 1024
HEADS = 16
HDIM = 64
F = 512
V = 50304
TOPK = 4
TEACH = 64
LAYERS = 2
ADAM_STEP = 10
LEN = 256
PICK = 8
E = 8
SEQS = 32
TOKENS = 8192
POSITIONS = 256
CAP = 144
GAINS_ROWS = 9


def draw_attention(key, part):
    values = jax.random.truncated_normal(key, -4.0, 4.0, (LAYERS, D, 4 * D), jnp.float32)
    column = jnp.arange(4 * D)
    column_scale = jnp.where(column < 3 * D, D ** (-0.5), (LEN / 4.0) ** 0.5 * D ** (-0.5))
    return (values * column_scale[None, None, :]).astype(jnp.float32)


def draw_picked(key, part):
    seq_keys = jax.random.split(jax.random.fold_in(key, 11), SEQS)

    def one_sequence(seq_key):
        shuffled = jax.random.permutation(seq_key, LEN - 2) + 1
        return shuffled[:PICK]
    chosen = jax.vmap(one_sequence)(seq_keys)
    chosen = chosen.at[0, 0].set(LEN - 1).at[0, 1].set(0)
    return chosen.reshape(SEQS * PICK).astype(jnp.int32)


def draw_loss_ids(key, part):
    position_count = SEQS * PICK
    key_target, key_base, key_stride = jax.random.split(jax.random.fold_in(key, 23), 3)
    target = jax.random.randint(key_target, (position_count, 1), 0, V, dtype=jnp.int32)
    base_id = jax.random.randint(key_base, (position_count, 1), 0, V, dtype=jnp.int32)
    stride_id = jax.random.randint(key_stride, (position_count, 1), 1, V // TEACH, dtype=jnp.int32)
    target = target.at[0, 0].set(V - 1)
    base_id = base_id.at[0, 0].set(0)
    teacher_ids = (base_id + stride_id * jnp.arange(TEACH, dtype=jnp.int32)[None, :]) % V
    return jnp.concatenate([target, teacher_ids], axis=1).astype(jnp.int32)


def set_ends(values, rng, smallest, largest):
    longest = values.shape.index(max(values.shape))
    spots = []
    for shift in (0, 1):
        where = [jax.random.randint(jax.random.fold_in(rng, axis), (), 0, length) for axis, length in enumerate(values.shape)]
        where[longest] = (where[longest] + shift) % values.shape[longest]
        spots.append(tuple(where))
    return values.at[spots[0]].set(smallest).at[spots[1]].set(largest)


def block_levels(own_key, shape, cuts, least, largest):
    level, own = 1.0, jax.random.fold_in(own_key, 6)
    for dim, blocks in cuts:
        heights = jnp.exp(jax.random.uniform(jax.random.fold_in(own, dim), (blocks,), jnp.float32, least / len(cuts), largest / len(cuts)))
        level = level * jnp.repeat(heights, shape[dim] // blocks).reshape([-1 if axis == dim else 1 for axis in range(len(shape))])
    return level


def rank_bounds(amount, slope):
    loads = [(1 << 20) // math.isqrt(grade ** slope) + 1 for grade in range(1, amount + 1)]
    deviation = 1 + sum(loads) // (1 << 30)
    return np.cumsum(np.array([max(1, weight // deviation) for weight in loads]))


def skewed_ids(key, shape, number_of, lean):
    listing = rank_bounds(number_of, lean)
    pick = jax.random.randint(jax.random.fold_in(key, 1), shape, 0, int(listing[number_of - 1]))
    grade = jnp.searchsorted(jnp.asarray(listing, jnp.int32), pick, side="right")
    return jax.random.permutation(jax.random.fold_in(key, 2), number_of)[grade].astype(jnp.int32)


def routed_block(own_key, own, number, rows, count, top, most, skew):
    sequence = jax.random.permutation(own_key, count)
    packed, common = shares(count, rows * top, most, skew, True), shares(count, rows * top, most, skew, False)
    places = jnp.arange(count)

    def named(sizes, offset_by):
        used = int((sizes > 0).sum())
        fixed = max(1, used // 4)
        shifted = fixed + (places - fixed + offset_by * (used - fixed)) % max(1, count - fixed)
        return jnp.zeros((count,), jnp.int32).at[sequence[jnp.where(places < fixed, places, shifted)]].set(jnp.asarray(sizes, jnp.int32))

    sizes = jnp.where(number % 4 == 0, named(packed, number // 4), named(common, number - number // 4 - 1))
    mixed = jax.random.permutation(jax.random.fold_in(own, 3), count)
    donor, sink = mixed[0:count // 2 * 2:2], mixed[1:count // 2 * 2:2]
    margin = jnp.minimum(sizes[donor] - 1, most - sizes[sink]) // 2
    margin = jnp.where((donor == sequence[0]) | (sink == sequence[0]) | (sizes[sink] == 0), 0, jnp.maximum(margin, 0))
    shifted = jax.random.randint(jax.random.fold_in(own, 4), (count // 2,), 0, 1 << 20) % (margin + 1)
    sizes = sizes.at[donor].add(-shifted).at[sink].add(shifted)
    members = jnp.searchsorted(jnp.cumsum(sizes), jnp.arange(rows * top), side="right").astype(jnp.int32)
    grid = members.reshape(top, rows).T
    grid = grid[jax.random.permutation(jax.random.fold_in(own, 1), rows)]
    offset_by = jax.random.randint(jax.random.fold_in(own, 2), (rows, 1), 0, top)
    return jnp.take_along_axis(grid, (jnp.arange(top)[None, :] + offset_by) % top, axis=1)


def shares(number_of, total, most, lean, full):
    weights = [(1 << 20) // math.isqrt(standing ** lean) + 1 for standing in range(1, number_of + 1)]
    largest = most if full else min(most, max(-(-total // number_of), total * weights[0] // sum(weights)))
    least = 1 if total - largest >= number_of - 1 else 0
    counts, spare = [largest] + [least] * (number_of - 1), total - largest - least * (number_of - 1)
    while spare > 0:
        movable = [i for i in range(1, number_of) if counts[i] < largest] or [i for i in range(1, number_of) if counts[i] < most]
        whole, left = sum([weights[i] for i in movable]), spare
        for i in movable:
            more = min(most - counts[i], max(1, left * weights[i] // whole), spare)
            counts[i] = counts[i] + more
            spare = spare - more
    return np.array(counts)


def bell_draw(key, shape, width, most, cuts=(), held_as=jnp.bfloat16):
    entries = jax.random.normal(key, shape, jnp.float32) * width
    if len(cuts) > 0:
        entries = block_levels(key, shape, cuts, -0.22, 0.18) * entries
    return jnp.clip(entries, min=-most, max=most).astype(held_as)


def setup_inputs(seed: int = 0) -> dict:
    key_list = jax.random.split(jax.random.key(seed), 28)
    tokens = set_ends(skewed_ids(key_list[0], (TOKENS,), V, 2), jax.random.fold_in(key_list[0], 3), 0, V - 1).astype(jnp.int32)
    prefix = set_ends(jax.random.randint(key_list[1], (SEQS,), 1, LEN + 1), jax.random.fold_in(key_list[1], 1), 1, LEN).astype(jnp.int32)
    routes_keys = jax.random.split(jax.random.fold_in(key_list[2], 1), TOKENS // LEN)
    routes_turns = jax.random.permutation(jax.random.fold_in(key_list[2], 3), TOKENS // LEN)
    routes = jax.vmap(lambda own, number: routed_block(jax.random.fold_in(key_list[2], 2), own, number, LEN, E, TOPK, CAP, 2))(routes_keys, routes_turns).reshape((TOKENS, TOPK))
    picked = draw_picked(jax.random.fold_in(key_list[27], 71), 0)
    loss_ids = draw_loss_ids(jax.random.fold_in(key_list[27], 71), 0)
    teacher_logits = bell_draw(key_list[5], (POSITIONS, TEACH), 2.0, 8.0, (), jnp.float32)
    embedding = bell_draw(key_list[6], (V, D), 1.0, 6.0, ((1, 32),), jnp.float32)
    embedding_mean = bell_draw(key_list[7], (V, D), (0.0625 * POSITIONS ** -1.0 * D ** -0.5), 4.57763671875e-05, ((1, 32),), jnp.float32)
    embedding_square = jnp.clip(jnp.exp(math.log(9.313225746154785e-08) - 4.6051702 * jax.random.uniform(key_list[8], (V, D), jnp.float32) ** block_levels(key_list[8], (V, D), ((1, 32),), -0.2, 0.2)), 9.313225746154785e-10, 9.313225746154785e-08)
    attention = draw_attention(jax.random.fold_in(key_list[27], 71), 0)
    attention_mean = bell_draw(key_list[10], (LAYERS, D, 4 * D), ((POSITIONS * D) ** -0.5), 0.01171875, ((1, 32),), jnp.float32)
    attention_square = jnp.clip(jnp.exp(math.log(2.384185791015625e-05) - 4.6051702 * jax.random.uniform(key_list[11], (LAYERS, D, 4 * D), jnp.float32) ** block_levels(key_list[11], (LAYERS, D, 4 * D), ((1, 32),), -0.2, 0.2)), 2.384185791015625e-07, 2.384185791015625e-05)
    router = bell_draw(key_list[12], (LAYERS, D, E), (D // 4) ** -0.5, 0.375, ((1, 32),), jnp.float32)
    router_mean = bell_draw(key_list[13], (LAYERS, D, E), ((POSITIONS * D) ** -0.5), 0.01171875, ((1, 32),), jnp.float32)
    router_square = jnp.clip(jnp.exp(math.log(0.00038146973) - 4.6051702 * jax.random.uniform(key_list[14], (LAYERS, D, E), jnp.float32) ** block_levels(key_list[14], (LAYERS, D, E), ((1, 32),), -0.2, 0.2)), 3.814697265625e-06, 0.00038146973)
    norm_gains = jnp.clip(1.0 + 0.1 * jax.random.normal(key_list[15], (GAINS_ROWS, D), jnp.float32), 0.5, 1.5)
    gains_mean = bell_draw(key_list[16], (GAINS_ROWS, D), ((POSITIONS * D) ** -0.5), 0.01171875, ((1, 32),), jnp.float32)
    gains_square = jnp.clip(jnp.exp(math.log(0.00038146973) - 4.6051702 * jax.random.uniform(key_list[17], (GAINS_ROWS, D), jnp.float32) ** block_levels(key_list[17], (GAINS_ROWS, D), ((1, 32),), -0.2, 0.2)), 3.814697265625e-06, 0.00038146973)
    expert_up = bell_draw(key_list[18], (E, LAYERS, D, 2 * F), D ** -0.5, 0.1875, ((0, 8), (2, 4)), jnp.float32)
    upward_mean = bell_draw(key_list[19], (E, LAYERS, D, 2 * F), (0.125 * (POSITIONS * D) ** -0.5), 0.0014648438, ((0, 8), (2, 4)), jnp.float32)
    upward_square = jnp.clip(jnp.exp(math.log(2.9802322387695312e-06) - 4.6051702 * jax.random.uniform(key_list[20], (E, LAYERS, D, 2 * F), jnp.float32) ** block_levels(key_list[20], (E, LAYERS, D, 2 * F), ((0, 8), (2, 4)), -0.2, 0.2)), 2.9802322387695312e-08, 2.9802322387695312e-06)
    expert_down = bell_draw(key_list[21], (E, LAYERS, F, D), (max(F // 64, 1)) ** -0.5, 2.0, ((0, 8), (3, 4)), jnp.float32)
    downward_mean = bell_draw(key_list[22], (E, LAYERS, F, D), (0.0078125 * (POSITIONS * D) ** -0.5), 9.1552734375e-05, ((0, 8), (3, 4)), jnp.float32)
    downward_square = jnp.clip(jnp.exp(math.log(2.3283064365386963e-08) - 4.6051702 * jax.random.uniform(key_list[23], (E, LAYERS, F, D), jnp.float32) ** block_levels(key_list[23], (E, LAYERS, F, D), ((0, 8), (3, 4)), -0.2, 0.2)), 2.3283064365386963e-10, 2.3283064365386963e-08)
    output_table = bell_draw(key_list[24], (V, D), (D // 4) ** -0.5, 0.375, ((0, 32),), jnp.float32)
    table_mean = bell_draw(key_list[25], (V, D), (2.0 * V ** -1.0 * POSITIONS ** -0.5), 1.4909351193637121e-05, ((0, 32),), jnp.float32)
    table_square = jnp.clip(jnp.exp(math.log(6.174687428028847e-10) - 4.6051702 * jax.random.uniform(key_list[26], (V, D), jnp.float32) ** block_levels(key_list[26], (V, D), ((0, 32),), -0.2, 0.2)), 6.174687497417786e-12, 6.174687428028847e-10)
    return {"tokens": tokens, "prefix": prefix, "routes": routes, "picked": picked, "loss_ids": loss_ids, "teacher_logits": teacher_logits, "embedding": embedding, "embedding_mean": embedding_mean, "embedding_square": embedding_square, "attention": attention, "attention_mean": attention_mean, "attention_square": attention_square, "router": router, "router_mean": router_mean, "router_square": router_square, "norm_gains": norm_gains, "gains_mean": gains_mean, "gains_square": gains_square, "expert_up": expert_up, "upward_mean": upward_mean, "upward_square": upward_square, "expert_down": expert_down, "downward_mean": downward_mean, "downward_square": downward_square, "output_table": output_table, "table_mean": table_mean, "table_square": table_square}


EPS_NORM = 1e-05
BETA_ONE = 0.9
BETA_TWO = 0.95
ADAM_EPS = 1e-08
LEARN_RATE = 0.01
DECAY_RATE = 0.1
ROPE_BASE = 10000.0
MASK_FILL = -1e+30
HIGHEST = lax.Precision.HIGHEST

@jax.custom_vjp
def low(v):
    return lax.optimization_barrier(v.astype(jnp.bfloat16)).astype(jnp.float32)

@jax.custom_vjp
def low_back(v):
    return v

def low_keep(v):
    return (low(v), None)

def low_pass(kept, grad):
    return (grad,)

def back_keep(v):
    return (v, None)

def back_low(kept, grad):
    return (low(grad),)
low.defvjp(low_keep, low_pass)
low_back.defvjp(back_keep, back_low)

def rms_norm(inputs, gain_row):
    return inputs * lax.rsqrt(lax.optimization_barrier(jnp.mean(inputs * inputs, axis=-1, keepdims=True)) + EPS_NORM) * gain_row

def rotary(inputs):
    row_count = inputs.shape[0]
    split_heads = inputs.reshape(row_count, HEADS, HDIM)
    half_dim = HDIM // 2
    position = jnp.arange(row_count, dtype=jnp.float32)[:, None, None]
    frequency = ROPE_BASE ** (-jnp.arange(half_dim, dtype=jnp.float32) * 2.0 / HDIM)
    angles = position * frequency[None, None, :]
    cosines = jnp.cos(angles)
    sine_values = jnp.sin(angles)
    lower_half = split_heads[..., :half_dim]
    upper_half = split_heads[..., half_dim:]
    turned = jnp.concatenate([lower_half * cosines - upper_half * sine_values, upper_half * cosines + lower_half * sine_values], axis=-1)
    return turned.reshape(row_count, HEADS * HDIM)

def slot_table(route_rows, expert_count, capacity):
    row_count = route_rows.shape[0]
    top_count = route_rows.shape[1]
    one_hot = (route_rows[:, :, None] == jnp.arange(expert_count, dtype=jnp.int32)[None, None, :]).astype(jnp.int32)
    one_hot = one_hot.reshape(row_count * top_count, expert_count)
    before = jnp.cumsum(one_hot, axis=0) - one_hot
    slot_index = lax.optimization_barrier(jnp.sum(before * one_hot, axis=1))
    kept_mask = slot_index < capacity
    flat_slot = jnp.where(kept_mask, route_rows.reshape(row_count * top_count) * capacity + slot_index, expert_count * capacity)
    return (flat_slot.astype(jnp.int32), kept_mask)

def sequence_rows(weights_low, inputs):
    table_low, attention_low, router_low, gain_rows, upward_low, downward_low = weights_low
    seq_tokens, seq_routes, seq_prefix, seq_picked = inputs
    hidden = jnp.take(table_low, seq_tokens, axis=0)
    position = jnp.arange(LEN, dtype=jnp.int32)
    visible = (position[None, :] <= position[:, None]) | (position[None, :] < seq_prefix)
    for layer_index in range(LAYERS):
        weights_now = attention_low[layer_index]
        normed_low = low(rms_norm(hidden, gain_rows[4 * layer_index]))
        projected = low_back(jnp.dot(normed_low, weights_now[:, :3 * D], precision=HIGHEST))
        queries = low_back(low(rotary(rms_norm(projected[:, :D], gain_rows[4 * layer_index + 1]))))
        key_rows = low_back(low(rotary(rms_norm(projected[:, D:2 * D], gain_rows[4 * layer_index + 2]))))
        value_rows = low_back(low(projected[:, 2 * D:]))
        scores = jnp.einsum('qhd,khd->hqk', queries.reshape(LEN, HEADS, HDIM), key_rows.reshape(LEN, HEADS, HDIM), precision=HIGHEST)
        scores = low_back(scores * HDIM ** (-0.5))
        probs = jax.nn.softmax(jnp.where(visible[None], scores, MASK_FILL), axis=-1)
        attended = jnp.einsum('hqk,khd->qhd', low(probs), value_rows.reshape(LEN, HEADS, HDIM), precision=HIGHEST).reshape(LEN, D)
        attended_low = low_back(low(attended))
        middle = hidden + low_back(jnp.dot(attended_low, weights_now[:, 3 * D:], precision=HIGHEST))
        ffn_low = low(rms_norm(middle, gain_rows[4 * layer_index + 3]))
        router_logits = low_back(jnp.dot(ffn_low, router_low[layer_index], precision=HIGHEST))
        router_probs = jax.nn.softmax(router_logits, axis=-1)
        gate_weights = jnp.take_along_axis(router_probs, seq_routes, axis=1)
        flat_slot, kept_mask = slot_table(seq_routes, E, CAP)
        spread = jnp.broadcast_to(ffn_low[:, None, :], (LEN, TOPK, D)).reshape(LEN * TOPK, D)
        buffer = jnp.zeros((E * CAP + 1, D), jnp.float32).at[flat_slot].add(spread)
        dispatched = buffer[:E * CAP].reshape(E, CAP, D)
        gate_up = low_back(jnp.einsum('ecd,edf->ecf', dispatched, upward_low[:, layer_index], precision=HIGHEST))
        activated = low_back(low(jax.nn.silu(gate_up[..., :F]) * gate_up[..., F:]))
        produced = low_back(low(jnp.einsum('ecf,efd->ecd', activated, downward_low[:, layer_index], precision=HIGHEST)))
        safe_slot = jnp.minimum(flat_slot, E * CAP - 1)
        collected = jnp.take(produced.reshape(E * CAP, D), safe_slot, axis=0)
        collected = jnp.where(kept_mask[:, None], collected, 0.0).reshape(LEN, TOPK, D)
        hidden = middle + lax.optimization_barrier(jnp.sum(gate_weights[:, :, None] * collected, axis=1))
    final_rows = jnp.take(hidden, seq_picked, axis=0)
    return low(rms_norm(final_rows, gain_rows[4 * LAYERS]))

def block_loss(table_low, inputs):
    rows_low, block_ids, teacher_block = inputs
    logits = low_back(jnp.dot(rows_low, table_low.T, precision=HIGHEST))
    log_norm = jax.nn.logsumexp(logits, axis=1)
    selected = jnp.take_along_axis(logits, block_ids, axis=1)
    teacher_log = jax.nn.log_softmax(teacher_block, axis=1)
    teacher_prob = jnp.exp(teacher_log)
    row_loss = log_norm - selected[:, 0] + lax.optimization_barrier(jnp.sum(teacher_prob * (teacher_log - selected[:, 1:] + log_norm[:, None]), axis=1))
    return jnp.sum(row_loss)

def adam_step(weight, mean_old, square_old, gradient):
    mean_new = BETA_ONE * mean_old + (1.0 - BETA_ONE) * gradient
    square_new = BETA_TWO * square_old + (1.0 - BETA_TWO) * gradient * gradient
    bias_one = 1.0 - BETA_ONE ** ADAM_STEP
    bias_two = 1.0 - BETA_TWO ** ADAM_STEP
    update = -LEARN_RATE * (mean_new / bias_one / (jnp.sqrt(square_new / bias_two) + ADAM_EPS) + DECAY_RATE * weight)
    return (mean_new, square_new, update)

def reference(tokens, prefix, routes, picked, loss_ids, teacher_logits, embedding, embedding_mean, embedding_square, attention, attention_mean, attention_square, router, router_mean, router_square, norm_gains, gains_mean, gains_square, expert_up, upward_mean, upward_square, expert_down, downward_mean, downward_square, output_table, table_mean, table_square):
    sequence_inputs = (tokens.reshape(SEQS, LEN), routes.reshape(SEQS, LEN, TOPK), prefix, picked.reshape(SEQS, PICK))
    block_size = min(512, POSITIONS)
    block_count = POSITIONS // block_size

    def total_loss(params):
        emb_w, att_w, rou_w, gain_w, up_w, down_w, table_w = params
        weights_low = (low(emb_w), low(att_w), low(rou_w), low(gain_w), low(up_w), low(down_w))
        table_low = low(table_w)
        final_rows = lax.map(jax.checkpoint(partial(sequence_rows, weights_low)), sequence_inputs)
        final_rows = final_rows.reshape(block_count, block_size, D)
        sums = lax.map(jax.checkpoint(partial(block_loss, table_low)), (final_rows, loss_ids.reshape(block_count, block_size, TEACH + 1), teacher_logits.reshape(block_count, block_size, TEACH)))
        return jnp.sum(sums) / POSITIONS
    params = (embedding, attention, router, norm_gains, expert_up, expert_down, output_table)
    loss_value, pullback = jax.vjp(total_loss, params)
    grads = pullback(jnp.ones_like(loss_value))[0]
    embedding_mean_next, embedding_square_next, embedding_update = adam_step(embedding, embedding_mean, embedding_square, grads[0])
    attention_mean_next, attention_square_next, attention_update = adam_step(attention, attention_mean, attention_square, grads[1])
    router_mean_next, router_square_next, router_update = adam_step(router, router_mean, router_square, grads[2])
    gains_mean_next, gains_square_next, gains_update = adam_step(norm_gains, gains_mean, gains_square, grads[3])
    upward_mean_next, upward_square_next, upward_update = adam_step(expert_up, upward_mean, upward_square, grads[4])
    downward_mean_next, downward_square_next, downward_update = adam_step(expert_down, downward_mean, downward_square, grads[5])
    table_mean_next, table_square_next, table_update = adam_step(output_table, table_mean, table_square, grads[6])
    return (loss_value, embedding_mean_next, embedding_square_next, embedding_update, attention_mean_next, attention_square_next, attention_update, router_mean_next, router_square_next, router_update, gains_mean_next, gains_square_next, gains_update, upward_mean_next, upward_square_next, upward_update, downward_mean_next, downward_square_next, downward_update, table_mean_next, table_square_next, table_update)
```

```python
import jax
import jax.numpy as jnp
from jax import lax
from jax.sharding import Mesh, PartitionSpec as P

D = 1024
HEADS = 16
HDIM = 64
F = 512
TOPK = 4
ADAM_STEP = 10


EPS_NORM = 1e-05
BETA_ONE = 0.9
BETA_TWO = 0.95
ADAM_EPS = 1e-08
LEARN_RATE = 0.01
DECAY_RATE = 0.1
ROPE_BASE = 10000.0
MASK_FILL = -1e30


def rms_norm(inputs, gain_row):
    return (
        inputs * lax.rsqrt(jnp.mean(inputs * inputs, axis=-1, keepdims=True) + EPS_NORM) * gain_row
    )


def norm_back(inputs, gain_row, upstream):
    _, pullback = jax.vjp(rms_norm, inputs, gain_row)
    return pullback(upstream)


def rotary(inputs):
    row_count = inputs.shape[0]
    split_heads = inputs.reshape(row_count, HEADS, HDIM)
    half_dim = HDIM // 2
    position = jnp.arange(row_count, dtype=jnp.float32)[:, None, None]
    frequency = ROPE_BASE ** (-jnp.arange(half_dim, dtype=jnp.float32) * 2.0 / HDIM)
    angles = position * frequency[None, None, :]
    cosines = jnp.cos(angles)
    sine_values = jnp.sin(angles)
    lower_half = split_heads[..., :half_dim]
    upper_half = split_heads[..., half_dim:]
    turned = jnp.concatenate(
        [
            lower_half * cosines - upper_half * sine_values,
            upper_half * cosines + lower_half * sine_values,
        ],
        axis=-1,
    )
    return turned.reshape(row_count, HEADS * HDIM)


def rotary_back(upstream):
    _, pullback = jax.vjp(rotary, upstream)
    return pullback(upstream)[0]


def rounded(values):
    return lax.optimization_barrier(values.astype(jnp.bfloat16)).astype(jnp.float32)


AXES = ("z", "x", "h", "y", "c")
PLANES = 4


def head_terms(values):
    high = lax.reduce_precision(values, 8, 7)
    rest = (values - high).astype(jnp.bfloat16)
    return high.astype(jnp.bfloat16), rest


def split_dot(left, right):
    high, rest = head_terms(left)
    return jnp.dot(high, right, preferred_element_type=jnp.float32) + jnp.dot(
        rest, right, preferred_element_type=jnp.float32
    )


def visible_mask(seq_len, prefix_len):
    query_place = jnp.arange(seq_len, dtype=jnp.int32)[:, None]
    key_place = jnp.arange(seq_len, dtype=jnp.int32)[None, :]
    return (key_place <= query_place) | (key_place < prefix_len)


def attend(queries, key_rows, value_rows, visible):
    seq_len = queries.shape[0]
    query_heads = queries.reshape(seq_len, HEADS, HDIM)
    key_heads = key_rows.reshape(seq_len, HEADS, HDIM)
    value_heads = value_rows.reshape(seq_len, HEADS, HDIM)
    scores = jnp.einsum(
        "bhd,khd->hbk", query_heads, key_heads, preferred_element_type=jnp.float32
    ) * HDIM ** (-0.5)
    scores = jnp.where(visible[None], scores, MASK_FILL)
    peak_score = jnp.max(scores, axis=-1, keepdims=True)
    weights = jnp.exp(scores - peak_score)
    summed = jnp.sum(weights, axis=-1, keepdims=True)
    probs_low = (weights / summed).astype(jnp.bfloat16)
    attended = jnp.einsum(
        "hbk,khd->bhd", probs_low, value_heads, preferred_element_type=jnp.float32
    )
    return attended.reshape(seq_len, HEADS * HDIM), peak_score + jnp.log(summed)


def attend_back(queries, key_rows, value_rows, grad_low, log_total, visible):
    seq_len = queries.shape[0]
    query_heads = queries.reshape(seq_len, HEADS, HDIM)
    key_heads = key_rows.reshape(seq_len, HEADS, HDIM)
    value_heads = value_rows.reshape(seq_len, HEADS, HDIM)
    grad_heads = grad_low.reshape(seq_len, HEADS, HDIM)
    factor = HDIM ** (-0.5)
    scores = (
        jnp.einsum("bhd,khd->hbk", query_heads, key_heads, preferred_element_type=jnp.float32)
        * factor
    )
    scores = jnp.where(visible[None], scores, MASK_FILL)
    probs = jnp.exp(scores - log_total)
    grad_probs = jnp.einsum(
        "bhd,khd->hbk", grad_heads, value_heads, preferred_element_type=jnp.float32
    )
    row_dot = jnp.sum(probs * grad_probs, axis=-1, keepdims=True)
    grad_scores = (probs * (grad_probs - row_dot)).astype(jnp.bfloat16)
    query_grad = (
        jnp.einsum("hbk,khd->bhd", grad_scores, key_heads, preferred_element_type=jnp.float32)
        * factor
    )
    key_grad = (
        jnp.einsum("hbk,bhd->khd", grad_scores, query_heads, preferred_element_type=jnp.float32)
        * factor
    )
    value_grad = jnp.einsum(
        "hbk,bhd->khd", probs.astype(jnp.bfloat16), grad_heads, preferred_element_type=jnp.float32
    )
    full = (seq_len, HEADS * HDIM)
    return query_grad.reshape(full), key_grad.reshape(full), value_grad.reshape(full)


def swap_pairs(planes, rows, turn_plane, turn_row):
    pairs = []
    for plane in range(planes):
        for row in range(rows):
            for part in range(planes):
                source = (plane * rows + row) * planes + part
                target = (
                    ((part + turn_plane) % planes) * rows + (row + turn_row) % rows
                ) * planes + plane
                pairs.append((source, target))
    return pairs


def take_piece(pieces, place):
    return lax.dynamic_index_in_dim(pieces, place, 0, False)


def spread_experts(piece, row_groups):
    me_plane = lax.axis_index("z")
    me_row = lax.axis_index("h")
    arrived = []
    for turn_row in range(row_groups):
        for turn_plane in range(PLANES):
            arrived.append(
                lax.ppermute(
                    piece,
                    ("z", "h", "y", "c"),
                    swap_pairs(PLANES, row_groups, turn_plane, turn_row),
                )
            )
    stacked = jnp.stack(arrived)
    places = jnp.arange(row_groups * PLANES)
    row, part = places // PLANES, places % PLANES
    order = ((me_row - row) % row_groups) * PLANES + (me_plane - part) % PLANES
    return jnp.take(stacked, order, axis=0)


def gather_expert_grads(pieces, row_groups):
    me_plane = lax.axis_index("z")
    me_row = lax.axis_index("h")
    total = None
    for turn_row in range(row_groups):
        for turn_plane in range(PLANES):
            place = ((me_row - turn_row) % row_groups) * PLANES + (me_plane - turn_plane) % PLANES
            back = [
                (target, source)
                for source, target in swap_pairs(PLANES, row_groups, turn_plane, turn_row)
            ]
            term = lax.ppermute(take_piece(pieces, place), ("z", "h", "y", "c"), back)
            term = term.astype(jnp.float32)
            total = term if total is None else total + term
    return total


def scatter_axis(values, axis_name, dim):
    count = lax.axis_size(axis_name)
    if count == 1:
        return jnp.squeeze(values, dim)
    me = lax.axis_index(axis_name)
    total = lax.dynamic_index_in_dim(values, me, dim, False).astype(jnp.float32)
    for turn in range(1, count):
        sent = lax.dynamic_index_in_dim(values, (me + turn) % count, dim, False)
        got = lax.ppermute(sent, axis_name, [(i, (i + turn) % count) for i in range(count)])
        total = total + got.astype(jnp.float32)
    return total.astype(jnp.bfloat16)


def scatter_all(values):
    sizes = [lax.axis_size(name) for name in AXES]
    rows, columns = values.shape
    count = 1
    for size in sizes:
        count *= size
    blocks = values.reshape(*sizes, rows // count, columns)
    blocks = scatter_axis(blocks, "c", 4)
    half = columns // 2
    first, second = blocks[..., :half], blocks[..., half:]
    first = scatter_axis(first, "x", 1)
    second = scatter_axis(second, "y", 3)
    first = scatter_axis(first, "y", 2)
    second = scatter_axis(second, "x", 1)
    joined = jnp.concatenate([first, second], axis=-1)
    joined = scatter_axis(joined, "h", 1)
    me = lax.axis_index("z")
    total = take_piece(joined, me).astype(jnp.float32)
    for turn in range(1, sizes[0]):
        sent = take_piece(joined, (me + turn) % sizes[0])
        got = lax.ppermute(sent, "z", [(i, (i + turn) % sizes[0]) for i in range(sizes[0])])
        total = total + got.astype(jnp.float32)
    return total


def send_all(values):
    return lax.all_to_all(values, AXES, split_axis=0, concat_axis=0, tiled=True)


def send_plane(values):
    return lax.all_to_all(values, ("x", "y", "c"), split_axis=0, concat_axis=0, tiled=True)


def three_terms(values):
    first = lax.reduce_precision(values, 8, 7)
    second = lax.reduce_precision(values - first, 8, 7)
    third = lax.reduce_precision(values - first - second, 8, 7)
    return [first, second, third]

def adam_step(weight, mean_old, square_old, gradient):
    mean_new = BETA_ONE * mean_old + (1.0 - BETA_ONE) * gradient
    square_new = BETA_TWO * square_old + (1.0 - BETA_TWO) * gradient * gradient
    bias_one = 1.0 - BETA_ONE**ADAM_STEP
    bias_two = 1.0 - BETA_TWO**ADAM_STEP
    update = -LEARN_RATE * (
        mean_new / bias_one / (jnp.sqrt(square_new / bias_two) + ADAM_EPS) + DECAY_RATE * weight
    )
    return (mean_new, square_new, update)


def shards(
    tokens,
    prefix,
    routes,
    picked,
    loss_ids,
    teacher_logits,
    embedding,
    embedding_mean,
    embedding_square,
    attention,
    attention_mean,
    attention_square,
    router,
    router_mean,
    router_square,
    norm_gains,
    gains_mean,
    gains_square,
    expert_up,
    upward_mean,
    upward_square,
    expert_down,
    downward_mean,
    downward_square,
    output_table,
    table_mean,
    table_square,
):
    devices_all = lax.axis_size(AXES)
    me_all = lax.axis_index(AXES)
    row_groups = lax.axis_size("h")
    columns_x = lax.axis_size("x")
    seq_len = routes.shape[0]
    layer_count = attention.shape[0]
    experts_all = router.shape[2]
    capacity = 9 * seq_len * TOPK // (8 * experts_all)
    column_count = embedding.shape[1]
    prefix_len = prefix[0]
    slot_total = experts_all * capacity
    piece_rows = expert_up.shape[2]
    gain_count = norm_gains.shape[0]
    group_experts = [
        (group % PLANES) * columns_x + group // PLANES for group in range(experts_all)
    ]
    group_order = jnp.array(group_experts, jnp.int32)
    group_back = jnp.array(
        [group_experts.index(expert) for expert in range(experts_all)], jnp.int32
    )

    attention_low = lax.all_gather(attention.astype(jnp.bfloat16), AXES, axis=1, tiled=True)

    table_low = embedding.astype(jnp.bfloat16)
    looked_up = jnp.take(table_low, tokens, axis=0).reshape(devices_all, seq_len * column_count)
    small_count = gain_count + layer_count * experts_all
    small = jnp.concatenate(
        [norm_gains.T, router.transpose(1, 0, 2).reshape(column_count, layer_count * experts_all)],
        axis=1,
    ).astype(jnp.bfloat16)
    small = jnp.broadcast_to(
        small.reshape(1, column_count * small_count), (devices_all, column_count * small_count)
    )
    arrived_rows = send_all(jnp.concatenate([looked_up, small], axis=1))
    hidden = (
        arrived_rows[:, : seq_len * column_count]
        .reshape(devices_all, seq_len, column_count)
        .transpose(1, 0, 2)
        .reshape(seq_len, D)
        .astype(jnp.float32)
    )
    small_all = arrived_rows[:, seq_len * column_count :].reshape(D, small_count)
    gain_rows = small_all[:, :gain_count].T.astype(jnp.float32)
    router_low = (
        small_all[:, gain_count:]
        .reshape(D, layer_count, experts_all)
        .transpose(1, 0, 2)[:, :, group_order]
    )

    upward_low, downward_low = [], []
    for layer_index in range(layer_count):
        down_piece = (
            expert_down[0, layer_index]
            .reshape(F // piece_rows, piece_rows, piece_rows)
            .transpose(1, 0, 2)
            .reshape(piece_rows, F)
        )
        piece = jnp.concatenate([expert_up[0, layer_index], down_piece], axis=1).astype(
            jnp.bfloat16
        )
        pieces = spread_experts(piece, row_groups)
        upward_low.append(pieces[:, :, : 2 * F].reshape(D, 2 * F))
        downward_low.append(
            pieces[:, :, 2 * F :]
            .reshape(D // piece_rows, piece_rows, F // piece_rows, piece_rows)
            .transpose(2, 1, 0, 3)
            .reshape(F, D)
        )

    member = jnp.any(routes[:, :, None] == group_order[None, None, :], axis=1)
    before = jnp.dot(
        jnp.tril(jnp.ones((seq_len, seq_len), jnp.bfloat16), -1),
        member.astype(jnp.bfloat16),
        preferred_element_type=jnp.float32,
    ).astype(jnp.int32)
    spread = (
        (before.T[:, None, :] == jnp.arange(capacity, dtype=jnp.int32)[None, :, None])
        & member.T[:, None, :]
    ).astype(jnp.bfloat16)
    spread_flat = spread.reshape(slot_total, seq_len)
    spread_back = spread_flat.T
    kept = (member & (before < capacity)).astype(jnp.float32)

    head_low = output_table.astype(jnp.bfloat16)
    vocab_local = head_low.shape[0]
    teacher_log = jax.nn.log_softmax(teacher_logits, axis=1)
    teacher_prob = jnp.exp(teacher_log)
    position_count = loss_ids.shape[0]
    teacher_mass = jnp.sum(teacher_prob, axis=1)
    coefficients = jnp.concatenate(
        [jnp.ones((position_count, 1), jnp.float32), teacher_prob], axis=1
    )
    local_ids = loss_ids - me_all * vocab_local
    vocab_place = jnp.arange(vocab_local, dtype=jnp.int32)
    marked = jnp.sum(
        jnp.where(
            local_ids[:, :, None] == vocab_place[None, None, :], coefficients[:, :, None], 0.0
        ),
        axis=1,
    )
    marked_pull = jnp.dot(
        marked.astype(jnp.bfloat16), head_low, preferred_element_type=jnp.float32
    )
    own_count = position_count // devices_all
    marked_arrived = send_all(
        marked_pull.astype(jnp.bfloat16).reshape(devices_all, own_count, D)
    )
    marked_total = jnp.sum(marked_arrived.astype(jnp.float32), axis=0)

    visible = visible_mask(seq_len, prefix_len)
    stored = []
    for layer_index in range(layer_count):
        weights_now = attention_low[layer_index]
        normed_low = rms_norm(hidden, gain_rows[4 * layer_index]).astype(jnp.bfloat16)
        projected = jnp.dot(normed_low, weights_now[:, : 3 * D], preferred_element_type=jnp.float32)
        queries = rotary(rms_norm(projected[:, :D], gain_rows[4 * layer_index + 1])).astype(
            jnp.bfloat16
        )
        key_rows = rotary(rms_norm(projected[:, D : 2 * D], gain_rows[4 * layer_index + 2])).astype(
            jnp.bfloat16
        )
        value_rows = projected[:, 2 * D :].astype(jnp.bfloat16)
        attended, log_total = attend(queries, key_rows, value_rows, visible)
        attended_low = attended.astype(jnp.bfloat16)
        middle = hidden + jnp.dot(
            attended_low, weights_now[:, 3 * D :], preferred_element_type=jnp.float32
        )
        ffn_low = rms_norm(middle, gain_rows[4 * layer_index + 3]).astype(jnp.bfloat16)
        outgoing = jnp.dot(spread_flat, ffn_low, preferred_element_type=jnp.float32).astype(
            jnp.bfloat16
        )
        received = send_plane(outgoing.reshape(experts_all, capacity, D)).reshape(slot_total, D)
        router_logits = jnp.dot(
            ffn_low, router_low[layer_index], preferred_element_type=jnp.float32
        )
        router_probs = jax.nn.softmax(router_logits, axis=-1)
        gates = router_probs * kept
        gate_up = jnp.dot(received, upward_low[layer_index], preferred_element_type=jnp.float32)
        activated_low = (jax.nn.silu(gate_up[:, :F]) * gate_up[:, F:]).astype(jnp.bfloat16)
        produced = jnp.dot(
            activated_low, downward_low[layer_index], preferred_element_type=jnp.float32
        ).astype(jnp.bfloat16)
        returned = send_plane(produced.reshape(experts_all, capacity, D)).reshape(slot_total, D)
        gate_spread = (
            spread_back.reshape(seq_len, experts_all, capacity).astype(jnp.float32)
            * gates[:, :, None]
        ).reshape(seq_len, slot_total)
        stored.append(
            (
                hidden,
                normed_low,
                projected,
                queries,
                key_rows,
                value_rows,
                log_total,
                attended_low,
                middle,
                ffn_low,
                router_probs,
                gates,
                received,
                gate_up,
                activated_low,
                returned,
            )
        )
        hidden = middle + split_dot(gate_spread, returned)

    final_gain = gain_rows[4 * layer_count]
    final_rows = jnp.take(hidden, picked, axis=0)
    final_low = rms_norm(final_rows, final_gain).astype(jnp.bfloat16)
    all_rows = send_all(jnp.broadcast_to(final_low[None], (devices_all, own_count, D))).reshape(
        position_count, D
    )
    logits = jnp.einsum("pd,vd->pv", all_rows, head_low, preferred_element_type=jnp.float32)
    local_peak = jnp.max(logits, axis=1)
    local_exp = jnp.exp(logits - local_peak[:, None])
    local_sum = jnp.sum(local_exp, axis=1)
    local_dot = jnp.sum(marked * logits, axis=1)
    pull = jnp.dot(local_exp.astype(jnp.bfloat16), head_low, preferred_element_type=jnp.float32)
    stats = jnp.stack(
        three_terms(local_peak) + three_terms(local_sum) + three_terms(local_dot), axis=1
    )
    stats = jnp.pad(stats, ((0, 0), (0, 128 - stats.shape[1])))
    pull_sent = jnp.concatenate([pull, stats], axis=1).astype(jnp.bfloat16)
    pull_got = send_all(pull_sent.reshape(devices_all, own_count, D + 128)).astype(jnp.float32)
    stats_got = pull_got[:, :, D:]
    peaks = jnp.sum(stats_got[:, :, 0:3], axis=2)
    sums = jnp.sum(stats_got[:, :, 3:6], axis=2)
    dots = jnp.sum(stats_got[:, :, 6:9], axis=2)
    peak_own = jnp.max(peaks, axis=0)
    log_norm_own = peak_own + jnp.log(jnp.sum(sums * jnp.exp(peaks - peak_own), axis=0))
    mass_own = lax.dynamic_slice_in_dim(teacher_mass, me_all * own_count, own_count)
    entropy_own = lax.dynamic_slice_in_dim(
        jnp.sum(teacher_prob * teacher_log, axis=1), me_all * own_count, own_count
    )
    loss_own = (1.0 + mass_own) * log_norm_own - jnp.sum(dots, axis=0) + entropy_own
    scale_own = (1.0 + mass_own)[None, :] * jnp.exp(peaks - log_norm_own[None, :])
    final_grad = (
        jnp.sum(scale_own[:, :, None] * pull_got[:, :, :D], axis=0) - marked_total
    ) / position_count
    spread_stats = jnp.concatenate([log_norm_own, loss_own]).reshape(1, 2 * own_count)
    stats_all = send_all(jnp.broadcast_to(spread_stats, (devices_all, 2 * own_count)))
    log_norm = stats_all[:, :own_count].reshape(position_count)
    loss_value = jnp.sum(stats_all[:, own_count:]) / position_count
    grad_logits = (
        jnp.exp(logits - log_norm[:, None]) * (1.0 + teacher_mass)[:, None] - marked
    ) / position_count
    table_grad = jnp.einsum(
        "pv,pd->vd",
        grad_logits.astype(jnp.bfloat16),
        all_rows,
        preferred_element_type=jnp.float32,
    )
    rows_grad, final_gain_grad = norm_back(final_rows, final_gain, final_grad)
    place = jnp.arange(seq_len, dtype=jnp.int32)
    grad_hidden = jnp.sum(
        jnp.where(picked[:, None, None] == place[None, :, None], rows_grad[:, None, :], 0.0), axis=0
    )

    gain_parts = [None] * (4 * layer_count + 1)
    gain_parts[4 * layer_count] = final_gain_grad
    attention_parts = [None] * layer_count
    router_parts = [None] * layer_count
    up_parts = [None] * layer_count
    down_parts = [None] * layer_count
    for layer_index in reversed(range(layer_count)):
        (
            hidden_in,
            normed_low,
            projected,
            queries,
            key_rows,
            value_rows,
            log_total,
            attended_low,
            middle,
            ffn_low,
            router_probs,
            gates,
            received,
            gate_up,
            activated_low,
            returned,
        ) = stored[layer_index]
        weights_now = attention_low[layer_index]
        gate_slots = jnp.sum(spread.astype(jnp.float32) * gates.T[:, None, :], axis=2).reshape(
            slot_total, 1
        )
        grad_high, grad_rest = head_terms(grad_hidden)
        grad_slots = jnp.dot(
            spread_flat, grad_high, preferred_element_type=jnp.float32
        ) + jnp.dot(spread_flat, grad_rest, preferred_element_type=jnp.float32)
        sent_back = (gate_slots * grad_slots).astype(jnp.bfloat16)
        output_grad = send_plane(sent_back.reshape(experts_all, capacity, D)).reshape(
            slot_total, D
        )
        gate_dots = (
            jnp.einsum("ld,rd->lr", grad_high, returned, preferred_element_type=jnp.float32)
            + jnp.einsum("ld,rd->lr", grad_rest, returned, preferred_element_type=jnp.float32)
        ) * spread_back.astype(jnp.float32)
        prob_grad = jnp.sum(gate_dots.reshape(seq_len, experts_all, capacity), axis=2)
        logit_grad = router_probs * (
            prob_grad - jnp.sum(router_probs * prob_grad, axis=-1, keepdims=True)
        )
        logit_low = logit_grad.astype(jnp.bfloat16)
        router_parts[layer_index] = jnp.einsum(
            "ld,le->de", ffn_low, logit_low, preferred_element_type=jnp.float32
        )
        activated_grad = rounded(
            jnp.einsum(
                "rd,fd->rf",
                output_grad,
                downward_low[layer_index],
                preferred_element_type=jnp.float32,
            )
        )
        gate_part = gate_up[:, :F]
        up_part = gate_up[:, F:]
        sigmoid_gate = jax.nn.sigmoid(gate_part)
        gate_side = (
            activated_grad * up_part * sigmoid_gate * (1.0 + gate_part * (1.0 - sigmoid_gate))
        )
        up_side = activated_grad * gate_part * sigmoid_gate
        gate_up_grad = jnp.concatenate([gate_side, up_side], axis=-1).astype(jnp.bfloat16)
        input_grad = jnp.einsum(
            "rf,df->rd",
            gate_up_grad,
            upward_low[layer_index],
            preferred_element_type=jnp.float32,
        ).astype(jnp.bfloat16)
        back_inputs = send_plane(input_grad.reshape(experts_all, capacity, D)).reshape(
            slot_total, D
        )
        up_grad = jnp.einsum(
            "rd,rf->df", received, gate_up_grad, preferred_element_type=jnp.float32
        )
        down_grad = jnp.einsum(
            "rf,rd->fd", activated_low, output_grad, preferred_element_type=jnp.float32
        )
        grad_pieces = jnp.concatenate(
            [
                up_grad.reshape(D // piece_rows, piece_rows, 2 * F),
                down_grad.reshape(F // piece_rows, piece_rows, D // piece_rows, piece_rows)
                .transpose(2, 1, 0, 3)
                .reshape(D // piece_rows, piece_rows, F),
            ],
            axis=2,
        ).astype(jnp.bfloat16)
        piece_grad = gather_expert_grads(grad_pieces, row_groups)
        up_parts[layer_index] = piece_grad[:, : 2 * F]
        down_parts[layer_index] = (
            piece_grad[:, 2 * F :]
            .reshape(piece_rows, F // piece_rows, piece_rows)
            .transpose(1, 0, 2)
            .reshape(F, piece_rows)
        )
        ffn_grad = jnp.dot(
            spread_back, back_inputs, preferred_element_type=jnp.float32
        ) + jnp.einsum(
            "le,de->ld", logit_low, router_low[layer_index], preferred_element_type=jnp.float32
        )
        middle_grad, ffn_gain_grad = norm_back(middle, gain_rows[4 * layer_index + 3], ffn_grad)
        gain_parts[4 * layer_index + 3] = ffn_gain_grad
        grad_middle = grad_hidden + middle_grad
        branch_low = grad_middle.astype(jnp.bfloat16)
        out_weight_grad = jnp.einsum(
            "ld,le->de", attended_low, branch_low, preferred_element_type=jnp.float32
        )
        attended_grad = jnp.einsum(
            "le,de->ld", branch_low, weights_now[:, 3 * D :], preferred_element_type=jnp.float32
        ).astype(jnp.bfloat16)
        query_grad, key_grad, value_grad = attend_back(
            queries, key_rows, value_rows, attended_grad, log_total, visible
        )
        query_pre = rotary_back(rounded(query_grad))
        key_pre = rotary_back(rounded(key_grad))
        query_in, query_gain_grad = norm_back(
            projected[:, :D], gain_rows[4 * layer_index + 1], query_pre
        )
        key_in, key_gain_grad = norm_back(
            projected[:, D : 2 * D], gain_rows[4 * layer_index + 2], key_pre
        )
        gain_parts[4 * layer_index + 1] = query_gain_grad
        gain_parts[4 * layer_index + 2] = key_gain_grad
        projected_grad = jnp.concatenate([query_in, key_in, value_grad], axis=1).astype(
            jnp.bfloat16
        )
        qkv_weight_grad = jnp.einsum(
            "ld,le->de", normed_low, projected_grad, preferred_element_type=jnp.float32
        )
        normed_grad = jnp.einsum(
            "le,de->ld", projected_grad, weights_now[:, : 3 * D], preferred_element_type=jnp.float32
        )
        hidden_grad, attn_gain_grad = norm_back(hidden_in, gain_rows[4 * layer_index], normed_grad)
        gain_parts[4 * layer_index] = attn_gain_grad
        attention_parts[layer_index] = scatter_all(
            jnp.concatenate([qkv_weight_grad, out_weight_grad], axis=1).astype(jnp.bfloat16)
        )
        grad_hidden = grad_middle + hidden_grad

    sending = (
        grad_hidden.astype(jnp.bfloat16)
        .reshape(seq_len, devices_all, column_count)
        .transpose(1, 0, 2)
        .reshape(devices_all, seq_len * column_count)
    )
    small_grads = jnp.concatenate(
        [jnp.stack(gain_parts, axis=1)] + [part[:, group_back] for part in router_parts], axis=1
    ).astype(jnp.bfloat16)
    arrived_grads = send_all(
        jnp.concatenate(
            [sending, small_grads.reshape(devices_all, column_count * small_count)], axis=1
        )
    )
    embedding_grad = jax.ops.segment_sum(
        arrived_grads[:, : seq_len * column_count]
        .astype(jnp.float32)
        .reshape(devices_all * seq_len, column_count),
        tokens,
        num_segments=embedding.shape[0],
    )
    small_total = jnp.sum(
        arrived_grads[:, seq_len * column_count :].astype(jnp.float32), axis=0
    ).reshape(column_count, small_count)
    gains_grad = small_total[:, :gain_count].T
    router_grad = (
        small_total[:, gain_count:]
        .reshape(column_count, layer_count, experts_all)
        .transpose(1, 0, 2)
    )
    attention_grad = jnp.stack(attention_parts)
    upward_grad = jnp.stack(up_parts)[None]
    downward_grad = jnp.stack(down_parts)[None]
    embedding_mean_next, embedding_square_next, embedding_update = adam_step(
        embedding, embedding_mean, embedding_square, embedding_grad
    )
    attention_mean_next, attention_square_next, attention_update = adam_step(
        attention, attention_mean, attention_square, attention_grad
    )
    router_mean_next, router_square_next, router_update = adam_step(
        router, router_mean, router_square, router_grad
    )
    gains_mean_next, gains_square_next, gains_update = adam_step(
        norm_gains, gains_mean, gains_square, gains_grad
    )
    upward_mean_next, upward_square_next, upward_update = adam_step(
        expert_up, upward_mean, upward_square, upward_grad
    )
    downward_mean_next, downward_square_next, downward_update = adam_step(
        expert_down, downward_mean, downward_square, downward_grad
    )
    table_mean_next, table_square_next, table_update = adam_step(
        output_table, table_mean, table_square, table_grad
    )
    return (
        loss_value,
        embedding_mean_next,
        embedding_square_next,
        embedding_update,
        attention_mean_next,
        attention_square_next,
        attention_update,
        router_mean_next,
        router_square_next,
        router_update,
        gains_mean_next,
        gains_square_next,
        gains_update,
        upward_mean_next,
        upward_square_next,
        upward_update,
        downward_mean_next,
        downward_square_next,
        downward_update,
        table_mean_next,
        table_square_next,
        table_update,
    )


def solution(mesh):
    expert_count, shard_count = mesh.devices.shape
    mesh = Mesh(
        mesh.devices.reshape(PLANES, expert_count // PLANES, shard_count // 4, 2, 2), AXES
    )
    return jax.shard_map(
        shards,
        mesh=mesh,
        in_specs=(
            P(),
            P(AXES),
            P(AXES, None),
            P(AXES),
            P(),
            P(),
            P(None, AXES),
            P(None, AXES),
            P(None, AXES),
            P(None, AXES, None),
            P(None, AXES, None),
            P(None, AXES, None),
            P(None, AXES, None),
            P(None, AXES, None),
            P(None, AXES, None),
            P(None, AXES),
            P(None, AXES),
            P(None, AXES),
            P(("z", "x"), None, ("h", "y", "c"), None),
            P(("z", "x"), None, ("h", "y", "c"), None),
            P(("z", "x"), None, ("h", "y", "c"), None),
            P(("z", "x"), None, None, ("h", "y", "c")),
            P(("z", "x"), None, None, ("h", "y", "c")),
            P(("z", "x"), None, None, ("h", "y", "c")),
            P(AXES, None),
            P(AXES, None),
            P(AXES, None),
        ),
        out_specs=(
            P(),
            P(None, AXES),
            P(None, AXES),
            P(None, AXES),
            P(None, AXES, None),
            P(None, AXES, None),
            P(None, AXES, None),
            P(None, AXES, None),
            P(None, AXES, None),
            P(None, AXES, None),
            P(None, AXES),
            P(None, AXES),
            P(None, AXES),
            P(("z", "x"), None, ("h", "y", "c"), None),
            P(("z", "x"), None, ("h", "y", "c"), None),
            P(("z", "x"), None, ("h", "y", "c"), None),
            P(("z", "x"), None, None, ("h", "y", "c")),
            P(("z", "x"), None, None, ("h", "y", "c")),
            P(("z", "x"), None, None, ("h", "y", "c")),
            P(AXES, None),
            P(AXES, None),
            P(AXES, None),
        ),
        check_vma=False,
    )
```

```python
import functools

import jax
import jax.numpy as jnp
from jax import lax
from jax.experimental import pallas as pl
from jax.experimental.pallas import tpu as pltpu
from jax.sharding import Mesh, PartitionSpec as P

D = 1024
HEADS = 16
HDIM = 64
F = 512
TOPK = 4
ADAM_STEP = 10


EPS_NORM = 1e-05
BETA_ONE = 0.9
BETA_TWO = 0.95
ADAM_EPS = 1e-08
LEARN_RATE = 0.01
DECAY_RATE = 0.1
ROPE_BASE = 10000.0
MASK_FILL = -1e30


def rms_norm(inputs, gain_row):
    return (
        inputs * lax.rsqrt(jnp.mean(inputs * inputs, axis=-1, keepdims=True) + EPS_NORM) * gain_row
    )


def norm_back(inputs, gain_row, upstream):
    _, pullback = jax.vjp(rms_norm, inputs, gain_row)
    return pullback(upstream)


AXES = ("z", "x", "h", "y", "c")
PLANES = 4
SHIFTS = (0, 2, 1, 3)
LANES = 128
CHUNKS = D // LANES


def dot_nn(left, right):
    return lax.dot_general(
        left, right, (((1,), (0,)), ((), ())), preferred_element_type=jnp.float32
    )


def dot_nt(left, right):
    return lax.dot_general(
        left, right, (((1,), (1,)), ((), ())), preferred_element_type=jnp.float32
    )


def dot_tn(left, right):
    return lax.dot_general(
        left, right, (((0,), (0,)), ((), ())), preferred_element_type=jnp.float32
    )


def inverse_root(values):
    return lax.rsqrt(jnp.mean(values * values, axis=-1, keepdims=True) + EPS_NORM)


def two_terms(values):
    high = values.astype(jnp.bfloat16)
    return high, (values - high.astype(jnp.float32)).astype(jnp.bfloat16)


def chunk(values, place):
    return values[:, place * LANES : (place + 1) * LANES]


def half_turn(values):
    lane = lax.broadcasted_iota(jnp.int32, values.shape, 1)
    ahead = pltpu.roll(values, LANES - HDIM // 2, 1)
    behind = pltpu.roll(values, HDIM // 2, 1)
    return jnp.where(lane % HDIM < HDIM // 2, ahead, behind)


def slot_gates(spread, gates, capacity):
    high, rest = two_terms(gates)
    full = dot_nn(spread, high) + dot_nn(spread, rest)
    expert = lax.broadcasted_iota(jnp.int32, full.shape, 0) // capacity
    lane = lax.broadcasted_iota(jnp.int32, full.shape, 1)
    return jnp.sum(jnp.where(lane == expert, full, 0.0), axis=1, keepdims=True)


def combine(middle, spread, spread_back, gates, returned, capacity):
    weighted = slot_gates(spread, gates, capacity) * returned.astype(jnp.float32)
    high, rest = two_terms(weighted)
    return middle + (dot_nn(spread_back, high) + dot_nn(spread_back, rest))


def masked_probs(query, key, visible):
    scores = dot_nt(query, key) * HDIM ** (-0.5)
    scores = jnp.where(visible, scores, MASK_FILL)
    weights = jnp.exp(scores - jnp.max(scores, axis=-1, keepdims=True))
    return weights / jnp.sum(weights, axis=-1, keepdims=True)


def visible_keys(prefix_ref, seq_len):
    query_place = lax.broadcasted_iota(jnp.int32, (seq_len, seq_len), 0)
    key_place = lax.broadcasted_iota(jnp.int32, (seq_len, seq_len), 1)
    return (key_place <= query_place) | (key_place < prefix_ref[0])


def head_masks(seq_len):
    lane = lax.broadcasted_iota(jnp.int32, (seq_len, LANES), 1)
    return lane < HDIM, lane >= HDIM


def fetch_weights(weight_ref, held_ref, copy_sem, layer_index, order):
    copies = {}
    for part in order:
        copies[part] = pltpu.make_async_copy(
            weight_ref.at[layer_index, :, pl.ds(part * D, D)], held_ref.at[part], copy_sem.at[part]
        )
        copies[part].start()
    return copies


def forward_kernel(
    layer_index,
    capacity,
    expert_count,
    prefix_ref,
    hidden_ref,
    *refs,
):
    if layer_index > 0:
        gates_in_ref, returned_ref, refs = refs[0], refs[1], refs[2:]
    (
        weight_ref,
        gain_ref,
        turn_ref,
        router_ref,
        kept_ref,
        spread_ref,
        spread_back_ref,
        hidden_out_ref,
        projected_ref,
        query_ref,
        key_ref,
        value_ref,
        attended_ref,
        middle_ref,
        ffn_ref,
        probs_ref,
        gates_ref,
        outgoing_ref,
        held_ref,
        copy_sem,
    ) = refs
    copies = fetch_weights(weight_ref, held_ref, copy_sem, layer_index, (0, 1, 2, 3))
    seq_len = hidden_ref.shape[0]
    hidden = hidden_ref[...]
    if layer_index > 0:
        hidden = combine(
            hidden,
            spread_ref[...],
            spread_back_ref[...],
            gates_in_ref[...],
            returned_ref[...],
            capacity,
        )
    hidden_out_ref[...] = hidden
    row = 4 * layer_index
    normed = (hidden * inverse_root(hidden) * gain_ref[row : row + 1, :]).astype(jnp.bfloat16)
    cosines, sines = turn_ref[0], turn_ref[1]
    for part, out_ref in ((0, query_ref), (1, key_ref)):
        columns = slice(part * D, (part + 1) * D)
        copies[part].wait()
        projected = dot_nn(normed, held_ref[part])
        projected_ref[:, columns] = projected
        scaled = projected * inverse_root(projected) * gain_ref[row + 1 + part : row + 2 + part, :]
        for place in range(CHUNKS):
            block = chunk(scaled, place)
            out_ref[:, place * LANES : (place + 1) * LANES] = (
                block * cosines + half_turn(block) * sines
            ).astype(jnp.bfloat16)
    copies[2].wait()
    value_ref[...] = dot_nn(normed, held_ref[2]).astype(jnp.bfloat16)
    visible = visible_keys(prefix_ref, seq_len)
    masks = head_masks(seq_len)
    zero = jnp.zeros((), jnp.bfloat16)
    for place in range(CHUNKS):
        columns = slice(place * LANES, (place + 1) * LANES)
        query, key, value = query_ref[:, columns], key_ref[:, columns], value_ref[:, columns]
        total = None
        for mask in masks:
            probs = masked_probs(query, jnp.where(mask, key, zero), visible).astype(jnp.bfloat16)
            term = dot_nn(probs, jnp.where(mask, value, zero))
            total = term if total is None else total + term
        attended_ref[:, columns] = total.astype(jnp.bfloat16)
    copies[3].wait()
    middle = hidden + dot_nn(attended_ref[...], held_ref[3])
    middle_ref[...] = middle
    ffn = (middle * inverse_root(middle) * gain_ref[row + 3 : row + 4, :]).astype(jnp.bfloat16)
    ffn_ref[...] = ffn
    outgoing_ref[...] = dot_nn(spread_ref[...], ffn).astype(jnp.bfloat16)
    logits = dot_nn(ffn, router_ref[layer_index])
    lane = lax.broadcasted_iota(jnp.int32, logits.shape, 1)
    logits = jnp.where(lane < expert_count, logits, MASK_FILL)
    weights = jnp.exp(logits - jnp.max(logits, axis=-1, keepdims=True))
    probs = weights / jnp.sum(weights, axis=-1, keepdims=True)
    probs_ref[...] = probs
    gates_ref[...] = probs * kept_ref[...]


def forward_layer(
    layer_index,
    capacity,
    expert_count,
    prefix,
    hidden,
    extra,
    weights,
    gains,
    turns,
    router,
    kept,
    spread,
    spread_back,
):
    seq_len = hidden.shape[0]
    whole = pl.BlockSpec(memory_space=pltpu.VMEM)
    wide = jax.ShapeDtypeStruct((seq_len, D), jnp.float32)
    low = jax.ShapeDtypeStruct((seq_len, D), jnp.bfloat16)
    small = jax.ShapeDtypeStruct((seq_len, LANES), jnp.float32)
    return pl.pallas_call(
        functools.partial(forward_kernel, layer_index, capacity, expert_count),
        out_shape=(
            wide,
            jax.ShapeDtypeStruct((seq_len, 2 * D), jnp.float32),
            low,
            low,
            low,
            low,
            wide,
            low,
            small,
            small,
            jax.ShapeDtypeStruct((spread.shape[0], D), jnp.bfloat16),
        ),
        in_specs=[pl.BlockSpec(memory_space=pltpu.SMEM), whole]
        + [whole] * len(extra)
        + [pl.BlockSpec(memory_space=pl.ANY)]
        + [whole] * 6,
        out_specs=[whole] * 11,
        scratch_shapes=[
            pltpu.VMEM((4, D, D), jnp.bfloat16),
            pltpu.SemaphoreType.DMA((4,)),
        ],
        compiler_params=pltpu.CompilerParams(vmem_limit_bytes=60 * 1024 * 1024),
        cost_estimate=pl.CostEstimate(
            flops=4 * seq_len * D * D * 3, bytes_accessed=24 * 1024 * 1024, transcendentals=1 << 20
        ),
    )(prefix, hidden, *extra, weights, gains, turns, router, kept, spread, spread_back)


def norm_pull(values, gain, upstream):
    root = inverse_root(values)
    scaled = values * root
    weighted = upstream * gain
    mean = jnp.mean(weighted * scaled, axis=-1, keepdims=True)
    return root * (weighted - scaled * mean), jnp.sum(upstream * scaled, axis=0, keepdims=True)


def backward_kernel(
    layer_index,
    capacity,
    prefix_ref,
    grad_ref,
    back_ref,
    logit_ref,
    hidden_ref,
    projected_ref,
    query_ref,
    key_ref,
    value_ref,
    attended_ref,
    middle_ref,
    weight_ref,
    gain_ref,
    turn_ref,
    router_ref,
    spread_back_ref,
    *refs,
):
    if layer_index > 0:
        spread_ref, gates_ref, refs = refs[0], refs[1], refs[2:]
        outgoing_ref, refs = refs[3], refs[:3] + refs[4:]
    grad_out_ref, weight_grad_ref, gain_grad_ref, pull_ref, key_pull_ref, held_ref, copy_sem = refs
    copies = fetch_weights(weight_ref, held_ref, copy_sem, layer_index, (3, 2, 0, 1))
    seq_len = hidden_ref.shape[0]
    row = 4 * layer_index
    ffn_grad = dot_nn(spread_back_ref[...], back_ref[...]) + dot_nt(
        logit_ref[...], router_ref[layer_index]
    )
    middle_grad, gain_three = norm_pull(
        middle_ref[...], gain_ref[row + 3 : row + 4, :], ffn_grad
    )
    grad_middle = grad_ref[...] + middle_grad
    grad_out_ref[...] = grad_middle
    branch = grad_middle.astype(jnp.bfloat16)
    weight_grad_ref[:, 3 * D :] = dot_tn(attended_ref[...], branch).astype(jnp.bfloat16)
    copies[3].wait()
    pull_ref[...] = dot_nt(branch, held_ref[3]).astype(jnp.bfloat16)
    visible = visible_keys(prefix_ref, seq_len)
    masks = head_masks(seq_len)
    zero = jnp.zeros((), jnp.bfloat16)
    cosines, sines = turn_ref[0], turn_ref[1]
    factor = HDIM ** (-0.5)
    hidden = hidden_ref[...]
    normed = (hidden * inverse_root(hidden) * gain_ref[row : row + 1, :]).astype(jnp.bfloat16)
    for place in range(CHUNKS):
        columns = slice(place * LANES, (place + 1) * LANES)
        query, key, value = query_ref[:, columns], key_ref[:, columns], value_ref[:, columns]
        pull = pull_ref[:, columns]
        totals = [None, None, None]
        for mask in masks:
            key_half = jnp.where(mask, key, zero)
            probs = masked_probs(query, key_half, visible)
            pulled = dot_nt(pull, jnp.where(mask, value, zero))
            inner = jnp.sum(probs * pulled, axis=-1, keepdims=True)
            score_grad = (probs * (pulled - inner)).astype(jnp.bfloat16)
            terms = (
                dot_nn(score_grad, key_half),
                dot_tn(score_grad, jnp.where(mask, query, zero)),
                dot_tn(probs.astype(jnp.bfloat16), jnp.where(mask, pull, zero)),
            )
            totals = [b if a is None else a + b for a, b in zip(totals, terms)]
        for part, target_ref in ((0, key_pull_ref.at[0]), (1, key_pull_ref.at[1])):
            turned = (totals[part] * factor).astype(jnp.bfloat16).astype(jnp.float32)
            target_ref[:, columns] = turned * cosines - half_turn(turned) * sines
        pull_ref[:, columns] = totals[2].astype(jnp.bfloat16)
    gain_rows = []
    value_pull = pull_ref[...]
    copies[2].wait()
    back = dot_nt(value_pull, held_ref[2])
    weight_grad_ref[:, 2 * D : 3 * D] = dot_tn(normed, value_pull).astype(jnp.bfloat16)
    for part in range(2):
        columns = slice(part * D, (part + 1) * D)
        input_pull, gain_row = norm_pull(
            projected_ref[:, columns],
            gain_ref[row + 1 + part : row + 2 + part, :],
            key_pull_ref[part],
        )
        gain_rows.append(gain_row)
        low_pull = input_pull.astype(jnp.bfloat16)
        weight_grad_ref[:, columns] = dot_tn(normed, low_pull).astype(jnp.bfloat16)
        copies[part].wait()
        back = back + dot_nt(low_pull, held_ref[part])
    hidden_grad, gain_zero = norm_pull(hidden, gain_ref[row : row + 1, :], back)
    grad_out = grad_out_ref[...] + hidden_grad
    grad_out_ref[...] = grad_out
    if layer_index > 0:
        outgoing_ref[...] = outgoing_pull(grad_out, spread_ref[...], gates_ref[...], capacity)
    gain_grad_ref[...] = jnp.concatenate(
        [gain_zero] + gain_rows + [gain_three, jnp.zeros((4, D), jnp.float32)], axis=0
    )


def backward_layer(
    layer_index,
    capacity,
    prefix,
    grad,
    back_inputs,
    logit_low,
    hidden,
    projected,
    queries,
    keys,
    values,
    attended,
    middle,
    weights,
    gains,
    turns,
    router,
    spread_back,
    extra,
):
    seq_len = hidden.shape[0]
    whole = pl.BlockSpec(memory_space=pltpu.VMEM)
    out_shape = [
        jax.ShapeDtypeStruct((seq_len, D), jnp.float32),
        jax.ShapeDtypeStruct((D, 4 * D), jnp.bfloat16),
        jax.ShapeDtypeStruct((8, D), jnp.float32),
    ]
    if layer_index > 0:
        out_shape.append(jax.ShapeDtypeStruct((spread_back.shape[1], D), jnp.bfloat16))
    return pl.pallas_call(
        functools.partial(backward_kernel, layer_index, capacity),
        out_shape=out_shape,
        in_specs=[pl.BlockSpec(memory_space=pltpu.SMEM)]
        + [whole] * 10
        + [pl.BlockSpec(memory_space=pl.ANY)]
        + [whole] * (4 + len(extra)),
        out_specs=[whole] * len(out_shape),
        scratch_shapes=[
            pltpu.VMEM((seq_len, D), jnp.bfloat16),
            pltpu.VMEM((2, seq_len, D), jnp.float32),
            pltpu.VMEM((4, D, D), jnp.bfloat16),
            pltpu.SemaphoreType.DMA((4,)),
        ],
        compiler_params=pltpu.CompilerParams(vmem_limit_bytes=60 * 1024 * 1024),
        cost_estimate=pl.CostEstimate(
            flops=8 * seq_len * D * D * 3, bytes_accessed=32 * 1024 * 1024, transcendentals=1 << 20
        ),
    )(
        prefix,
        grad,
        back_inputs,
        logit_low,
        hidden,
        projected,
        queries,
        keys,
        values,
        attended,
        middle,
        weights,
        gains,
        turns,
        router,
        spread_back,
        *extra,
    )


def turn_tables(seq_len):
    position = jnp.arange(seq_len, dtype=jnp.float32)[:, None]
    frequency = ROPE_BASE ** (-jnp.arange(HDIM // 2, dtype=jnp.float32) * 2.0 / HDIM)
    angles = position * frequency[None, :]
    cosines, sines = jnp.cos(angles), jnp.sin(angles)
    return jnp.stack(
        [
            jnp.concatenate([cosines] * 4, axis=1),
            jnp.concatenate([-sines, sines, -sines, sines], axis=1),
        ]
    )


def silu_parts(gate_up):
    gate_part, up_part = gate_up[:, :F], gate_up[:, F:]
    sigmoid = 1.0 / (1.0 + jnp.exp(-gate_part))
    return gate_part, up_part, sigmoid


def fetch_expert(place_ref, part_refs, up_ref, down_ref, copy_sem):
    copies = []
    rows = part_refs[0].shape[0]
    for turn, part_ref in enumerate(part_refs):
        place = pl.multiple_of(place_ref[turn] * rows, rows)
        copies.append(
            pltpu.make_async_copy(
                part_ref.at[:, pl.ds(0, 2 * F)],
                up_ref.at[pl.ds(place, rows), :],
                copy_sem.at[len(copies)],
            )
        )
        for block in range(F // rows):
            copies.append(
                pltpu.make_async_copy(
                    part_ref.at[:, pl.ds(2 * F + block * rows, rows)],
                    down_ref.at[pl.ds(block * rows, rows), pl.ds(place, rows)],
                    copy_sem.at[len(copies)],
                )
            )
    for copy in copies:
        copy.start()
    for copy in copies:
        copy.wait()


def expert_kernel(part_count, row_block, place_ref, received_ref, *refs):
    part_refs, (produced_ref, up_ref, down_ref, copy_sem) = refs[:part_count], refs[part_count:]
    fetch_expert(place_ref, part_refs, up_ref, down_ref, copy_sem)

    @pl.loop(0, received_ref.shape[0] // row_block)
    def _(step):
        rows = pl.ds(pl.multiple_of(step * row_block, row_block), row_block)
        gate_part, up_part, sigmoid = silu_parts(dot_nn(received_ref[rows, :], up_ref[...]))
        activated = (gate_part * sigmoid * up_part).astype(jnp.bfloat16)
        produced_ref[rows, :] = dot_nn(activated, down_ref[...]).astype(jnp.bfloat16)


def expert_specs(parts):
    rows = parts[0].shape[0]
    whole = pl.BlockSpec(memory_space=pltpu.VMEM)
    specs = [pl.BlockSpec(memory_space=pltpu.SMEM)]
    apart = [pl.BlockSpec(memory_space=pl.ANY)] * len(parts)
    scratch = [
        pltpu.VMEM((D, 2 * F), jnp.bfloat16),
        pltpu.VMEM((F, D), jnp.bfloat16),
        pltpu.SemaphoreType.DMA((len(parts) * (1 + F // rows),)),
    ]
    return whole, specs, apart, scratch


def run_expert(places, received, parts):
    whole, specs, apart, scratch = expert_specs(parts)
    slot_total = received.shape[0]
    return pl.pallas_call(
        functools.partial(expert_kernel, len(parts), slot_total // 4),
        out_shape=jax.ShapeDtypeStruct((slot_total, D), jnp.bfloat16),
        in_specs=specs + [whole] + apart,
        out_specs=whole,
        scratch_shapes=scratch,
        compiler_params=pltpu.CompilerParams(vmem_limit_bytes=56 * 1024 * 1024),
        cost_estimate=pl.CostEstimate(
            flops=slot_total * D * F * 6, bytes_accessed=8 * 1024 * 1024, transcendentals=1 << 19
        ),
    )(places, received, *parts)


def expert_back_kernel(part_count, row_block, place_ref, received_ref, pull_ref, *refs):
    part_refs, refs = refs[:part_count], refs[part_count:]
    input_grad_ref, gate_grad_ref, activated_ref, up_ref, down_ref, copy_sem = refs
    fetch_expert(place_ref, part_refs, up_ref, down_ref, copy_sem)

    @pl.loop(0, received_ref.shape[0] // row_block)
    def _(step):
        rows = pl.ds(pl.multiple_of(step * row_block, row_block), row_block)
        gate_part, up_part, sigmoid = silu_parts(dot_nn(received_ref[rows, :], up_ref[...]))
        side = gate_part * sigmoid
        activated_ref[rows, :] = (side * up_part).astype(jnp.bfloat16)
        pulled = dot_nt(pull_ref[rows, :], down_ref[...]).astype(jnp.bfloat16)
        pulled = pulled.astype(jnp.float32)
        gate_side = pulled * up_part * sigmoid * (1.0 + gate_part * (1.0 - sigmoid))
        gate_grad_ref[rows, :F] = gate_side.astype(jnp.bfloat16)
        gate_grad_ref[rows, F:] = (pulled * side).astype(jnp.bfloat16)
        input_grad_ref[rows, :] = dot_nt(gate_grad_ref[rows, :], up_ref[...]).astype(jnp.bfloat16)


def run_expert_back(places, received, pull, parts):
    whole, specs, apart, scratch = expert_specs(parts)
    slot_total = received.shape[0]
    return pl.pallas_call(
        functools.partial(expert_back_kernel, len(parts), slot_total // 4),
        out_shape=(
            jax.ShapeDtypeStruct((slot_total, D), jnp.bfloat16),
            jax.ShapeDtypeStruct((slot_total, 2 * F), jnp.bfloat16),
            jax.ShapeDtypeStruct((slot_total, F), jnp.bfloat16),
        ),
        in_specs=specs + [whole] * 2 + apart,
        out_specs=[whole] * 3,
        scratch_shapes=scratch,
        compiler_params=pltpu.CompilerParams(vmem_limit_bytes=56 * 1024 * 1024),
        cost_estimate=pl.CostEstimate(
            flops=slot_total * D * F * 12, bytes_accessed=12 * 1024 * 1024, transcendentals=1 << 19
        ),
    )(places, received, pull, *parts)


def expert_grad_kernel(
    part_count, place_ref, received_ref, pull_ref, gate_grad_ref, activated_ref, *refs
):
    out_refs, (up_ref, down_ref) = refs[:part_count], refs[part_count:]
    block = 256

    @pl.loop(0, D // block)
    def _(step):
        columns = pl.ds(pl.multiple_of(step * block, block), block)
        up_ref[columns, :] = dot_tn(received_ref[:, columns], gate_grad_ref[...]).astype(
            jnp.bfloat16
        )

    @pl.loop(0, F // block)
    def _(step):
        columns = pl.ds(pl.multiple_of(step * block, block), block)
        down_ref[columns, :] = dot_tn(activated_ref[:, columns], pull_ref[...]).astype(
            jnp.bfloat16
        )

    rows = out_refs[0].shape[0]
    for turn, out_ref in enumerate(out_refs):
        place = pl.multiple_of(place_ref[turn] * rows, rows)
        out_ref[:, : 2 * F] = up_ref[pl.ds(place, rows), :]
        for part in range(F // rows):
            out_ref[:, 2 * F + part * rows : 2 * F + (part + 1) * rows] = down_ref[
                part * rows : (part + 1) * rows, pl.ds(place, rows)
            ]


def run_expert_grad(places, received, pull, gate_grad, activated, piece_rows):
    whole = pl.BlockSpec(memory_space=pltpu.VMEM)
    part_count = D // piece_rows
    slot_total = received.shape[0]
    return pl.pallas_call(
        functools.partial(expert_grad_kernel, part_count),
        out_shape=[jax.ShapeDtypeStruct((piece_rows, 3 * F), jnp.bfloat16)] * part_count,
        in_specs=[pl.BlockSpec(memory_space=pltpu.SMEM)] + [whole] * 4,
        out_specs=[whole] * part_count,
        scratch_shapes=[
            pltpu.VMEM((D, 2 * F), jnp.bfloat16),
            pltpu.VMEM((F, D), jnp.bfloat16),
        ],
        compiler_params=pltpu.CompilerParams(vmem_limit_bytes=56 * 1024 * 1024),
        cost_estimate=pl.CostEstimate(
            flops=slot_total * D * F * 6, bytes_accessed=12 * 1024 * 1024, transcendentals=0
        ),
    )(places, received, pull, gate_grad, activated)


def outgoing_pull(grad, spread, gates, capacity):
    high, rest = two_terms(grad)
    wide = dot_nn(spread, high) + dot_nn(spread, rest)
    return (slot_gates(spread, gates, capacity) * wide).astype(jnp.bfloat16)


def first_pull_kernel(capacity, picked_ref, rows_ref, spread_ref, gates_ref, grad_ref, out_ref):
    grad_ref[...] = jnp.zeros_like(grad_ref)
    for place in range(rows_ref.shape[0]):
        grad_ref[pl.ds(picked_ref[place], 1), :] = rows_ref[place : place + 1, :]
    out_ref[...] = outgoing_pull(grad_ref[...], spread_ref[...], gates_ref[...], capacity)


def first_pull(capacity, picked, rows, spread, gates):
    whole = pl.BlockSpec(memory_space=pltpu.VMEM)
    return pl.pallas_call(
        functools.partial(first_pull_kernel, capacity),
        out_shape=(
            jax.ShapeDtypeStruct((spread.shape[1], D), jnp.float32),
            jax.ShapeDtypeStruct((spread.shape[0], D), jnp.bfloat16),
        ),
        in_specs=[pl.BlockSpec(memory_space=pltpu.SMEM)] + [whole] * 3,
        out_specs=[whole] * 2,
        compiler_params=pltpu.CompilerParams(vmem_limit_bytes=48 * 1024 * 1024),
        cost_estimate=pl.CostEstimate(
            flops=4 * spread.shape[0] * spread.shape[1] * D,
            bytes_accessed=5 * 1024 * 1024,
            transcendentals=0,
        ),
    )(picked, rows, spread, gates)


def router_kernel(
    capacity, grad_ref, returned_ref, spread_back_ref, probs_ref, ffn_ref, low_ref, router_grad_ref
):
    high, rest = two_terms(grad_ref[...])
    dots = dot_nt(high, returned_ref[...]) + dot_nt(rest, returned_ref[...])
    dots = dots * spread_back_ref[...].astype(jnp.float32)
    slot_total = returned_ref.shape[0]
    slot = lax.broadcasted_iota(jnp.int32, (slot_total, LANES), 0) // capacity
    lane = lax.broadcasted_iota(jnp.int32, (slot_total, LANES), 1)
    owner = jnp.where(slot == lane, 1.0, 0.0).astype(jnp.bfloat16)
    high, rest = two_terms(dots)
    pull = dot_nn(high, owner) + dot_nn(rest, owner)
    probs = probs_ref[...]
    low = (probs * (pull - jnp.sum(probs * pull, axis=-1, keepdims=True))).astype(jnp.bfloat16)
    low_ref[...] = low
    router_grad_ref[...] = dot_tn(ffn_ref[...], low)


def router_back(capacity, grad, returned, spread_back, probs, ffn):
    whole = pl.BlockSpec(memory_space=pltpu.VMEM)
    seq_len = grad.shape[0]
    return pl.pallas_call(
        functools.partial(router_kernel, capacity),
        out_shape=(
            jax.ShapeDtypeStruct((seq_len, LANES), jnp.bfloat16),
            jax.ShapeDtypeStruct((D, LANES), jnp.float32),
        ),
        in_specs=[whole] * 5,
        out_specs=[whole] * 2,
        compiler_params=pltpu.CompilerParams(vmem_limit_bytes=48 * 1024 * 1024),
        cost_estimate=pl.CostEstimate(
            flops=4 * seq_len * returned.shape[0] * D,
            bytes_accessed=6 * 1024 * 1024,
            transcendentals=0,
        ),
    )(grad, returned, spread_back, probs, ffn)


def final_kernel(
    capacity,
    gain_row,
    picked_ref,
    middle_ref,
    gates_ref,
    returned_ref,
    spread_ref,
    spread_back_ref,
    gain_ref,
    rows_ref,
    low_ref,
):
    count = rows_ref.shape[0]
    for place in range(count):
        rows_ref[place : place + 1, :] = middle_ref[pl.ds(picked_ref[place], 1), :]
    sublane = lax.broadcasted_iota(jnp.int32, (count, LANES), 0)
    wanted = jnp.zeros((count, LANES), jnp.int32)
    for place in range(count):
        wanted = jnp.where(sublane == place, picked_ref[place], wanted)
    seq_len = middle_ref.shape[0]
    token = lax.broadcasted_iota(jnp.int32, (count, seq_len), 1)
    wanted = jnp.concatenate([wanted] * (seq_len // LANES), axis=1)
    chosen = jnp.where(token == wanted, 1.0, 0.0).astype(jnp.bfloat16)
    slots = dot_nn(chosen, spread_back_ref[...]).astype(jnp.bfloat16)
    weighted = slot_gates(spread_ref[...], gates_ref[...], capacity) * returned_ref[...].astype(
        jnp.float32
    )
    high, rest = two_terms(weighted)
    rows = rows_ref[...] + (dot_nn(slots, high) + dot_nn(slots, rest))
    rows_ref[...] = rows
    low_ref[...] = (rows * inverse_root(rows) * gain_ref[gain_row : gain_row + 1, :]).astype(
        jnp.bfloat16
    )


def final_rows_of(capacity, gain_row, picked, middle, gates, returned, spread, spread_back, gains):
    whole = pl.BlockSpec(memory_space=pltpu.VMEM)
    count = picked.shape[0]
    return pl.pallas_call(
        functools.partial(final_kernel, capacity, gain_row),
        out_shape=(
            jax.ShapeDtypeStruct((count, D), jnp.float32),
            jax.ShapeDtypeStruct((count, D), jnp.bfloat16),
        ),
        in_specs=[pl.BlockSpec(memory_space=pltpu.SMEM)] + [whole] * 6,
        out_specs=[whole] * 2,
        compiler_params=pltpu.CompilerParams(vmem_limit_bytes=48 * 1024 * 1024),
        cost_estimate=pl.CostEstimate(
            flops=1 << 28, bytes_accessed=5 * 1024 * 1024, transcendentals=0
        ),
    )(picked, middle, gates, returned, spread, spread_back, gains)


def tie(first, second):
    return lax.optimization_barrier((first, second))


def swap_pairs(row_groups, turn_plane, turn_row):
    pairs = []
    for plane in range(PLANES):
        for row in range(row_groups):
            for part in range(PLANES):
                source = (plane * row_groups + row) * PLANES + part
                target_plane = (plane + SHIFTS[part ^ turn_plane]) % PLANES
                target_row = (row + turn_row) % row_groups
                pairs.append((source, (target_plane * row_groups + target_row) * PLANES + plane))
    return pairs


def all_turns(row_groups):
    return [(plane, row) for row in range(row_groups) for plane in range(PLANES)]


def shift_inverse(shift):
    return jnp.array(SHIFTS, jnp.int32)[shift]


def part_of_turn(turn_plane):
    me_plane = lax.axis_index("z")
    me_part = lax.axis_index(("y", "c"))
    return shift_inverse((me_plane - me_part) % PLANES) ^ turn_plane


def piece_place(turn, row_groups):
    turn_plane, turn_row = turn
    row = (lax.axis_index("h") - turn_row) % row_groups
    return row * PLANES + part_of_turn(turn_plane)


def spread_experts(piece, row_groups):
    return [
        lax.ppermute(
            piece, ("z", "h", "y", "c"), swap_pairs(row_groups, turn_plane, turn_row)
        )
        for turn_plane, turn_row in all_turns(row_groups)
    ]


def return_expert_grads(pieces, row_groups):
    arrived = []
    for piece, turn in zip(pieces, all_turns(row_groups)):
        back = [(target, source) for source, target in swap_pairs(row_groups, *turn)]
        arrived.append(lax.ppermute(piece, ("z", "h", "y", "c"), back))
    return arrived


def take_piece(pieces, place):
    return lax.dynamic_index_in_dim(pieces, place, 0, False)


def scatter_axis(values, axis_name, dim):
    count = lax.axis_size(axis_name)
    if count == 1:
        return jnp.squeeze(values, dim)
    me = lax.axis_index(axis_name)
    total = lax.dynamic_index_in_dim(values, me, dim, False).astype(jnp.float32)
    for turn in range(1, count):
        sent = lax.dynamic_index_in_dim(values, (me + turn) % count, dim, False)
        got = lax.ppermute(sent, axis_name, [(i, (i + turn) % count) for i in range(count)])
        total = total + got.astype(jnp.float32)
    return total.astype(jnp.bfloat16)


def scatter_near(values):
    sizes = [lax.axis_size(name) for name in AXES]
    rows, columns = values.shape
    count = 1
    for size in sizes:
        count *= size
    blocks = values.reshape(*sizes, rows // count, columns)
    return scatter_axis(blocks, "c", 4)


def scatter_middle(blocks):
    half = blocks.shape[-1] // 2
    return [
        scatter_axis(blocks[..., :half], "x", 1),
        scatter_axis(blocks[..., half:], "y", 3),
    ]


def scatter_turn(parts):
    first = scatter_axis(parts[0], "y", 2)
    second = scatter_axis(parts[1], "x", 1)
    return scatter_axis(jnp.concatenate([first, second], axis=-1), "h", 1)


def scatter_planes(joined):
    planes = lax.axis_size("z")
    me = lax.axis_index("z")
    parts = [take_piece(joined, me)]
    for turn in range(1, planes):
        sent = take_piece(joined, (me + turn) % planes)
        parts.append(lax.ppermute(sent, "z", [(i, (i + turn) % planes) for i in range(planes)]))
    return parts


def scatter_sum(parts):
    total = parts[0].astype(jnp.float32)
    for part in parts[1:]:
        total = total + part.astype(jnp.float32)
    return total


def send_all(values):
    return lax.all_to_all(values, AXES, split_axis=0, concat_axis=0, tiled=True)


def send_plane(values):
    return lax.all_to_all(values, ("x", "y", "c"), split_axis=0, concat_axis=0, tiled=True)


def three_terms(values):
    first = lax.reduce_precision(values, 8, 7)
    second = lax.reduce_precision(values - first, 8, 7)
    third = lax.reduce_precision(values - first - second, 8, 7)
    return [first, second, third]

def adam_step(weight, mean_old, square_old, gradient):
    mean_new = BETA_ONE * mean_old + (1.0 - BETA_ONE) * gradient
    square_new = BETA_TWO * square_old + (1.0 - BETA_TWO) * gradient * gradient
    bias_one = 1.0 - BETA_ONE**ADAM_STEP
    bias_two = 1.0 - BETA_TWO**ADAM_STEP
    update = -LEARN_RATE * (
        mean_new / bias_one / (jnp.sqrt(square_new / bias_two) + ADAM_EPS) + DECAY_RATE * weight
    )
    return (mean_new, square_new, update)


def shards(
    tokens,
    prefix,
    routes,
    picked,
    loss_ids,
    teacher_logits,
    embedding,
    embedding_mean,
    embedding_square,
    attention,
    attention_mean,
    attention_square,
    router,
    router_mean,
    router_square,
    norm_gains,
    gains_mean,
    gains_square,
    expert_up,
    upward_mean,
    upward_square,
    expert_down,
    downward_mean,
    downward_square,
    output_table,
    table_mean,
    table_square,
):
    devices_all = lax.axis_size(AXES)
    me_all = lax.axis_index(AXES)
    row_groups = lax.axis_size("h")
    columns_x = lax.axis_size("x")
    seq_len = routes.shape[0]
    layer_count = attention.shape[0]
    experts_all = router.shape[2]
    capacity = 9 * seq_len * TOPK // (8 * experts_all)
    column_count = embedding.shape[1]
    prefix_len = prefix[0]
    slot_total = experts_all * capacity
    piece_rows = expert_up.shape[2]
    gain_count = norm_gains.shape[0]
    group_experts = [
        (group % PLANES) * columns_x + group // PLANES for group in range(experts_all)
    ]
    group_order = jnp.array(group_experts, jnp.int32)
    group_back = jnp.array(
        [group_experts.index(expert) for expert in range(experts_all)], jnp.int32
    )

    attention_low = lax.all_gather(attention.astype(jnp.bfloat16), AXES, axis=1, tiled=True)

    table_low = embedding.astype(jnp.bfloat16)
    looked_up = jnp.take(table_low, tokens, axis=0).reshape(devices_all, seq_len * column_count)
    small_count = gain_count + layer_count * experts_all
    small = jnp.concatenate(
        [norm_gains.T, router.transpose(1, 0, 2).reshape(column_count, layer_count * experts_all)],
        axis=1,
    ).astype(jnp.bfloat16)
    small = jnp.broadcast_to(
        small.reshape(1, column_count * small_count), (devices_all, column_count * small_count)
    )
    arrived_rows = send_all(jnp.concatenate([looked_up, small], axis=1))
    hidden = (
        arrived_rows[:, : seq_len * column_count]
        .reshape(devices_all, seq_len, column_count)
        .transpose(1, 0, 2)
        .reshape(seq_len, D)
        .astype(jnp.float32)
    )
    small_all = arrived_rows[:, seq_len * column_count :].reshape(D, small_count)
    gain_rows = jnp.pad(
        small_all[:, :gain_count].T.astype(jnp.float32), ((0, 16 - gain_count), (0, 0))
    )
    router_low = jnp.pad(
        small_all[:, gain_count:]
        .reshape(D, layer_count, experts_all)
        .transpose(1, 0, 2)[:, :, group_order],
        ((0, 0), (0, 0), (0, LANES - experts_all)),
    )

    head_low = output_table.astype(jnp.bfloat16)
    vocab_local = head_low.shape[0]
    teacher_log = jax.nn.log_softmax(teacher_logits, axis=1)
    teacher_prob = jnp.exp(teacher_log)
    position_count = loss_ids.shape[0]
    teacher_mass = jnp.sum(teacher_prob, axis=1)
    coefficients = jnp.concatenate(
        [jnp.ones((position_count, 1), jnp.float32), teacher_prob], axis=1
    )
    local_ids = loss_ids - me_all * vocab_local
    vocab_place = jnp.arange(vocab_local, dtype=jnp.int32)
    marked = jnp.sum(
        jnp.where(
            local_ids[:, :, None] == vocab_place[None, None, :], coefficients[:, :, None], 0.0
        ),
        axis=1,
    )
    marked_pull = jnp.dot(
        marked.astype(jnp.bfloat16), head_low, preferred_element_type=jnp.float32
    )
    own_count = position_count // devices_all
    marked_arrived = send_all(
        marked_pull.astype(jnp.bfloat16).reshape(devices_all, own_count, D)
    )

    expert_parts = []
    for layer_index in range(layer_count):
        if layer_index == 1:
            attention_low, marked, marked_arrived = lax.optimization_barrier(
                (attention_low, marked, marked_arrived)
            )
        down_piece = (
            expert_down[0, layer_index]
            .reshape(F // piece_rows, piece_rows, piece_rows)
            .transpose(1, 0, 2)
            .reshape(piece_rows, F)
        )
        piece = jnp.concatenate([expert_up[0, layer_index], down_piece], axis=1).astype(
            jnp.bfloat16
        )
        if layer_index > 0:
            piece, attention_low = tie(piece, attention_low)
        expert_parts.append(spread_experts(piece, row_groups))

    member = jnp.any(routes[:, :, None] == group_order[None, None, :], axis=1)
    before = jnp.dot(
        jnp.tril(jnp.ones((seq_len, seq_len), jnp.bfloat16), -1),
        member.astype(jnp.bfloat16),
        preferred_element_type=jnp.float32,
    ).astype(jnp.int32)
    spread = (
        (before.T[:, None, :] == jnp.arange(capacity, dtype=jnp.int32)[None, :, None])
        & member.T[:, None, :]
    ).astype(jnp.bfloat16)
    spread_flat = spread.reshape(slot_total, seq_len)
    spread_back = spread_flat.T
    kept = jnp.pad(
        (member & (before < capacity)).astype(jnp.float32), ((0, 0), (0, LANES - experts_all))
    )
    turns = turn_tables(seq_len)
    places = jnp.stack([piece_place(turn, row_groups) for turn in all_turns(row_groups)]).astype(
        jnp.int32
    )

    stored = []
    extra = ()
    for layer_index in range(layer_count):
        saved = forward_layer(
            layer_index,
            capacity,
            experts_all,
            prefix,
            hidden,
            extra,
            attention_low,
            gain_rows,
            turns,
            router_low,
            kept,
            spread_flat,
            spread_back,
        )
        hidden = saved[6]
        gates, outgoing = saved[9], saved[10]
        if layer_index > 0:
            expert_parts[layer_index][2], outgoing = tie(expert_parts[layer_index][2], outgoing)
        received = send_plane(outgoing.reshape(experts_all, capacity, D)).reshape(slot_total, D)
        upcoming = expert_parts[layer_index + 1] if layer_index + 1 < layer_count else None
        if upcoming is not None:
            upcoming[0], received = tie(upcoming[0], received)
        produced = run_expert(places, received, expert_parts[layer_index])
        returned = send_plane(produced.reshape(experts_all, capacity, D)).reshape(slot_total, D)
        if upcoming is not None:
            upcoming[1], returned = tie(upcoming[1], returned)
        stored.append((saved, received, returned))
        extra = (gates, returned)

    final_gain = gain_rows[4 * layer_count]
    final_rows, final_low = final_rows_of(
        capacity,
        4 * layer_count,
        picked,
        hidden,
        *extra,
        spread_flat,
        spread_back,
        gain_rows,
    )
    all_rows = send_all(jnp.broadcast_to(final_low[None], (devices_all, own_count, D))).reshape(
        position_count, D
    )
    logits = jnp.einsum("pd,vd->pv", all_rows, head_low, preferred_element_type=jnp.float32)
    local_peak = jnp.max(logits, axis=1)
    local_exp = jnp.exp(logits - local_peak[:, None])
    local_sum = jnp.sum(local_exp, axis=1)
    local_dot = jnp.sum(marked * logits, axis=1)
    pull = jnp.dot(local_exp.astype(jnp.bfloat16), head_low, preferred_element_type=jnp.float32)
    stats = jnp.stack(
        three_terms(local_peak) + three_terms(local_sum) + three_terms(local_dot), axis=1
    )
    stats = jnp.pad(stats, ((0, 0), (0, 128 - stats.shape[1])))
    pull_sent = jnp.concatenate([pull, stats], axis=1).astype(jnp.bfloat16)
    pull_got = send_all(pull_sent.reshape(devices_all, own_count, D + 128)).astype(jnp.float32)
    stats_got = pull_got[:, :, D:]
    peaks = jnp.sum(stats_got[:, :, 0:3], axis=2)
    sums = jnp.sum(stats_got[:, :, 3:6], axis=2)
    dots = jnp.sum(stats_got[:, :, 6:9], axis=2)
    peak_own = jnp.max(peaks, axis=0)
    log_norm_own = peak_own + jnp.log(jnp.sum(sums * jnp.exp(peaks - peak_own), axis=0))
    mass_own = lax.dynamic_slice_in_dim(teacher_mass, me_all * own_count, own_count)
    entropy_own = lax.dynamic_slice_in_dim(
        jnp.sum(teacher_prob * teacher_log, axis=1), me_all * own_count, own_count
    )
    loss_own = (1.0 + mass_own) * log_norm_own - jnp.sum(dots, axis=0) + entropy_own
    scale_own = (1.0 + mass_own)[None, :] * jnp.exp(peaks - log_norm_own[None, :])
    marked_total = jnp.sum(marked_arrived.astype(jnp.float32), axis=0)
    final_grad = (
        jnp.sum(scale_own[:, :, None] * pull_got[:, :, :D], axis=0) - marked_total
    ) / position_count
    spread_stats = jnp.concatenate([log_norm_own, loss_own]).reshape(1, 2 * own_count)
    stats_all = send_all(jnp.broadcast_to(spread_stats, (devices_all, 2 * own_count)))
    log_norm = stats_all[:, :own_count].reshape(position_count)
    loss_value = jnp.sum(stats_all[:, own_count:]) / position_count
    grad_logits = (
        jnp.exp(logits - log_norm[:, None]) * (1.0 + teacher_mass)[:, None] - marked
    ) / position_count
    table_grad = jnp.einsum(
        "pv,pd->vd",
        grad_logits.astype(jnp.bfloat16),
        all_rows,
        preferred_element_type=jnp.float32,
    )
    rows_grad, final_gain_grad = norm_back(final_rows, final_gain, final_grad)
    grad_hidden, sent_back = first_pull(capacity, picked, rows_grad, spread_flat, extra[0])
    gain_parts = [None] * (4 * layer_count) + [final_gain_grad]
    attention_parts = [None] * layer_count
    router_parts = [None] * layer_count
    piece_parts = [None] * layer_count
    for layer_index in reversed(range(layer_count)):
        saved, received, returned = stored[layer_index]
        hidden_in, projected, queries, keys, values, attended, middle, ffn_low, probs = saved[:9]
        upper = layer_index + 1 if layer_index + 1 < layer_count else None
        output_grad = send_plane(sent_back.reshape(experts_all, capacity, D)).reshape(
            slot_total, D
        )
        logit_low, router_parts[layer_index] = router_back(
            capacity, grad_hidden, returned, spread_back, probs, ffn_low
        )
        if upper is not None:
            near, output_grad = tie(attention_parts[upper], output_grad)
            middle_parts = scatter_middle(near)
        input_grad, gate_grad, activated = run_expert_back(
            places, received, output_grad, expert_parts[layer_index]
        )
        back_inputs = send_plane(input_grad.reshape(experts_all, capacity, D)).reshape(
            slot_total, D
        )
        grad_pieces = run_expert_grad(
            places, received, output_grad, gate_grad, activated, piece_rows
        )
        piece_parts[layer_index] = return_expert_grads(grad_pieces, row_groups)
        if upper is not None:
            piece_parts[upper][2:], back_inputs = tie(piece_parts[upper][2:], back_inputs)
        lower = (spread_flat, stored[layer_index - 1][0][9]) if layer_index > 0 else ()
        results = backward_layer(
            layer_index,
            capacity,
            prefix,
            grad_hidden,
            back_inputs,
            logit_low,
            hidden_in,
            projected,
            queries,
            keys,
            values,
            attended,
            middle,
            attention_low,
            gain_rows,
            turns,
            router_low,
            spread_back,
            lower,
        )
        grad_hidden, weight_grad, gain_grads = results[:3]
        gain_parts[4 * layer_index : 4 * layer_index + 4] = list(gain_grads[:4])
        if layer_index > 0:
            sent_back = results[3]
            piece_parts[layer_index][:2], sent_back = tie(piece_parts[layer_index][:2], sent_back)
        attention_parts[layer_index] = scatter_near(weight_grad)
        if upper is not None:
            middle_parts, grad_hidden = tie(middle_parts, grad_hidden)
            attention_parts[upper] = scatter_sum(scatter_planes(scatter_turn(middle_parts)))

    sending = (
        grad_hidden.astype(jnp.bfloat16)
        .reshape(seq_len, devices_all, column_count)
        .transpose(1, 0, 2)
        .reshape(devices_all, seq_len * column_count)
    )
    small_grads = jnp.concatenate(
        [jnp.stack(gain_parts, axis=1)] + [part[:, group_back] for part in router_parts], axis=1
    ).astype(jnp.bfloat16)
    arrived_grads = send_all(
        jnp.concatenate(
            [sending, small_grads.reshape(devices_all, column_count * small_count)], axis=1
        )
    )
    attention_parts[0], arrived_grads, piece_parts = lax.optimization_barrier(
        (attention_parts[0], arrived_grads, piece_parts)
    )
    attention_parts[0] = scatter_sum(
        scatter_planes(scatter_turn(scatter_middle(attention_parts[0])))
    )
    up_parts, down_parts = [], []
    for parts in piece_parts:
        piece_grad = scatter_sum(parts)
        up_parts.append(piece_grad[:, : 2 * F])
        down_parts.append(
            piece_grad[:, 2 * F :]
            .reshape(piece_rows, F // piece_rows, piece_rows)
            .transpose(1, 0, 2)
            .reshape(F, piece_rows)
        )
    embedding_grad = jax.ops.segment_sum(
        arrived_grads[:, : seq_len * column_count]
        .astype(jnp.float32)
        .reshape(devices_all * seq_len, column_count),
        tokens,
        num_segments=embedding.shape[0],
    )
    small_total = jnp.sum(
        arrived_grads[:, seq_len * column_count :].astype(jnp.float32), axis=0
    ).reshape(column_count, small_count)
    gains_grad = small_total[:, :gain_count].T
    router_grad = (
        small_total[:, gain_count:]
        .reshape(column_count, layer_count, experts_all)
        .transpose(1, 0, 2)
    )
    attention_grad = jnp.stack(attention_parts)
    upward_grad = jnp.stack(up_parts)[None]
    downward_grad = jnp.stack(down_parts)[None]
    embedding_mean_next, embedding_square_next, embedding_update = adam_step(
        embedding, embedding_mean, embedding_square, embedding_grad
    )
    attention_mean_next, attention_square_next, attention_update = adam_step(
        attention, attention_mean, attention_square, attention_grad
    )
    router_mean_next, router_square_next, router_update = adam_step(
        router, router_mean, router_square, router_grad
    )
    gains_mean_next, gains_square_next, gains_update = adam_step(
        norm_gains, gains_mean, gains_square, gains_grad
    )
    upward_mean_next, upward_square_next, upward_update = adam_step(
        expert_up, upward_mean, upward_square, upward_grad
    )
    downward_mean_next, downward_square_next, downward_update = adam_step(
        expert_down, downward_mean, downward_square, downward_grad
    )
    table_mean_next, table_square_next, table_update = adam_step(
        output_table, table_mean, table_square, table_grad
    )
    return (
        loss_value,
        embedding_mean_next,
        embedding_square_next,
        embedding_update,
        attention_mean_next,
        attention_square_next,
        attention_update,
        router_mean_next,
        router_square_next,
        router_update,
        gains_mean_next,
        gains_square_next,
        gains_update,
        upward_mean_next,
        upward_square_next,
        upward_update,
        downward_mean_next,
        downward_square_next,
        downward_update,
        table_mean_next,
        table_square_next,
        table_update,
    )


def solution(mesh):
    expert_count, shard_count = mesh.devices.shape
    mesh = Mesh(
        mesh.devices.reshape(PLANES, expert_count // PLANES, shard_count // 4, 2, 2), AXES
    )
    return jax.shard_map(
        shards,
        mesh=mesh,
        in_specs=(
            P(),
            P(AXES),
            P(AXES, None),
            P(AXES),
            P(),
            P(),
            P(None, AXES),
            P(None, AXES),
            P(None, AXES),
            P(None, AXES, None),
            P(None, AXES, None),
            P(None, AXES, None),
            P(None, AXES, None),
            P(None, AXES, None),
            P(None, AXES, None),
            P(None, AXES),
            P(None, AXES),
            P(None, AXES),
            P(("z", "x"), None, ("h", "y", "c"), None),
            P(("z", "x"), None, ("h", "y", "c"), None),
            P(("z", "x"), None, ("h", "y", "c"), None),
            P(("z", "x"), None, None, ("h", "y", "c")),
            P(("z", "x"), None, None, ("h", "y", "c")),
            P(("z", "x"), None, None, ("h", "y", "c")),
            P(AXES, None),
            P(AXES, None),
            P(AXES, None),
        ),
        out_specs=(
            P(),
            P(None, AXES),
            P(None, AXES),
            P(None, AXES),
            P(None, AXES, None),
            P(None, AXES, None),
            P(None, AXES, None),
            P(None, AXES, None),
            P(None, AXES, None),
            P(None, AXES, None),
            P(None, AXES),
            P(None, AXES),
            P(None, AXES),
            P(("z", "x"), None, ("h", "y", "c"), None),
            P(("z", "x"), None, ("h", "y", "c"), None),
            P(("z", "x"), None, ("h", "y", "c"), None),
            P(("z", "x"), None, None, ("h", "y", "c")),
            P(("z", "x"), None, None, ("h", "y", "c")),
            P(("z", "x"), None, None, ("h", "y", "c")),
            P(AXES, None),
            P(AXES, None),
            P(AXES, None),
        ),
        check_vma=False,
    )
```

```python
import functools

import jax
import jax.numpy as jnp
from jax import lax
from jax.experimental import pallas as pl
from jax.experimental.pallas import tpu as pltpu
from jax.sharding import Mesh, PartitionSpec as P

D = 1024
HEADS = 16
HDIM = 64
F = 512
TOPK = 4
ADAM_STEP = 10


EPS_NORM = 1e-05
BETA_ONE = 0.9
BETA_TWO = 0.95
ADAM_EPS = 1e-08
LEARN_RATE = 0.01
DECAY_RATE = 0.1
ROPE_BASE = 10000.0
MASK_FILL = -1e30


def rms_norm(inputs, gain_row):
    return (
        inputs * lax.rsqrt(jnp.mean(inputs * inputs, axis=-1, keepdims=True) + EPS_NORM) * gain_row
    )


def norm_back(inputs, gain_row, upstream):
    _, pullback = jax.vjp(rms_norm, inputs, gain_row)
    return pullback(upstream)


AXES = ("z", "x", "h", "y", "c")
PLANES = 4
SHIFTS = (0, 2, 1, 3)
LANES = 128
CHUNKS = D // LANES


def dot_nn(left, right):
    return lax.dot_general(
        left, right, (((1,), (0,)), ((), ())), preferred_element_type=jnp.float32
    )


def dot_nt(left, right):
    return lax.dot_general(
        left, right, (((1,), (1,)), ((), ())), preferred_element_type=jnp.float32
    )


def dot_tn(left, right):
    return lax.dot_general(
        left, right, (((0,), (0,)), ((), ())), preferred_element_type=jnp.float32
    )


def inverse_root(values):
    return lax.rsqrt(jnp.mean(values * values, axis=-1, keepdims=True) + EPS_NORM)


def two_terms(values):
    high = values.astype(jnp.bfloat16)
    return high, (values - high.astype(jnp.float32)).astype(jnp.bfloat16)


def chunk(values, place):
    return values[:, place * LANES : (place + 1) * LANES]


def half_turn(values):
    lane = lax.broadcasted_iota(jnp.int32, values.shape, 1)
    ahead = pltpu.roll(values, LANES - HDIM // 2, 1)
    behind = pltpu.roll(values, HDIM // 2, 1)
    return jnp.where(lane % HDIM < HDIM // 2, ahead, behind)


def slot_gates(spread, gates, capacity):
    high, rest = two_terms(gates)
    full = dot_nn(spread, high) + dot_nn(spread, rest)
    expert = lax.broadcasted_iota(jnp.int32, full.shape, 0) // capacity
    lane = lax.broadcasted_iota(jnp.int32, full.shape, 1)
    return jnp.sum(jnp.where(lane == expert, full, 0.0), axis=1, keepdims=True)


def combine(middle, spread, spread_back, gates, returned, capacity):
    weighted = slot_gates(spread, gates, capacity) * returned.astype(jnp.float32)
    high, rest = two_terms(weighted)
    return middle + (dot_nn(spread_back, high) + dot_nn(spread_back, rest))


def masked_probs(query, key, visible):
    scores = dot_nt(query, key) * HDIM ** (-0.5)
    scores = jnp.where(visible, scores, MASK_FILL)
    weights = jnp.exp(scores - jnp.max(scores, axis=-1, keepdims=True))
    return weights / jnp.sum(weights, axis=-1, keepdims=True)


def visible_keys(prefix_ref, seq_len):
    query_place = lax.broadcasted_iota(jnp.int32, (seq_len, seq_len), 0)
    key_place = lax.broadcasted_iota(jnp.int32, (seq_len, seq_len), 1)
    return (key_place <= query_place) | (key_place < prefix_ref[0])


def head_masks(seq_len):
    lane = lax.broadcasted_iota(jnp.int32, (seq_len, LANES), 1)
    return lane < HDIM, lane >= HDIM


def fetch_weights(weight_ref, held_ref, copy_sem, order):
    copies = {}
    for part in order:
        copies[part] = pltpu.make_async_copy(
            weight_ref.at[:, pl.ds(part * D, D)], held_ref.at[part], copy_sem.at[part]
        )
        copies[part].start()
    return copies


def forward_kernel(
    layer_index,
    capacity,
    expert_count,
    prefix_ref,
    hidden_ref,
    *refs,
):
    if layer_index > 0:
        gates_in_ref, returned_ref, refs = refs[0], refs[1], refs[2:]
    (
        weight_ref,
        gain_ref,
        turn_ref,
        router_ref,
        kept_ref,
        spread_ref,
        spread_back_ref,
        hidden_out_ref,
        projected_ref,
        query_ref,
        key_ref,
        value_ref,
        attended_ref,
        middle_ref,
        ffn_ref,
        probs_ref,
        gates_ref,
        outgoing_ref,
        held_ref,
        copy_sem,
    ) = refs
    copies = fetch_weights(weight_ref, held_ref, copy_sem, (0, 1, 2, 3))
    seq_len = hidden_ref.shape[0]
    hidden = hidden_ref[...]
    if layer_index > 0:
        hidden = combine(
            hidden,
            spread_ref[...],
            spread_back_ref[...],
            gates_in_ref[...],
            returned_ref[...],
            capacity,
        )
    hidden_out_ref[...] = hidden
    row = 4 * layer_index
    normed = (hidden * inverse_root(hidden) * gain_ref[row : row + 1, :]).astype(jnp.bfloat16)
    cosines, sines = turn_ref[0], turn_ref[1]
    for part, out_ref in ((0, query_ref), (1, key_ref)):
        columns = slice(part * D, (part + 1) * D)
        copies[part].wait()
        projected = dot_nn(normed, held_ref[part])
        projected_ref[:, columns] = projected
        scaled = projected * inverse_root(projected) * gain_ref[row + 1 + part : row + 2 + part, :]
        for place in range(CHUNKS):
            block = chunk(scaled, place)
            out_ref[:, place * LANES : (place + 1) * LANES] = (
                block * cosines + half_turn(block) * sines
            ).astype(jnp.bfloat16)
    copies[2].wait()
    value_ref[...] = dot_nn(normed, held_ref[2]).astype(jnp.bfloat16)
    visible = visible_keys(prefix_ref, seq_len)
    masks = head_masks(seq_len)
    zero = jnp.zeros((), jnp.bfloat16)
    for place in range(CHUNKS):
        columns = slice(place * LANES, (place + 1) * LANES)
        query, key, value = query_ref[:, columns], key_ref[:, columns], value_ref[:, columns]
        total = None
        for mask in masks:
            probs = masked_probs(query, jnp.where(mask, key, zero), visible).astype(jnp.bfloat16)
            term = dot_nn(probs, jnp.where(mask, value, zero))
            total = term if total is None else total + term
        attended_ref[:, columns] = total.astype(jnp.bfloat16)
    copies[3].wait()
    middle = hidden + dot_nn(attended_ref[...], held_ref[3])
    middle_ref[...] = middle
    ffn = (middle * inverse_root(middle) * gain_ref[row + 3 : row + 4, :]).astype(jnp.bfloat16)
    ffn_ref[...] = ffn
    outgoing_ref[...] = dot_nn(spread_ref[...], ffn).astype(jnp.bfloat16)
    logits = dot_nn(ffn, router_ref[layer_index])
    lane = lax.broadcasted_iota(jnp.int32, logits.shape, 1)
    logits = jnp.where(lane < expert_count, logits, MASK_FILL)
    weights = jnp.exp(logits - jnp.max(logits, axis=-1, keepdims=True))
    probs = weights / jnp.sum(weights, axis=-1, keepdims=True)
    probs_ref[...] = probs
    gates_ref[...] = probs * kept_ref[...]


def forward_layer(
    layer_index,
    capacity,
    expert_count,
    prefix,
    hidden,
    extra,
    weights,
    gains,
    turns,
    router,
    kept,
    spread,
    spread_back,
):
    seq_len = hidden.shape[0]
    whole = pl.BlockSpec(memory_space=pltpu.VMEM)
    wide = jax.ShapeDtypeStruct((seq_len, D), jnp.float32)
    low = jax.ShapeDtypeStruct((seq_len, D), jnp.bfloat16)
    small = jax.ShapeDtypeStruct((seq_len, LANES), jnp.float32)
    return pl.pallas_call(
        functools.partial(forward_kernel, layer_index, capacity, expert_count),
        out_shape=(
            wide,
            jax.ShapeDtypeStruct((seq_len, 2 * D), jnp.float32),
            low,
            low,
            low,
            low,
            wide,
            low,
            small,
            small,
            jax.ShapeDtypeStruct((spread.shape[0], D), jnp.bfloat16),
        ),
        in_specs=[pl.BlockSpec(memory_space=pltpu.SMEM), whole]
        + [whole] * len(extra)
        + [pl.BlockSpec(memory_space=pl.ANY)]
        + [whole] * 6,
        out_specs=[whole] * 11,
        scratch_shapes=[
            pltpu.VMEM((4, D, D), jnp.bfloat16),
            pltpu.SemaphoreType.DMA((4,)),
        ],
        compiler_params=pltpu.CompilerParams(vmem_limit_bytes=60 * 1024 * 1024),
        cost_estimate=pl.CostEstimate(
            flops=4 * seq_len * D * D * 3, bytes_accessed=24 * 1024 * 1024, transcendentals=1 << 20
        ),
    )(prefix, hidden, *extra, weights, gains, turns, router, kept, spread, spread_back)


def norm_pull(values, gain, upstream):
    root = inverse_root(values)
    scaled = values * root
    weighted = upstream * gain
    mean = jnp.mean(weighted * scaled, axis=-1, keepdims=True)
    return root * (weighted - scaled * mean), jnp.sum(upstream * scaled, axis=0, keepdims=True)


def backward_kernel(
    layer_index,
    capacity,
    prefix_ref,
    grad_ref,
    back_ref,
    logit_ref,
    hidden_ref,
    projected_ref,
    query_ref,
    key_ref,
    value_ref,
    attended_ref,
    middle_ref,
    weight_ref,
    gain_ref,
    turn_ref,
    router_ref,
    spread_back_ref,
    *refs,
):
    if layer_index > 0:
        spread_ref, gates_ref, refs = refs[0], refs[1], refs[2:]
        outgoing_ref, refs = refs[3], refs[:3] + refs[4:]
    grad_out_ref, weight_grad_ref, gain_grad_ref, pull_ref, key_pull_ref, held_ref, copy_sem = refs
    copies = fetch_weights(weight_ref, held_ref, copy_sem, (3, 2, 0, 1))
    seq_len = hidden_ref.shape[0]
    row = 4 * layer_index
    ffn_grad = dot_nn(spread_back_ref[...], back_ref[...]) + dot_nt(
        logit_ref[...], router_ref[layer_index]
    )
    middle_grad, gain_three = norm_pull(
        middle_ref[...], gain_ref[row + 3 : row + 4, :], ffn_grad
    )
    grad_middle = grad_ref[...] + middle_grad
    grad_out_ref[...] = grad_middle
    branch = grad_middle.astype(jnp.bfloat16)
    weight_grad_ref[:, 3 * D :] = dot_tn(attended_ref[...], branch).astype(jnp.bfloat16)
    copies[3].wait()
    pull_ref[...] = dot_nt(branch, held_ref[3]).astype(jnp.bfloat16)
    visible = visible_keys(prefix_ref, seq_len)
    masks = head_masks(seq_len)
    zero = jnp.zeros((), jnp.bfloat16)
    cosines, sines = turn_ref[0], turn_ref[1]
    factor = HDIM ** (-0.5)
    hidden = hidden_ref[...]
    normed = (hidden * inverse_root(hidden) * gain_ref[row : row + 1, :]).astype(jnp.bfloat16)
    for place in range(CHUNKS):
        columns = slice(place * LANES, (place + 1) * LANES)
        query, key, value = query_ref[:, columns], key_ref[:, columns], value_ref[:, columns]
        pull = pull_ref[:, columns]
        totals = [None, None, None]
        for mask in masks:
            key_half = jnp.where(mask, key, zero)
            probs = masked_probs(query, key_half, visible)
            pulled = dot_nt(pull, jnp.where(mask, value, zero))
            inner = jnp.sum(probs * pulled, axis=-1, keepdims=True)
            score_grad = (probs * (pulled - inner)).astype(jnp.bfloat16)
            terms = (
                dot_nn(score_grad, key_half),
                dot_tn(score_grad, jnp.where(mask, query, zero)),
                dot_tn(probs.astype(jnp.bfloat16), jnp.where(mask, pull, zero)),
            )
            totals = [b if a is None else a + b for a, b in zip(totals, terms)]
        for part, target_ref in ((0, key_pull_ref.at[0]), (1, key_pull_ref.at[1])):
            turned = (totals[part] * factor).astype(jnp.bfloat16).astype(jnp.float32)
            target_ref[:, columns] = turned * cosines - half_turn(turned) * sines
        pull_ref[:, columns] = totals[2].astype(jnp.bfloat16)
    gain_rows = []
    value_pull = pull_ref[...]
    copies[2].wait()
    back = dot_nt(value_pull, held_ref[2])
    weight_grad_ref[:, 2 * D : 3 * D] = dot_tn(normed, value_pull).astype(jnp.bfloat16)
    for part in range(2):
        columns = slice(part * D, (part + 1) * D)
        input_pull, gain_row = norm_pull(
            projected_ref[:, columns],
            gain_ref[row + 1 + part : row + 2 + part, :],
            key_pull_ref[part],
        )
        gain_rows.append(gain_row)
        low_pull = input_pull.astype(jnp.bfloat16)
        weight_grad_ref[:, columns] = dot_tn(normed, low_pull).astype(jnp.bfloat16)
        copies[part].wait()
        back = back + dot_nt(low_pull, held_ref[part])
    hidden_grad, gain_zero = norm_pull(hidden, gain_ref[row : row + 1, :], back)
    grad_out = grad_out_ref[...] + hidden_grad
    grad_out_ref[...] = grad_out
    if layer_index > 0:
        outgoing_ref[...] = outgoing_pull(grad_out, spread_ref[...], gates_ref[...], capacity)
    gain_grad_ref[...] = jnp.concatenate(
        [gain_zero] + gain_rows + [gain_three, jnp.zeros((4, D), jnp.float32)], axis=0
    )


def backward_layer(
    layer_index,
    capacity,
    prefix,
    grad,
    back_inputs,
    logit_low,
    hidden,
    projected,
    queries,
    keys,
    values,
    attended,
    middle,
    weights,
    gains,
    turns,
    router,
    spread_back,
    extra,
):
    seq_len = hidden.shape[0]
    whole = pl.BlockSpec(memory_space=pltpu.VMEM)
    out_shape = [
        jax.ShapeDtypeStruct((seq_len, D), jnp.float32),
        jax.ShapeDtypeStruct((D, 4 * D), jnp.bfloat16),
        jax.ShapeDtypeStruct((8, D), jnp.float32),
    ]
    if layer_index > 0:
        out_shape.append(jax.ShapeDtypeStruct((spread_back.shape[1], D), jnp.bfloat16))
    return pl.pallas_call(
        functools.partial(backward_kernel, layer_index, capacity),
        out_shape=out_shape,
        in_specs=[pl.BlockSpec(memory_space=pltpu.SMEM)]
        + [whole] * 10
        + [pl.BlockSpec(memory_space=pl.ANY)]
        + [whole] * (4 + len(extra)),
        out_specs=[whole] * len(out_shape),
        scratch_shapes=[
            pltpu.VMEM((seq_len, D), jnp.bfloat16),
            pltpu.VMEM((2, seq_len, D), jnp.float32),
            pltpu.VMEM((4, D, D), jnp.bfloat16),
            pltpu.SemaphoreType.DMA((4,)),
        ],
        compiler_params=pltpu.CompilerParams(vmem_limit_bytes=60 * 1024 * 1024),
        cost_estimate=pl.CostEstimate(
            flops=8 * seq_len * D * D * 3, bytes_accessed=32 * 1024 * 1024, transcendentals=1 << 20
        ),
    )(
        prefix,
        grad,
        back_inputs,
        logit_low,
        hidden,
        projected,
        queries,
        keys,
        values,
        attended,
        middle,
        weights,
        gains,
        turns,
        router,
        spread_back,
        *extra,
    )


def turn_tables(seq_len):
    position = jnp.arange(seq_len, dtype=jnp.float32)[:, None]
    frequency = ROPE_BASE ** (-jnp.arange(HDIM // 2, dtype=jnp.float32) * 2.0 / HDIM)
    angles = position * frequency[None, :]
    cosines, sines = jnp.cos(angles), jnp.sin(angles)
    return jnp.stack(
        [
            jnp.concatenate([cosines] * 4, axis=1),
            jnp.concatenate([-sines, sines, -sines, sines], axis=1),
        ]
    )


def silu_parts(gate_up):
    gate_part, up_part = gate_up[:, :F], gate_up[:, F:]
    sigmoid = 1.0 / (1.0 + jnp.exp(-gate_part))
    return gate_part, up_part, sigmoid


def fetch_expert(place_ref, part_refs, up_ref, down_ref, copy_sem):
    copies = []
    rows = part_refs[0].shape[0]
    for turn, part_ref in enumerate(part_refs):
        place = pl.multiple_of(place_ref[turn] * rows, rows)
        copies.append(
            pltpu.make_async_copy(
                part_ref.at[:, pl.ds(0, 2 * F)],
                up_ref.at[pl.ds(place, rows), :],
                copy_sem.at[len(copies)],
            )
        )
        for block in range(F // rows):
            copies.append(
                pltpu.make_async_copy(
                    part_ref.at[:, pl.ds(2 * F + block * rows, rows)],
                    down_ref.at[pl.ds(block * rows, rows), pl.ds(place, rows)],
                    copy_sem.at[len(copies)],
                )
            )
    for copy in copies:
        copy.start()
    for copy in copies:
        copy.wait()


def expert_kernel(part_count, row_block, place_ref, received_ref, *refs):
    part_refs, (produced_ref, up_ref, down_ref, copy_sem) = refs[:part_count], refs[part_count:]
    fetch_expert(place_ref, part_refs, up_ref, down_ref, copy_sem)

    @pl.loop(0, received_ref.shape[0] // row_block)
    def _(step):
        rows = pl.ds(pl.multiple_of(step * row_block, row_block), row_block)
        gate_part, up_part, sigmoid = silu_parts(dot_nn(received_ref[rows, :], up_ref[...]))
        activated = (gate_part * sigmoid * up_part).astype(jnp.bfloat16)
        produced_ref[rows, :] = dot_nn(activated, down_ref[...]).astype(jnp.bfloat16)


def expert_specs(parts):
    rows = parts[0].shape[0]
    whole = pl.BlockSpec(memory_space=pltpu.VMEM)
    specs = [pl.BlockSpec(memory_space=pltpu.SMEM)]
    apart = [pl.BlockSpec(memory_space=pl.ANY)] * len(parts)
    scratch = [
        pltpu.VMEM((D, 2 * F), jnp.bfloat16),
        pltpu.VMEM((F, D), jnp.bfloat16),
        pltpu.SemaphoreType.DMA((len(parts) * (1 + F // rows),)),
    ]
    return whole, specs, apart, scratch


def run_expert(places, received, parts):
    whole, specs, apart, scratch = expert_specs(parts)
    slot_total = received.shape[0]
    return pl.pallas_call(
        functools.partial(expert_kernel, len(parts), slot_total // 4),
        out_shape=jax.ShapeDtypeStruct((slot_total, D), jnp.bfloat16),
        in_specs=specs + [whole] + apart,
        out_specs=whole,
        scratch_shapes=scratch,
        compiler_params=pltpu.CompilerParams(vmem_limit_bytes=56 * 1024 * 1024),
        cost_estimate=pl.CostEstimate(
            flops=slot_total * D * F * 6, bytes_accessed=8 * 1024 * 1024, transcendentals=1 << 19
        ),
    )(places, received, *parts)


def expert_back_kernel(part_count, row_block, place_ref, received_ref, pull_ref, *refs):
    part_refs, refs = refs[:part_count], refs[part_count:]
    input_grad_ref, gate_grad_ref, activated_ref, up_ref, down_ref, copy_sem = refs
    fetch_expert(place_ref, part_refs, up_ref, down_ref, copy_sem)

    @pl.loop(0, received_ref.shape[0] // row_block)
    def _(step):
        rows = pl.ds(pl.multiple_of(step * row_block, row_block), row_block)
        gate_part, up_part, sigmoid = silu_parts(dot_nn(received_ref[rows, :], up_ref[...]))
        side = gate_part * sigmoid
        activated_ref[rows, :] = (side * up_part).astype(jnp.bfloat16)
        pulled = dot_nt(pull_ref[rows, :], down_ref[...]).astype(jnp.bfloat16)
        pulled = pulled.astype(jnp.float32)
        gate_side = pulled * up_part * sigmoid * (1.0 + gate_part * (1.0 - sigmoid))
        gate_grad_ref[rows, :F] = gate_side.astype(jnp.bfloat16)
        gate_grad_ref[rows, F:] = (pulled * side).astype(jnp.bfloat16)
        input_grad_ref[rows, :] = dot_nt(gate_grad_ref[rows, :], up_ref[...]).astype(jnp.bfloat16)


def run_expert_back(places, received, pull, parts):
    whole, specs, apart, scratch = expert_specs(parts)
    slot_total = received.shape[0]
    return pl.pallas_call(
        functools.partial(expert_back_kernel, len(parts), slot_total // 4),
        out_shape=(
            jax.ShapeDtypeStruct((slot_total, D), jnp.bfloat16),
            jax.ShapeDtypeStruct((slot_total, 2 * F), jnp.bfloat16),
            jax.ShapeDtypeStruct((slot_total, F), jnp.bfloat16),
        ),
        in_specs=specs + [whole] * 2 + apart,
        out_specs=[whole] * 3,
        scratch_shapes=scratch,
        compiler_params=pltpu.CompilerParams(vmem_limit_bytes=56 * 1024 * 1024),
        cost_estimate=pl.CostEstimate(
            flops=slot_total * D * F * 12, bytes_accessed=12 * 1024 * 1024, transcendentals=1 << 19
        ),
    )(places, received, pull, *parts)


def expert_grad_kernel(
    part_count, place_ref, received_ref, pull_ref, gate_grad_ref, activated_ref, *refs
):
    out_refs, (up_ref, down_ref) = refs[:part_count], refs[part_count:]
    block = 256

    @pl.loop(0, D // block)
    def _(step):
        columns = pl.ds(pl.multiple_of(step * block, block), block)
        up_ref[columns, :] = dot_tn(received_ref[:, columns], gate_grad_ref[...]).astype(
            jnp.bfloat16
        )

    @pl.loop(0, F // block)
    def _(step):
        columns = pl.ds(pl.multiple_of(step * block, block), block)
        down_ref[columns, :] = dot_tn(activated_ref[:, columns], pull_ref[...]).astype(
            jnp.bfloat16
        )

    rows = out_refs[0].shape[0]
    for turn, out_ref in enumerate(out_refs):
        place = pl.multiple_of(place_ref[turn] * rows, rows)
        out_ref[:, : 2 * F] = up_ref[pl.ds(place, rows), :]
        for part in range(F // rows):
            out_ref[:, 2 * F + part * rows : 2 * F + (part + 1) * rows] = down_ref[
                part * rows : (part + 1) * rows, pl.ds(place, rows)
            ]


def run_expert_grad(places, received, pull, gate_grad, activated, piece_rows):
    whole = pl.BlockSpec(memory_space=pltpu.VMEM)
    part_count = D // piece_rows
    slot_total = received.shape[0]
    return pl.pallas_call(
        functools.partial(expert_grad_kernel, part_count),
        out_shape=[jax.ShapeDtypeStruct((piece_rows, 3 * F), jnp.bfloat16)] * part_count,
        in_specs=[pl.BlockSpec(memory_space=pltpu.SMEM)] + [whole] * 4,
        out_specs=[whole] * part_count,
        scratch_shapes=[
            pltpu.VMEM((D, 2 * F), jnp.bfloat16),
            pltpu.VMEM((F, D), jnp.bfloat16),
        ],
        compiler_params=pltpu.CompilerParams(vmem_limit_bytes=56 * 1024 * 1024),
        cost_estimate=pl.CostEstimate(
            flops=slot_total * D * F * 6, bytes_accessed=12 * 1024 * 1024, transcendentals=0
        ),
    )(places, received, pull, gate_grad, activated)


def outgoing_pull(grad, spread, gates, capacity):
    high, rest = two_terms(grad)
    wide = dot_nn(spread, high) + dot_nn(spread, rest)
    return (slot_gates(spread, gates, capacity) * wide).astype(jnp.bfloat16)


def first_pull_kernel(capacity, picked_ref, rows_ref, spread_ref, gates_ref, grad_ref, out_ref):
    grad_ref[...] = jnp.zeros_like(grad_ref)
    for place in range(rows_ref.shape[0]):
        grad_ref[pl.ds(picked_ref[place], 1), :] = rows_ref[place : place + 1, :]
    out_ref[...] = outgoing_pull(grad_ref[...], spread_ref[...], gates_ref[...], capacity)


def first_pull(capacity, picked, rows, spread, gates):
    whole = pl.BlockSpec(memory_space=pltpu.VMEM)
    return pl.pallas_call(
        functools.partial(first_pull_kernel, capacity),
        out_shape=(
            jax.ShapeDtypeStruct((spread.shape[1], D), jnp.float32),
            jax.ShapeDtypeStruct((spread.shape[0], D), jnp.bfloat16),
        ),
        in_specs=[pl.BlockSpec(memory_space=pltpu.SMEM)] + [whole] * 3,
        out_specs=[whole] * 2,
        compiler_params=pltpu.CompilerParams(vmem_limit_bytes=48 * 1024 * 1024),
        cost_estimate=pl.CostEstimate(
            flops=4 * spread.shape[0] * spread.shape[1] * D,
            bytes_accessed=5 * 1024 * 1024,
            transcendentals=0,
        ),
    )(picked, rows, spread, gates)


def router_kernel(
    capacity, grad_ref, returned_ref, spread_back_ref, probs_ref, ffn_ref, low_ref, router_grad_ref
):
    high, rest = two_terms(grad_ref[...])
    dots = dot_nt(high, returned_ref[...]) + dot_nt(rest, returned_ref[...])
    dots = dots * spread_back_ref[...].astype(jnp.float32)
    slot_total = returned_ref.shape[0]
    slot = lax.broadcasted_iota(jnp.int32, (slot_total, LANES), 0) // capacity
    lane = lax.broadcasted_iota(jnp.int32, (slot_total, LANES), 1)
    owner = jnp.where(slot == lane, 1.0, 0.0).astype(jnp.bfloat16)
    high, rest = two_terms(dots)
    pull = dot_nn(high, owner) + dot_nn(rest, owner)
    probs = probs_ref[...]
    low = (probs * (pull - jnp.sum(probs * pull, axis=-1, keepdims=True))).astype(jnp.bfloat16)
    low_ref[...] = low
    router_grad_ref[...] = dot_tn(ffn_ref[...], low)


def router_back(capacity, grad, returned, spread_back, probs, ffn):
    whole = pl.BlockSpec(memory_space=pltpu.VMEM)
    seq_len = grad.shape[0]
    return pl.pallas_call(
        functools.partial(router_kernel, capacity),
        out_shape=(
            jax.ShapeDtypeStruct((seq_len, LANES), jnp.bfloat16),
            jax.ShapeDtypeStruct((D, LANES), jnp.float32),
        ),
        in_specs=[whole] * 5,
        out_specs=[whole] * 2,
        compiler_params=pltpu.CompilerParams(vmem_limit_bytes=48 * 1024 * 1024),
        cost_estimate=pl.CostEstimate(
            flops=4 * seq_len * returned.shape[0] * D,
            bytes_accessed=6 * 1024 * 1024,
            transcendentals=0,
        ),
    )(grad, returned, spread_back, probs, ffn)


def final_kernel(
    capacity,
    gain_row,
    picked_ref,
    middle_ref,
    gates_ref,
    returned_ref,
    spread_ref,
    spread_back_ref,
    gain_ref,
    rows_ref,
    low_ref,
):
    count = rows_ref.shape[0]
    for place in range(count):
        rows_ref[place : place + 1, :] = middle_ref[pl.ds(picked_ref[place], 1), :]
    sublane = lax.broadcasted_iota(jnp.int32, (count, LANES), 0)
    wanted = jnp.zeros((count, LANES), jnp.int32)
    for place in range(count):
        wanted = jnp.where(sublane == place, picked_ref[place], wanted)
    seq_len = middle_ref.shape[0]
    token = lax.broadcasted_iota(jnp.int32, (count, seq_len), 1)
    wanted = jnp.concatenate([wanted] * (seq_len // LANES), axis=1)
    chosen = jnp.where(token == wanted, 1.0, 0.0).astype(jnp.bfloat16)
    slots = dot_nn(chosen, spread_back_ref[...]).astype(jnp.bfloat16)
    weighted = slot_gates(spread_ref[...], gates_ref[...], capacity) * returned_ref[...].astype(
        jnp.float32
    )
    high, rest = two_terms(weighted)
    rows = rows_ref[...] + (dot_nn(slots, high) + dot_nn(slots, rest))
    rows_ref[...] = rows
    low_ref[...] = (rows * inverse_root(rows) * gain_ref[gain_row : gain_row + 1, :]).astype(
        jnp.bfloat16
    )


def final_rows_of(capacity, gain_row, picked, middle, gates, returned, spread, spread_back, gains):
    whole = pl.BlockSpec(memory_space=pltpu.VMEM)
    count = picked.shape[0]
    return pl.pallas_call(
        functools.partial(final_kernel, capacity, gain_row),
        out_shape=(
            jax.ShapeDtypeStruct((count, D), jnp.float32),
            jax.ShapeDtypeStruct((count, D), jnp.bfloat16),
        ),
        in_specs=[pl.BlockSpec(memory_space=pltpu.SMEM)] + [whole] * 6,
        out_specs=[whole] * 2,
        compiler_params=pltpu.CompilerParams(vmem_limit_bytes=48 * 1024 * 1024),
        cost_estimate=pl.CostEstimate(
            flops=1 << 28, bytes_accessed=5 * 1024 * 1024, transcendentals=0
        ),
    )(picked, middle, gates, returned, spread, spread_back, gains)


def tie(first, second):
    return lax.optimization_barrier((first, second))


def swap_pairs(row_groups, turn_plane, turn_row):
    pairs = []
    for plane in range(PLANES):
        for row in range(row_groups):
            for part in range(PLANES):
                source = (plane * row_groups + row) * PLANES + part
                target_plane = (plane + SHIFTS[part ^ turn_plane]) % PLANES
                target_row = (row + turn_row) % row_groups
                pairs.append((source, (target_plane * row_groups + target_row) * PLANES + plane))
    return pairs


def all_turns(row_groups):
    return [(plane, row) for row in range(row_groups) for plane in range(PLANES)]


def shift_inverse(shift):
    return jnp.array(SHIFTS, jnp.int32)[shift]


def part_of_turn(turn_plane):
    me_plane = lax.axis_index("z")
    me_part = lax.axis_index(("y", "c"))
    return shift_inverse((me_plane - me_part) % PLANES) ^ turn_plane


def piece_place(turn, row_groups):
    turn_plane, turn_row = turn
    row = (lax.axis_index("h") - turn_row) % row_groups
    return row * PLANES + part_of_turn(turn_plane)


def spread_experts(piece, row_groups):
    return [
        lax.ppermute(
            piece, ("z", "h", "y", "c"), swap_pairs(row_groups, turn_plane, turn_row)
        )
        for turn_plane, turn_row in all_turns(row_groups)
    ]


def return_expert_grads(pieces, row_groups):
    arrived = []
    for piece, turn in zip(pieces, all_turns(row_groups)):
        back = [(target, source) for source, target in swap_pairs(row_groups, *turn)]
        arrived.append(lax.ppermute(piece, ("z", "h", "y", "c"), back))
    return arrived


def scatter_sum(parts):
    total = parts[0].astype(jnp.float32)
    for part in parts[1:]:
        total = total + part.astype(jnp.float32)
    return total


def send_all(values):
    return lax.all_to_all(values, AXES, split_axis=0, concat_axis=0, tiled=True)


def send_plane(values):
    return lax.all_to_all(values, ("x", "y", "c"), split_axis=0, concat_axis=0, tiled=True)


def three_terms(values):
    first = lax.reduce_precision(values, 8, 7)
    second = lax.reduce_precision(values - first, 8, 7)
    third = lax.reduce_precision(values - first - second, 8, 7)
    return [first, second, third]

RING = ("z", "x", "y", "c")


def owner_sum_kernel(
    layers,
    *refs,
):
    grads, refs = refs[:layers], refs[layers:]
    (
        out_ref,
        own_ref,
        core_ref,
        near_ref,
        joined_ref,
        turn_ref,
        last_ref,
        got_ref,
        local_sem,
        send_sem,
        recv_sem,
    ) = refs
    at = {name: lax.axis_index(name) for name in RING}
    planes = lax.axis_size("z")
    barrier = pltpu.get_barrier_semaphore()
    partners = [{name: 1 - at[name]} for name in ("c", "x", "y")]
    partners += [{"z": lax.rem(at["z"] + turn, planes)} for turn in range(1, planes)]
    for partner in partners:
        pl.semaphore_signal(
            barrier, inc=1, device_id=partner, device_id_type=pl.DeviceIdType.MESH
        )
    pl.semaphore_wait(barrier, len(partners))

    width = own_ref.shape[-1]
    half = width // 2
    per_layer = grads[0].shape[-1] // width
    chunk_count = layers * per_layer
    copies = {}

    def send(chunk_index, step, source, target, partner):
        place = chunk_index * 8 + step
        copy = pltpu.make_async_remote_copy(
            src_ref=source,
            dst_ref=target,
            send_sem=send_sem.at[place],
            recv_sem=recv_sem.at[place],
            device_id=partner,
            device_id_type=pl.DeviceIdType.MESH,
        )
        copy.start()
        copies[place] = copy

    def arrived(chunk_index, *steps):
        for step in steps:
            copies[chunk_index * 8 + step].wait()

    def source_of(chunk_index, core):
        layer, part = chunk_index // per_layer, chunk_index % per_layer
        return grads[layer].at[:, :, :, core, :, pl.ds(part * width, width)]

    def added(left, right):
        return (left.astype(jnp.float32) + right.astype(jnp.float32)).astype(jnp.bfloat16)

    local = []
    for index in range(chunk_count):
        copy = pltpu.make_async_copy(
            source_of(index, at["c"]), own_ref.at[index], local_sem.at[index]
        )
        copy.start()
        local.append(copy)
        send(index, 0, source_of(index, 1 - at["c"]), core_ref.at[index], partners[0])

    def stage_core(index):
        local[index].wait()
        arrived(index, 0)
        for plane in range(planes):
            own_ref[index, plane] = added(own_ref[index, plane], core_ref[index, plane])
        send(
            index,
            1,
            own_ref.at[index, :, 1 - at["x"], :, :, pl.ds(0, half)],
            near_ref.at[index, 0],
            partners[1],
        )
        send(
            index,
            2,
            own_ref.at[index, :, :, 1 - at["y"], :, pl.ds(half, half)],
            near_ref.at[index, 1],
            partners[2],
        )

    def stage_near(index):
        arrived(index, 1, 2)
        for plane in range(planes):
            for other in range(2):
                joined_ref[index, 0, plane, other] = added(
                    own_ref[index, plane, at["x"], other, :, :half],
                    near_ref[index, 0, plane, other],
                )
                joined_ref[index, 1, plane, other] = added(
                    own_ref[index, plane, other, at["y"], :, half:],
                    near_ref[index, 1, plane, other],
                )
        send(
            index,
            3,
            joined_ref.at[index, 0, :, 1 - at["y"]],
            turn_ref.at[index, 0],
            partners[2],
        )
        send(
            index,
            4,
            joined_ref.at[index, 1, :, 1 - at["x"]],
            turn_ref.at[index, 1],
            partners[1],
        )

    def stage_turn(index):
        arrived(index, 3, 4)
        for plane in range(planes):
            last_ref[index, plane, :, :half] = added(
                joined_ref[index, 0, plane, at["y"]], turn_ref[index, 0, plane]
            )
            last_ref[index, plane, :, half:] = added(
                joined_ref[index, 1, plane, at["x"]], turn_ref[index, 1, plane]
            )
        for turn in range(1, planes):
            send(
                index,
                4 + turn,
                last_ref.at[index, partners[2 + turn]["z"]],
                got_ref.at[index, turn - 1],
                partners[2 + turn],
            )

    def stage_planes(index):
        arrived(index, *[4 + turn for turn in range(1, planes)])
        total = last_ref[index, at["z"]].astype(jnp.float32)
        for turn in range(1, planes):
            total = total + got_ref[index, turn - 1].astype(jnp.float32)
        layer, part = index // per_layer, index % per_layer
        out_ref[layer, :, part * width : (part + 1) * width] = total

    stages = (stage_core, stage_near, stage_turn, stage_planes)
    for step in range(chunk_count + len(stages) - 1):
        for number, stage in enumerate(stages):
            if 0 <= step - number < chunk_count:
                stage(step - number)


def owner_sums(grads, width=2048):
    layers = len(grads)
    sizes = [lax.axis_size(name) for name in RING]
    rows, columns = grads[0].shape
    own_rows = rows // (sizes[0] * sizes[1] * sizes[2] * sizes[3])
    chunks = layers * columns // width
    blocks = [grad.reshape(*sizes, own_rows, columns) for grad in grads]
    half = width // 2
    low = jnp.bfloat16
    return pl.pallas_call(
        functools.partial(owner_sum_kernel, layers),
        out_shape=jax.ShapeDtypeStruct((layers, own_rows, columns), jnp.float32),
        in_specs=[pl.BlockSpec(memory_space=pl.ANY)] * layers,
        out_specs=pl.BlockSpec(memory_space=pltpu.VMEM),
        scratch_shapes=[
            pltpu.VMEM((chunks, sizes[0], 2, 2, own_rows, width), low),
            pltpu.VMEM((chunks, sizes[0], 2, 2, own_rows, width), low),
            pltpu.VMEM((chunks, 2, sizes[0], 2, own_rows, half), low),
            pltpu.VMEM((chunks, 2, sizes[0], 2, own_rows, half), low),
            pltpu.VMEM((chunks, 2, sizes[0], own_rows, half), low),
            pltpu.VMEM((chunks, sizes[0], own_rows, width), low),
            pltpu.VMEM((chunks, sizes[0] - 1, own_rows, width), low),
            pltpu.SemaphoreType.DMA((chunks,)),
            pltpu.SemaphoreType.DMA((chunks * 8,)),
            pltpu.SemaphoreType.DMA((chunks * 8,)),
        ],
        compiler_params=pltpu.CompilerParams(
            vmem_limit_bytes=56 * 1024 * 1024, collective_id=1, has_side_effects=True
        ),
        cost_estimate=pl.CostEstimate(
            flops=1 << 26, bytes_accessed=200 * 1024 * 1024, transcendentals=0
        ),
    )(*blocks)


def adam_step(weight, mean_old, square_old, gradient):
    mean_new = BETA_ONE * mean_old + (1.0 - BETA_ONE) * gradient
    square_new = BETA_TWO * square_old + (1.0 - BETA_TWO) * gradient * gradient
    bias_one = 1.0 - BETA_ONE**ADAM_STEP
    bias_two = 1.0 - BETA_TWO**ADAM_STEP
    update = -LEARN_RATE * (
        mean_new / bias_one / (jnp.sqrt(square_new / bias_two) + ADAM_EPS) + DECAY_RATE * weight
    )
    return (mean_new, square_new, update)


VOCAB_BLOCK = 2048
VOCAB_PART = 512


def embedding_kernel(
    row_ref,
    low_ref,
    high_ref,
    arrived_ref,
    word_ref,
    group_ref,
    weight_ref,
    mean_ref,
    square_ref,
    mean_out_ref,
    square_out_ref,
    update_ref,
    wide_ref,
    sorted_ref,
    turned_ref,
    total_ref,
):
    step = pl.program_id(0)
    device_count = arrived_ref.shape[0]
    token_count = sorted_ref.shape[0]
    columns = weight_ref.shape[0]
    groups = LANES // columns

    @pl.when(step == 0)
    def _():
        for part in range(wide_ref.shape[0] // device_count):
            wide_ref[part * device_count : (part + 1) * device_count, :] = arrived_ref[
                :, part * LANES : (part + 1) * LANES
            ].astype(jnp.float32)

        @pl.loop(0, token_count // 32)
        def _(block):
            start = pl.multiple_of(block * 32, 32)
            for place in range(32):
                sorted_ref[pl.ds(start + place, 1), :] = wide_ref[pl.ds(row_ref[start + place], 1), :]

        row_place = lax.broadcasted_iota(jnp.int32, (LANES, LANES), 0)
        lane = lax.broadcasted_iota(jnp.int32, (LANES, LANES), 1)
        same = jnp.where(row_place == lane, 1.0, 0.0).astype(jnp.bfloat16)

        @pl.loop(0, token_count // LANES)
        def _(block):
            rows = pl.ds(pl.multiple_of(block * LANES, LANES), LANES)
            turned = dot_nt(same, sorted_ref[rows, :].astype(jnp.bfloat16))
            group = group_ref[pl.ds(block, 1), :]
            kept = jnp.where(group == 0, turned[:columns, :], 0.0)
            for place in range(1, groups):
                kept += jnp.where(
                    group == place, turned[place * columns : (place + 1) * columns, :], 0.0
                )
            turned_ref[:, rows] = kept.astype(jnp.bfloat16)

    for part in range(VOCAB_BLOCK // VOCAB_PART):
        total_ref[...] = jnp.zeros_like(total_ref)
        place = step * (VOCAB_BLOCK // VOCAB_PART) + part
        first = place * VOCAB_PART

        @pl.loop(low_ref[place], high_ref[place])
        def _(block):
            rows = pl.ds(pl.multiple_of(block * LANES, LANES), LANES)
            word = lax.broadcasted_iota(jnp.int32, (VOCAB_PART, LANES), 0)
            hit = word == word_ref[pl.ds(block, 1), :] - first
            hit = jnp.where(hit, 1.0, 0.0).astype(jnp.bfloat16)
            total_ref[...] += dot_nt(turned_ref[:, rows], hit)

        gradient = total_ref[...]
        words = slice(part * VOCAB_PART, (part + 1) * VOCAB_PART)
        mean_new, square_new, update = adam_step(
            weight_ref[:, words], mean_ref[:, words], square_ref[:, words], gradient
        )
        mean_out_ref[:, words] = mean_new
        square_out_ref[:, words] = square_new
        update_ref[:, words] = update


def token_order(tokens, seq_len, vocabulary, groups):
    count = tokens.shape[0]
    devices = count // seq_len
    keys = lax.sort(tokens * count + jnp.arange(count, dtype=jnp.int32))
    words, origin = keys // count, keys % count
    device, place = origin // seq_len, origin % seq_len
    row = (place // groups) * devices + device
    words = words.reshape(count // LANES, LANES)
    group = (place % groups).reshape(count // LANES, LANES)
    steps = -(-vocabulary // VOCAB_BLOCK) * (VOCAB_BLOCK // VOCAB_PART)
    edges = jnp.arange(steps + 1, dtype=jnp.int32) * VOCAB_PART
    below = jnp.sum((tokens[None, :] < edges[:, None]).astype(jnp.int32), axis=1)
    low = below[:-1] // LANES
    high = (below[1:] + LANES - 1) // LANES
    high = jnp.where(below[1:] > below[:-1], high, low)
    return row, low, high, words, group


def embedding_update_of(order, arrived, weight, mean, square):
    row, low, high, words, group = order
    count = row.shape[0]
    columns, vocabulary = weight.shape
    block = pl.BlockSpec((columns, VOCAB_BLOCK), lambda step: (0, step))
    whole = pl.BlockSpec(memory_space=pltpu.VMEM)
    scalar = pl.BlockSpec(memory_space=pltpu.SMEM)
    wide = count * columns // LANES
    return pl.pallas_call(
        embedding_kernel,
        grid=(-(-vocabulary // VOCAB_BLOCK),),
        out_shape=[jax.ShapeDtypeStruct(weight.shape, jnp.float32)] * 3,
        in_specs=[scalar] * 3 + [whole] * 3 + [block] * 3,
        out_specs=[block] * 3,
        scratch_shapes=[
            pltpu.VMEM((wide, LANES), jnp.float32),
            pltpu.VMEM((count, LANES), jnp.float32),
            pltpu.VMEM((columns, count), jnp.bfloat16),
            pltpu.VMEM((columns, VOCAB_PART), jnp.float32),
        ],
        compiler_params=pltpu.CompilerParams(vmem_limit_bytes=48 * 1024 * 1024),
        cost_estimate=pl.CostEstimate(
            flops=1 << 32, bytes_accessed=50 * 1024 * 1024, transcendentals=1 << 20
        ),
    )(row, low, high, arrived, words, group, weight, mean, square)


def shards(
    tokens,
    prefix,
    routes,
    picked,
    loss_ids,
    teacher_logits,
    embedding,
    embedding_mean,
    embedding_square,
    attention,
    attention_mean,
    attention_square,
    router,
    router_mean,
    router_square,
    norm_gains,
    gains_mean,
    gains_square,
    expert_up,
    upward_mean,
    upward_square,
    expert_down,
    downward_mean,
    downward_square,
    output_table,
    table_mean,
    table_square,
):
    devices_all = lax.axis_size(AXES)
    me_all = lax.axis_index(AXES)
    row_groups = lax.axis_size("h")
    columns_x = lax.axis_size("x")
    seq_len = routes.shape[0]
    layer_count = attention.shape[0]
    experts_all = router.shape[2]
    capacity = 9 * seq_len * TOPK // (8 * experts_all)
    column_count = embedding.shape[1]
    prefix_len = prefix[0]
    slot_total = experts_all * capacity
    piece_rows = expert_up.shape[2]
    gain_count = norm_gains.shape[0]
    group_experts = [
        (group % PLANES) * columns_x + group // PLANES for group in range(experts_all)
    ]
    group_order = jnp.array(group_experts, jnp.int32)
    group_back = jnp.array(
        [group_experts.index(expert) for expert in range(experts_all)], jnp.int32
    )


    head_low = output_table.astype(jnp.bfloat16)
    vocab_local = head_low.shape[0]
    teacher_log = jax.nn.log_softmax(teacher_logits, axis=1)
    teacher_prob = jnp.exp(teacher_log)
    position_count = loss_ids.shape[0]
    teacher_mass = jnp.sum(teacher_prob, axis=1)
    coefficients = jnp.concatenate(
        [jnp.ones((position_count, 1), jnp.float32), teacher_prob], axis=1
    )
    table_low = embedding.astype(jnp.bfloat16)
    looked_up = jnp.take(table_low, tokens, axis=0).reshape(devices_all, seq_len * column_count)
    attention_low = []
    for layer_index in range(layer_count):
        rows_low = attention[layer_index].astype(jnp.bfloat16)
        if layer_index > 0:
            rows_low, looked_up = tie(rows_low, looked_up)
        attention_low.append(lax.all_gather(rows_low, AXES, axis=0, tiled=True))
    small_count = gain_count + layer_count * experts_all
    small = jnp.concatenate(
        [norm_gains.T, router.transpose(1, 0, 2).reshape(column_count, layer_count * experts_all)],
        axis=1,
    ).astype(jnp.bfloat16)
    small = jnp.broadcast_to(
        small.reshape(1, column_count * small_count), (devices_all, column_count * small_count)
    )
    arrived_rows = send_all(jnp.concatenate([looked_up, small], axis=1))
    expert_parts = []
    for layer_index in range(layer_count):
        down_piece = (
            expert_down[0, layer_index]
            .reshape(F // piece_rows, piece_rows, piece_rows)
            .transpose(1, 0, 2)
            .reshape(piece_rows, F)
        )
        piece = jnp.concatenate([expert_up[0, layer_index], down_piece], axis=1).astype(
            jnp.bfloat16
        )
        if layer_index > 0:
            piece, attention_low[0] = tie(piece, attention_low[0])
        else:
            piece, arrived_rows = tie(piece, arrived_rows)
        expert_parts.append(spread_experts(piece, row_groups))

    hidden = (
        arrived_rows[:, : seq_len * column_count]
        .reshape(devices_all, seq_len, column_count)
        .transpose(1, 0, 2)
        .reshape(seq_len, D)
        .astype(jnp.float32)
    )
    small_all = arrived_rows[:, seq_len * column_count :].reshape(D, small_count)
    gain_rows = jnp.pad(
        small_all[:, :gain_count].T.astype(jnp.float32), ((0, 16 - gain_count), (0, 0))
    )
    router_low = jnp.pad(
        small_all[:, gain_count:]
        .reshape(D, layer_count, experts_all)
        .transpose(1, 0, 2)[:, :, group_order],
        ((0, 0), (0, 0), (0, LANES - experts_all)),
    )

    fits_sum = [lax.axis_size(name) for name in AXES] == [PLANES, 2, 1, 2, 2]

    member = jnp.any(routes[:, :, None] == group_order[None, None, :], axis=1)
    before = jnp.dot(
        jnp.tril(jnp.ones((seq_len, seq_len), jnp.bfloat16), -1),
        member.astype(jnp.bfloat16),
        preferred_element_type=jnp.float32,
    ).astype(jnp.int32)
    spread = (
        (before.T[:, None, :] == jnp.arange(capacity, dtype=jnp.int32)[None, :, None])
        & member.T[:, None, :]
    ).astype(jnp.bfloat16)
    spread_flat = spread.reshape(slot_total, seq_len)
    spread_back = spread_flat.T
    kept = jnp.pad(
        (member & (before < capacity)).astype(jnp.float32), ((0, 0), (0, LANES - experts_all))
    )
    turns = turn_tables(seq_len)
    places = jnp.stack([piece_place(turn, row_groups) for turn in all_turns(row_groups)]).astype(
        jnp.int32
    )

    stored = []
    extra = ()
    for layer_index in range(layer_count):
        saved = forward_layer(
            layer_index,
            capacity,
            experts_all,
            prefix,
            hidden,
            extra,
            attention_low[layer_index],
            gain_rows,
            turns,
            router_low,
            kept,
            spread_flat,
            spread_back,
        )
        hidden = saved[6]
        gates, outgoing = saved[9], saved[10]
        if layer_index > 0:
            expert_parts[layer_index][2:], outgoing = tie(expert_parts[layer_index][2:], outgoing)
        received = send_plane(outgoing.reshape(experts_all, capacity, D)).reshape(slot_total, D)
        if layer_index == 0:
            ids_now, tokens_now, outgoing = lax.optimization_barrier((loss_ids, tokens, outgoing))
            local_ids = ids_now - me_all * vocab_local
            vocab_place = jnp.arange(vocab_local, dtype=jnp.int32)
            marked = jnp.sum(
                jnp.where(
                    local_ids[:, :, None] == vocab_place[None, None, :], coefficients[:, :, None], 0.0
                ),
                axis=1,
            )
            order = token_order(tokens_now, seq_len, embedding.shape[0], LANES // column_count)
            marked, order, received = lax.optimization_barrier((marked, order, received))
        upcoming = expert_parts[layer_index + 1] if layer_index + 1 < layer_count else None
        produced = run_expert(places, received, expert_parts[layer_index])
        returned = send_plane(produced.reshape(experts_all, capacity, D)).reshape(slot_total, D)
        if layer_index == 0:
            marked_pull = jnp.dot(
                marked.astype(jnp.bfloat16), head_low, preferred_element_type=jnp.float32
            )
            own_count = position_count // devices_all
            marked_arrived = send_all(
                marked_pull.astype(jnp.bfloat16).reshape(devices_all, own_count, D)
            )
            marked_arrived, returned = tie(marked_arrived, returned)
        if upcoming is not None:
            upcoming[:2], returned = tie(upcoming[:2], returned)
        stored.append((saved, received, returned))
        extra = (gates, returned)

    final_gain = gain_rows[4 * layer_count]
    final_rows, final_low = final_rows_of(
        capacity,
        4 * layer_count,
        picked,
        hidden,
        *extra,
        spread_flat,
        spread_back,
        gain_rows,
    )
    all_rows = send_all(jnp.broadcast_to(final_low[None], (devices_all, own_count, D))).reshape(
        position_count, D
    )
    logits = jnp.einsum("pd,vd->pv", all_rows, head_low, preferred_element_type=jnp.float32)
    local_peak = jnp.max(logits, axis=1)
    local_exp = jnp.exp(logits - local_peak[:, None])
    local_sum = jnp.sum(local_exp, axis=1)
    local_dot = jnp.sum(marked * logits, axis=1)
    pull = jnp.dot(local_exp.astype(jnp.bfloat16), head_low, preferred_element_type=jnp.float32)
    stats = jnp.stack(
        three_terms(local_peak) + three_terms(local_sum) + three_terms(local_dot), axis=1
    )
    stats = jnp.pad(stats, ((0, 0), (0, 128 - stats.shape[1])))
    pull_sent = jnp.concatenate([pull, stats], axis=1).astype(jnp.bfloat16)
    pull_got = send_all(pull_sent.reshape(devices_all, own_count, D + 128)).astype(jnp.float32)
    stats_got = pull_got[:, :, D:]
    peaks = jnp.sum(stats_got[:, :, 0:3], axis=2)
    sums = jnp.sum(stats_got[:, :, 3:6], axis=2)
    dots = jnp.sum(stats_got[:, :, 6:9], axis=2)
    peak_own = jnp.max(peaks, axis=0)
    log_norm_own = peak_own + jnp.log(jnp.sum(sums * jnp.exp(peaks - peak_own), axis=0))
    mass_own = lax.dynamic_slice_in_dim(teacher_mass, me_all * own_count, own_count)
    entropy_own = lax.dynamic_slice_in_dim(
        jnp.sum(teacher_prob * teacher_log, axis=1), me_all * own_count, own_count
    )
    loss_own = (1.0 + mass_own) * log_norm_own - jnp.sum(dots, axis=0) + entropy_own
    scale_own = (1.0 + mass_own)[None, :] * jnp.exp(peaks - log_norm_own[None, :])
    marked_total = jnp.sum(marked_arrived.astype(jnp.float32), axis=0)
    final_grad = (
        jnp.sum(scale_own[:, :, None] * pull_got[:, :, :D], axis=0) - marked_total
    ) / position_count
    spread_stats = jnp.concatenate([log_norm_own, loss_own]).reshape(1, 2 * own_count)
    stats_all = send_all(jnp.broadcast_to(spread_stats, (devices_all, 2 * own_count)))
    log_norm = stats_all[:, :own_count].reshape(position_count)
    loss_value = jnp.sum(stats_all[:, own_count:]) / position_count
    grad_logits = (
        jnp.exp(logits - log_norm[:, None]) * (1.0 + teacher_mass)[:, None] - marked
    ) / position_count
    table_grad = jnp.einsum(
        "pv,pd->vd",
        grad_logits.astype(jnp.bfloat16),
        all_rows,
        preferred_element_type=jnp.float32,
    )
    rows_grad, final_gain_grad = norm_back(final_rows, final_gain, final_grad)
    grad_hidden, sent_back = first_pull(capacity, picked, rows_grad, spread_flat, extra[0])
    gain_parts = [None] * (4 * layer_count) + [final_gain_grad]
    attention_parts = [None] * layer_count
    router_parts = [None] * layer_count
    piece_parts = [None] * layer_count
    for layer_index in reversed(range(layer_count)):
        saved, received, returned = stored[layer_index]
        hidden_in, projected, queries, keys, values, attended, middle, ffn_low, probs = saved[:9]
        upper = layer_index + 1 if layer_index + 1 < layer_count else None
        output_grad = send_plane(sent_back.reshape(experts_all, capacity, D)).reshape(
            slot_total, D
        )
        logit_low, router_parts[layer_index] = router_back(
            capacity, grad_hidden, returned, spread_back, probs, ffn_low
        )
        input_grad, gate_grad, activated = run_expert_back(
            places, received, output_grad, expert_parts[layer_index]
        )
        back_inputs = send_plane(input_grad.reshape(experts_all, capacity, D)).reshape(
            slot_total, D
        )
        grad_pieces = run_expert_grad(
            places, received, output_grad, gate_grad, activated, piece_rows
        )
        if layer_index > 0:
            piece_parts[layer_index] = return_expert_grads(grad_pieces, row_groups)
        if upper is not None:
            piece_parts[upper][2:], back_inputs = tie(piece_parts[upper][2:], back_inputs)
        lower = (spread_flat, stored[layer_index - 1][0][9]) if layer_index > 0 else ()
        results = backward_layer(
            layer_index,
            capacity,
            prefix,
            grad_hidden,
            back_inputs,
            logit_low,
            hidden_in,
            projected,
            queries,
            keys,
            values,
            attended,
            middle,
            attention_low[layer_index],
            gain_rows,
            turns,
            router_low,
            spread_back,
            lower,
        )
        grad_hidden, weight_grad, gain_grads = results[:3]
        gain_parts[4 * layer_index : 4 * layer_index + 4] = list(gain_grads[:4])
        if layer_index > 0:
            sent_back = results[3]
            piece_parts[layer_index][:2], sent_back = tie(piece_parts[layer_index][:2], sent_back)
        attention_parts[layer_index] = weight_grad
        if not fits_sum:
            attention_parts[layer_index] = lax.psum_scatter(
                weight_grad, AXES, scatter_dimension=0, tiled=True
            ).astype(jnp.float32)

    sending = (
        grad_hidden.astype(jnp.bfloat16)
        .reshape(seq_len, devices_all, column_count)
        .transpose(1, 0, 2)
        .reshape(devices_all, seq_len * column_count)
    )
    small_grads = jnp.concatenate(
        [jnp.stack(gain_parts, axis=1)] + [part[:, group_back] for part in router_parts], axis=1
    ).astype(jnp.bfloat16)
    arrived_grads = send_all(
        jnp.concatenate(
            [sending, small_grads.reshape(devices_all, column_count * small_count)], axis=1
        )
    )
    if fits_sum:
        attention_parts = list(owner_sums(attention_parts[::-1], 2048))[::-1]
    grad_pieces, arrived_grads, attention_parts = lax.optimization_barrier(
        (grad_pieces, arrived_grads, attention_parts)
    )
    piece_parts[0] = return_expert_grads(grad_pieces, row_groups)
    embedding_next = embedding_update_of(
        order,
        arrived_grads[:, : seq_len * column_count],
        embedding.T,
        embedding_mean.T,
        embedding_square.T,
    )
    piece_parts[0], embedding_next = tie(piece_parts[0], embedding_next)
    up_parts, down_parts = [], []
    for parts in piece_parts:
        piece_grad = scatter_sum(parts)
        up_parts.append(piece_grad[:, : 2 * F])
        down_parts.append(
            piece_grad[:, 2 * F :]
            .reshape(piece_rows, F // piece_rows, piece_rows)
            .transpose(1, 0, 2)
            .reshape(F, piece_rows)
        )
    small_total = jnp.sum(
        arrived_grads[:, seq_len * column_count :].astype(jnp.float32), axis=0
    ).reshape(column_count, small_count)
    gains_grad = small_total[:, :gain_count].T
    router_grad = (
        small_total[:, gain_count:]
        .reshape(column_count, layer_count, experts_all)
        .transpose(1, 0, 2)
    )
    attention_grad = jnp.stack(attention_parts)
    upward_grad = jnp.stack(up_parts)[None]
    downward_grad = jnp.stack(down_parts)[None]
    embedding_mean_next, embedding_square_next, embedding_update = [
        part.T for part in embedding_next
    ]
    attention_mean_next, attention_square_next, attention_update = adam_step(
        attention, attention_mean, attention_square, attention_grad
    )
    router_mean_next, router_square_next, router_update = adam_step(
        router, router_mean, router_square, router_grad
    )
    gains_mean_next, gains_square_next, gains_update = adam_step(
        norm_gains, gains_mean, gains_square, gains_grad
    )
    upward_mean_next, upward_square_next, upward_update = adam_step(
        expert_up, upward_mean, upward_square, upward_grad
    )
    downward_mean_next, downward_square_next, downward_update = adam_step(
        expert_down, downward_mean, downward_square, downward_grad
    )
    table_mean_next, table_square_next, table_update = adam_step(
        output_table, table_mean, table_square, table_grad
    )
    return (
        loss_value,
        embedding_mean_next,
        embedding_square_next,
        embedding_update,
        attention_mean_next,
        attention_square_next,
        attention_update,
        router_mean_next,
        router_square_next,
        router_update,
        gains_mean_next,
        gains_square_next,
        gains_update,
        upward_mean_next,
        upward_square_next,
        upward_update,
        downward_mean_next,
        downward_square_next,
        downward_update,
        table_mean_next,
        table_square_next,
        table_update,
    )


def solution(mesh):
    expert_count, shard_count = mesh.devices.shape
    mesh = Mesh(
        mesh.devices.reshape(PLANES, expert_count // PLANES, shard_count // 4, 2, 2), AXES
    )
    return jax.shard_map(
        shards,
        mesh=mesh,
        in_specs=(
            P(),
            P(AXES),
            P(AXES, None),
            P(AXES),
            P(),
            P(),
            P(None, AXES),
            P(None, AXES),
            P(None, AXES),
            P(None, AXES, None),
            P(None, AXES, None),
            P(None, AXES, None),
            P(None, AXES, None),
            P(None, AXES, None),
            P(None, AXES, None),
            P(None, AXES),
            P(None, AXES),
            P(None, AXES),
            P(("z", "x"), None, ("h", "y", "c"), None),
            P(("z", "x"), None, ("h", "y", "c"), None),
            P(("z", "x"), None, ("h", "y", "c"), None),
            P(("z", "x"), None, None, ("h", "y", "c")),
            P(("z", "x"), None, None, ("h", "y", "c")),
            P(("z", "x"), None, None, ("h", "y", "c")),
            P(AXES, None),
            P(AXES, None),
            P(AXES, None),
        ),
        out_specs=(
            P(),
            P(None, AXES),
            P(None, AXES),
            P(None, AXES),
            P(None, AXES, None),
            P(None, AXES, None),
            P(None, AXES, None),
            P(None, AXES, None),
            P(None, AXES, None),
            P(None, AXES, None),
            P(None, AXES),
            P(None, AXES),
            P(None, AXES),
            P(("z", "x"), None, ("h", "y", "c"), None),
            P(("z", "x"), None, ("h", "y", "c"), None),
            P(("z", "x"), None, ("h", "y", "c"), None),
            P(("z", "x"), None, None, ("h", "y", "c")),
            P(("z", "x"), None, None, ("h", "y", "c")),
            P(("z", "x"), None, None, ("h", "y", "c")),
            P(AXES, None),
            P(AXES, None),
            P(AXES, None),
        ),
        check_vma=False,
    )
```

```python
import functools

import jax
import jax.numpy as jnp
from jax import lax
from jax.experimental import pallas as pl
from jax.experimental.pallas import tpu as pltpu
from jax.sharding import Mesh, PartitionSpec as P

D = 1024
HEADS = 16
HDIM = 64
F = 512
TOPK = 4
ADAM_STEP = 10


EPS_NORM = 1e-05
BETA_ONE = 0.9
BETA_TWO = 0.95
ADAM_EPS = 1e-08
LEARN_RATE = 0.01
DECAY_RATE = 0.1
ROPE_BASE = 10000.0
MASK_FILL = -1e30


def rms_norm(inputs, gain_row):
    return (
        inputs * lax.rsqrt(jnp.mean(inputs * inputs, axis=-1, keepdims=True) + EPS_NORM) * gain_row
    )


def norm_back(inputs, gain_row, upstream):
    _, pullback = jax.vjp(rms_norm, inputs, gain_row)
    return pullback(upstream)


AXES = ("z", "x", "h", "y", "c")
PLANES = 4
SHIFTS = (0, 2, 1, 3)
LANES = 128
CHUNKS = D // LANES


def dot_nn(left, right):
    return lax.dot_general(
        left, right, (((1,), (0,)), ((), ())), preferred_element_type=jnp.float32
    )


def dot_nt(left, right):
    return lax.dot_general(
        left, right, (((1,), (1,)), ((), ())), preferred_element_type=jnp.float32
    )


def dot_tn(left, right):
    return lax.dot_general(
        left, right, (((0,), (0,)), ((), ())), preferred_element_type=jnp.float32
    )


def inverse_root(values):
    return lax.rsqrt(jnp.mean(values * values, axis=-1, keepdims=True) + EPS_NORM)


def two_terms(values):
    high = values.astype(jnp.bfloat16)
    return high, (values - high.astype(jnp.float32)).astype(jnp.bfloat16)


def chunk(values, place):
    return values[:, place * LANES : (place + 1) * LANES]


def half_turn(values):
    lane = lax.broadcasted_iota(jnp.int32, values.shape, 1)
    ahead = pltpu.roll(values, LANES - HDIM // 2, 1)
    behind = pltpu.roll(values, HDIM // 2, 1)
    return jnp.where(lane % HDIM < HDIM // 2, ahead, behind)


def slot_gates(spread, gates, capacity):
    high, rest = two_terms(gates)
    full = dot_nn(spread, high) + dot_nn(spread, rest)
    expert = lax.broadcasted_iota(jnp.int32, full.shape, 0) // capacity
    lane = lax.broadcasted_iota(jnp.int32, full.shape, 1)
    return jnp.sum(jnp.where(lane == expert, full, 0.0), axis=1, keepdims=True)


def combine(middle, spread, spread_back, gates, returned, capacity):
    weighted = slot_gates(spread, gates, capacity) * returned.astype(jnp.float32)
    high, rest = two_terms(weighted)
    return middle + (dot_nn(spread_back, high) + dot_nn(spread_back, rest))


def masked_probs(query, key, visible):
    scores = dot_nt(query, key) * HDIM ** (-0.5)
    scores = jnp.where(visible, scores, MASK_FILL)
    weights = jnp.exp(scores - jnp.max(scores, axis=-1, keepdims=True))
    return weights / jnp.sum(weights, axis=-1, keepdims=True)


def visible_keys(prefix_ref, seq_len):
    query_place = lax.broadcasted_iota(jnp.int32, (seq_len, seq_len), 0)
    key_place = lax.broadcasted_iota(jnp.int32, (seq_len, seq_len), 1)
    return (key_place <= query_place) | (key_place < prefix_ref[0])


def head_masks(seq_len):
    lane = lax.broadcasted_iota(jnp.int32, (seq_len, LANES), 1)
    return lane < HDIM, lane >= HDIM


def fetch_weights(weight_ref, held_ref, copy_sem, order):
    copies = {}
    for part in order:
        copies[part] = pltpu.make_async_copy(
            weight_ref.at[:, pl.ds(part * D, D)], held_ref.at[part], copy_sem.at[part]
        )
        copies[part].start()
    return copies


def forward_kernel(
    layer_index,
    capacity,
    expert_count,
    prefix_ref,
    hidden_ref,
    *refs,
):
    if layer_index > 0:
        gates_in_ref, returned_ref, refs = refs[0], refs[1], refs[2:]
    (
        weight_ref,
        gain_ref,
        turn_ref,
        router_ref,
        kept_ref,
        spread_ref,
        spread_back_ref,
        hidden_out_ref,
        projected_ref,
        query_ref,
        key_ref,
        value_ref,
        attended_ref,
        middle_ref,
        ffn_ref,
        probs_ref,
        gates_ref,
        outgoing_ref,
        held_ref,
        copy_sem,
    ) = refs
    copies = fetch_weights(weight_ref, held_ref, copy_sem, (0, 1, 2, 3))
    seq_len = hidden_ref.shape[0]
    hidden = hidden_ref[...]
    if layer_index > 0:
        hidden = combine(
            hidden,
            spread_ref[...],
            spread_back_ref[...],
            gates_in_ref[...],
            returned_ref[...],
            capacity,
        )
    hidden_out_ref[...] = hidden
    row = 4 * layer_index
    normed = (hidden * inverse_root(hidden) * gain_ref[row : row + 1, :]).astype(jnp.bfloat16)
    cosines, sines = turn_ref[0], turn_ref[1]
    for part, out_ref in ((0, query_ref), (1, key_ref)):
        columns = slice(part * D, (part + 1) * D)
        copies[part].wait()
        projected = dot_nn(normed, held_ref[part])
        projected_ref[:, columns] = projected
        scaled = projected * inverse_root(projected) * gain_ref[row + 1 + part : row + 2 + part, :]
        for place in range(CHUNKS):
            block = chunk(scaled, place)
            out_ref[:, place * LANES : (place + 1) * LANES] = (
                block * cosines + half_turn(block) * sines
            ).astype(jnp.bfloat16)
    copies[2].wait()
    value_ref[...] = dot_nn(normed, held_ref[2]).astype(jnp.bfloat16)
    visible = visible_keys(prefix_ref, seq_len)
    masks = head_masks(seq_len)
    zero = jnp.zeros((), jnp.bfloat16)
    for place in range(CHUNKS):
        columns = slice(place * LANES, (place + 1) * LANES)
        query, key, value = query_ref[:, columns], key_ref[:, columns], value_ref[:, columns]
        total = None
        for mask in masks:
            probs = masked_probs(query, jnp.where(mask, key, zero), visible).astype(jnp.bfloat16)
            term = dot_nn(probs, jnp.where(mask, value, zero))
            total = term if total is None else total + term
        attended_ref[:, columns] = total.astype(jnp.bfloat16)
    copies[3].wait()
    middle = hidden + dot_nn(attended_ref[...], held_ref[3])
    middle_ref[...] = middle
    ffn = (middle * inverse_root(middle) * gain_ref[row + 3 : row + 4, :]).astype(jnp.bfloat16)
    ffn_ref[...] = ffn
    outgoing_ref[...] = dot_nn(spread_ref[...], ffn).astype(jnp.bfloat16)
    logits = dot_nn(ffn, router_ref[layer_index])
    lane = lax.broadcasted_iota(jnp.int32, logits.shape, 1)
    logits = jnp.where(lane < expert_count, logits, MASK_FILL)
    weights = jnp.exp(logits - jnp.max(logits, axis=-1, keepdims=True))
    probs = weights / jnp.sum(weights, axis=-1, keepdims=True)
    probs_ref[...] = probs
    gates_ref[...] = probs * kept_ref[...]


def forward_layer(
    layer_index,
    capacity,
    expert_count,
    prefix,
    hidden,
    extra,
    weights,
    gains,
    turns,
    router,
    kept,
    spread,
    spread_back,
):
    seq_len = hidden.shape[0]
    whole = pl.BlockSpec(memory_space=pltpu.VMEM)
    wide = jax.ShapeDtypeStruct((seq_len, D), jnp.float32)
    low = jax.ShapeDtypeStruct((seq_len, D), jnp.bfloat16)
    small = jax.ShapeDtypeStruct((seq_len, LANES), jnp.float32)
    return pl.pallas_call(
        functools.partial(forward_kernel, layer_index, capacity, expert_count),
        out_shape=(
            wide,
            jax.ShapeDtypeStruct((seq_len, 2 * D), jnp.float32),
            low,
            low,
            low,
            low,
            wide,
            low,
            small,
            small,
            jax.ShapeDtypeStruct((spread.shape[0], D), jnp.bfloat16),
        ),
        in_specs=[pl.BlockSpec(memory_space=pltpu.SMEM), whole]
        + [whole] * len(extra)
        + [pl.BlockSpec(memory_space=pl.ANY)]
        + [whole] * 6,
        out_specs=[whole] * 11,
        scratch_shapes=[
            pltpu.VMEM((4, D, D), jnp.bfloat16),
            pltpu.SemaphoreType.DMA((4,)),
        ],
        compiler_params=pltpu.CompilerParams(vmem_limit_bytes=60 * 1024 * 1024),
        cost_estimate=pl.CostEstimate(
            flops=4 * seq_len * D * D * 3, bytes_accessed=24 * 1024 * 1024, transcendentals=1 << 20
        ),
    )(prefix, hidden, *extra, weights, gains, turns, router, kept, spread, spread_back)


def norm_pull(values, gain, upstream):
    root = inverse_root(values)
    scaled = values * root
    weighted = upstream * gain
    mean = jnp.mean(weighted * scaled, axis=-1, keepdims=True)
    return root * (weighted - scaled * mean), jnp.sum(upstream * scaled, axis=0, keepdims=True)


def backward_kernel(
    layer_index,
    capacity,
    prefix_ref,
    grad_ref,
    back_ref,
    logit_ref,
    hidden_ref,
    projected_ref,
    query_ref,
    key_ref,
    value_ref,
    attended_ref,
    middle_ref,
    weight_ref,
    gain_ref,
    turn_ref,
    router_ref,
    spread_back_ref,
    *refs,
):
    if layer_index > 0:
        spread_ref, gates_ref, refs = refs[0], refs[1], refs[2:]
        outgoing_ref, refs = refs[3], refs[:3] + refs[4:]
    grad_out_ref, weight_grad_ref, gain_grad_ref, pull_ref, key_pull_ref, held_ref, copy_sem = refs
    copies = fetch_weights(weight_ref, held_ref, copy_sem, (3, 2, 0, 1))
    seq_len = hidden_ref.shape[0]
    row = 4 * layer_index
    ffn_grad = dot_nn(spread_back_ref[...], back_ref[...]) + dot_nt(
        logit_ref[...], router_ref[layer_index]
    )
    middle_grad, gain_three = norm_pull(
        middle_ref[...], gain_ref[row + 3 : row + 4, :], ffn_grad
    )
    grad_middle = grad_ref[...] + middle_grad
    grad_out_ref[...] = grad_middle
    branch = grad_middle.astype(jnp.bfloat16)
    weight_grad_ref[:, 3 * D :] = dot_tn(attended_ref[...], branch).astype(jnp.bfloat16)
    copies[3].wait()
    pull_ref[...] = dot_nt(branch, held_ref[3]).astype(jnp.bfloat16)
    visible = visible_keys(prefix_ref, seq_len)
    masks = head_masks(seq_len)
    zero = jnp.zeros((), jnp.bfloat16)
    cosines, sines = turn_ref[0], turn_ref[1]
    factor = HDIM ** (-0.5)
    hidden = hidden_ref[...]
    normed = (hidden * inverse_root(hidden) * gain_ref[row : row + 1, :]).astype(jnp.bfloat16)
    for place in range(CHUNKS):
        columns = slice(place * LANES, (place + 1) * LANES)
        query, key, value = query_ref[:, columns], key_ref[:, columns], value_ref[:, columns]
        pull = pull_ref[:, columns]
        totals = [None, None, None]
        for mask in masks:
            key_half = jnp.where(mask, key, zero)
            probs = masked_probs(query, key_half, visible)
            pulled = dot_nt(pull, jnp.where(mask, value, zero))
            inner = jnp.sum(probs * pulled, axis=-1, keepdims=True)
            score_grad = (probs * (pulled - inner)).astype(jnp.bfloat16)
            terms = (
                dot_nn(score_grad, key_half),
                dot_tn(score_grad, jnp.where(mask, query, zero)),
                dot_tn(probs.astype(jnp.bfloat16), jnp.where(mask, pull, zero)),
            )
            totals = [b if a is None else a + b for a, b in zip(totals, terms)]
        for part, target_ref in ((0, key_pull_ref.at[0]), (1, key_pull_ref.at[1])):
            turned = (totals[part] * factor).astype(jnp.bfloat16).astype(jnp.float32)
            target_ref[:, columns] = turned * cosines - half_turn(turned) * sines
        pull_ref[:, columns] = totals[2].astype(jnp.bfloat16)
    gain_rows = []
    value_pull = pull_ref[...]
    copies[2].wait()
    back = dot_nt(value_pull, held_ref[2])
    weight_grad_ref[:, 2 * D : 3 * D] = dot_tn(normed, value_pull).astype(jnp.bfloat16)
    for part in range(2):
        columns = slice(part * D, (part + 1) * D)
        input_pull, gain_row = norm_pull(
            projected_ref[:, columns],
            gain_ref[row + 1 + part : row + 2 + part, :],
            key_pull_ref[part],
        )
        gain_rows.append(gain_row)
        low_pull = input_pull.astype(jnp.bfloat16)
        weight_grad_ref[:, columns] = dot_tn(normed, low_pull).astype(jnp.bfloat16)
        copies[part].wait()
        back = back + dot_nt(low_pull, held_ref[part])
    hidden_grad, gain_zero = norm_pull(hidden, gain_ref[row : row + 1, :], back)
    grad_out = grad_out_ref[...] + hidden_grad
    grad_out_ref[...] = grad_out
    if layer_index > 0:
        outgoing_ref[...] = outgoing_pull(grad_out, spread_ref[...], gates_ref[...], capacity)
    gain_grad_ref[...] = jnp.concatenate(
        [gain_zero] + gain_rows + [gain_three, jnp.zeros((4, D), jnp.float32)], axis=0
    )


def backward_layer(
    layer_index,
    capacity,
    prefix,
    grad,
    back_inputs,
    logit_low,
    hidden,
    projected,
    queries,
    keys,
    values,
    attended,
    middle,
    weights,
    gains,
    turns,
    router,
    spread_back,
    extra,
):
    seq_len = hidden.shape[0]
    whole = pl.BlockSpec(memory_space=pltpu.VMEM)
    out_shape = [
        jax.ShapeDtypeStruct((seq_len, D), jnp.float32),
        jax.ShapeDtypeStruct((D, 4 * D), jnp.bfloat16),
        jax.ShapeDtypeStruct((8, D), jnp.float32),
    ]
    if layer_index > 0:
        out_shape.append(jax.ShapeDtypeStruct((spread_back.shape[1], D), jnp.bfloat16))
    return pl.pallas_call(
        functools.partial(backward_kernel, layer_index, capacity),
        out_shape=out_shape,
        in_specs=[pl.BlockSpec(memory_space=pltpu.SMEM)]
        + [whole] * 10
        + [pl.BlockSpec(memory_space=pl.ANY)]
        + [whole] * (4 + len(extra)),
        out_specs=[whole] * len(out_shape),
        scratch_shapes=[
            pltpu.VMEM((seq_len, D), jnp.bfloat16),
            pltpu.VMEM((2, seq_len, D), jnp.float32),
            pltpu.VMEM((4, D, D), jnp.bfloat16),
            pltpu.SemaphoreType.DMA((4,)),
        ],
        compiler_params=pltpu.CompilerParams(vmem_limit_bytes=60 * 1024 * 1024),
        cost_estimate=pl.CostEstimate(
            flops=8 * seq_len * D * D * 3, bytes_accessed=32 * 1024 * 1024, transcendentals=1 << 20
        ),
    )(
        prefix,
        grad,
        back_inputs,
        logit_low,
        hidden,
        projected,
        queries,
        keys,
        values,
        attended,
        middle,
        weights,
        gains,
        turns,
        router,
        spread_back,
        *extra,
    )


def turn_tables(seq_len):
    position = jnp.arange(seq_len, dtype=jnp.float32)[:, None]
    frequency = ROPE_BASE ** (-jnp.arange(HDIM // 2, dtype=jnp.float32) * 2.0 / HDIM)
    angles = position * frequency[None, :]
    cosines, sines = jnp.cos(angles), jnp.sin(angles)
    return jnp.stack(
        [
            jnp.concatenate([cosines] * 4, axis=1),
            jnp.concatenate([-sines, sines, -sines, sines], axis=1),
        ]
    )


def silu_parts(gate_up):
    gate_part, up_part = gate_up[:, :F], gate_up[:, F:]
    sigmoid = 1.0 / (1.0 + jnp.exp(-gate_part))
    return gate_part, up_part, sigmoid


def fetch_expert(places, part_refs, up_ref, down_ref, copy_sem):
    copies = []
    rows = part_refs[0].shape[0]
    for turn, part_ref in enumerate(part_refs):
        place = pl.multiple_of(places[turn] * rows, rows)
        copies.append(
            pltpu.make_async_copy(
                part_ref.at[:, pl.ds(0, 2 * F)],
                up_ref.at[pl.ds(place, rows), :],
                copy_sem.at[len(copies)],
            )
        )
        for block in range(F // rows):
            copies.append(
                pltpu.make_async_copy(
                    part_ref.at[:, pl.ds(2 * F + block * rows, rows)],
                    down_ref.at[pl.ds(block * rows, rows), pl.ds(place, rows)],
                    copy_sem.at[len(copies)],
                )
            )
    for copy in copies:
        copy.start()
    for copy in copies:
        copy.wait()


def expert_kernel(part_count, row_block, place_ref, received_ref, *refs):
    part_refs, (produced_ref, up_ref, down_ref, copy_sem) = refs[:part_count], refs[part_count:]
    fetch_expert(place_ref, part_refs, up_ref, down_ref, copy_sem)

    @pl.loop(0, received_ref.shape[0] // row_block)
    def _(step):
        rows = pl.ds(pl.multiple_of(step * row_block, row_block), row_block)
        gate_part, up_part, sigmoid = silu_parts(dot_nn(received_ref[rows, :], up_ref[...]))
        activated = (gate_part * sigmoid * up_part).astype(jnp.bfloat16)
        produced_ref[rows, :] = dot_nn(activated, down_ref[...]).astype(jnp.bfloat16)


def expert_specs(parts):
    rows = parts[0].shape[0]
    whole = pl.BlockSpec(memory_space=pltpu.VMEM)
    specs = [pl.BlockSpec(memory_space=pltpu.SMEM)]
    apart = [pl.BlockSpec(memory_space=pl.ANY)] * len(parts)
    scratch = [
        pltpu.VMEM((D, 2 * F), jnp.bfloat16),
        pltpu.VMEM((F, D), jnp.bfloat16),
        pltpu.SemaphoreType.DMA((len(parts) * (1 + F // rows),)),
    ]
    return whole, specs, apart, scratch


def run_expert(places, received, parts):
    whole, specs, apart, scratch = expert_specs(parts)
    slot_total = received.shape[0]
    return pl.pallas_call(
        functools.partial(expert_kernel, len(parts), slot_total // 4),
        out_shape=jax.ShapeDtypeStruct((slot_total, D), jnp.bfloat16),
        in_specs=specs + [whole] + apart,
        out_specs=whole,
        scratch_shapes=scratch,
        compiler_params=pltpu.CompilerParams(vmem_limit_bytes=56 * 1024 * 1024),
        cost_estimate=pl.CostEstimate(
            flops=slot_total * D * F * 6, bytes_accessed=8 * 1024 * 1024, transcendentals=1 << 19
        ),
    )(places, received, *parts)


def expert_back_kernel(part_count, row_block, place_ref, received_ref, pull_ref, *refs):
    part_refs, refs = refs[:part_count], refs[part_count:]
    input_grad_ref, gate_grad_ref, activated_ref, up_ref, down_ref, copy_sem = refs
    fetch_expert(place_ref, part_refs, up_ref, down_ref, copy_sem)

    @pl.loop(0, received_ref.shape[0] // row_block)
    def _(step):
        rows = pl.ds(pl.multiple_of(step * row_block, row_block), row_block)
        gate_part, up_part, sigmoid = silu_parts(dot_nn(received_ref[rows, :], up_ref[...]))
        side = gate_part * sigmoid
        activated_ref[rows, :] = (side * up_part).astype(jnp.bfloat16)
        pulled = dot_nt(pull_ref[rows, :], down_ref[...]).astype(jnp.bfloat16)
        pulled = pulled.astype(jnp.float32)
        gate_side = pulled * up_part * sigmoid * (1.0 + gate_part * (1.0 - sigmoid))
        gate_grad_ref[rows, :F] = gate_side.astype(jnp.bfloat16)
        gate_grad_ref[rows, F:] = (pulled * side).astype(jnp.bfloat16)
        input_grad_ref[rows, :] = dot_nt(gate_grad_ref[rows, :], up_ref[...]).astype(jnp.bfloat16)


def run_expert_back(places, received, pull, parts):
    whole, specs, apart, scratch = expert_specs(parts)
    slot_total = received.shape[0]
    return pl.pallas_call(
        functools.partial(expert_back_kernel, len(parts), slot_total // 4),
        out_shape=(
            jax.ShapeDtypeStruct((slot_total, D), jnp.bfloat16),
            jax.ShapeDtypeStruct((slot_total, 2 * F), jnp.bfloat16),
            jax.ShapeDtypeStruct((slot_total, F), jnp.bfloat16),
        ),
        in_specs=specs + [whole] * 2 + apart,
        out_specs=[whole] * 3,
        scratch_shapes=scratch,
        compiler_params=pltpu.CompilerParams(vmem_limit_bytes=56 * 1024 * 1024),
        cost_estimate=pl.CostEstimate(
            flops=slot_total * D * F * 12, bytes_accessed=12 * 1024 * 1024, transcendentals=1 << 19
        ),
    )(places, received, pull, *parts)


def expert_grad_kernel(
    part_count, place_ref, received_ref, pull_ref, gate_grad_ref, activated_ref, *refs
):
    out_refs, (up_ref, down_ref) = refs[:part_count], refs[part_count:]
    block = 256

    @pl.loop(0, D // block)
    def _(step):
        columns = pl.ds(pl.multiple_of(step * block, block), block)
        up_ref[columns, :] = dot_tn(received_ref[:, columns], gate_grad_ref[...]).astype(
            jnp.bfloat16
        )

    @pl.loop(0, F // block)
    def _(step):
        columns = pl.ds(pl.multiple_of(step * block, block), block)
        down_ref[columns, :] = dot_tn(activated_ref[:, columns], pull_ref[...]).astype(
            jnp.bfloat16
        )

    rows = out_refs[0].shape[0]
    for turn, out_ref in enumerate(out_refs):
        place = pl.multiple_of(place_ref[turn] * rows, rows)
        out_ref[:, : 2 * F] = up_ref[pl.ds(place, rows), :]
        for part in range(F // rows):
            out_ref[:, 2 * F + part * rows : 2 * F + (part + 1) * rows] = down_ref[
                part * rows : (part + 1) * rows, pl.ds(place, rows)
            ]


def run_expert_grad(places, received, pull, gate_grad, activated, piece_rows):
    whole = pl.BlockSpec(memory_space=pltpu.VMEM)
    part_count = D // piece_rows
    slot_total = received.shape[0]
    return pl.pallas_call(
        functools.partial(expert_grad_kernel, part_count),
        out_shape=[jax.ShapeDtypeStruct((piece_rows, 3 * F), jnp.bfloat16)] * part_count,
        in_specs=[pl.BlockSpec(memory_space=pltpu.SMEM)] + [whole] * 4,
        out_specs=[whole] * part_count,
        scratch_shapes=[
            pltpu.VMEM((D, 2 * F), jnp.bfloat16),
            pltpu.VMEM((F, D), jnp.bfloat16),
        ],
        compiler_params=pltpu.CompilerParams(vmem_limit_bytes=56 * 1024 * 1024),
        cost_estimate=pl.CostEstimate(
            flops=slot_total * D * F * 6, bytes_accessed=12 * 1024 * 1024, transcendentals=0
        ),
    )(places, received, pull, gate_grad, activated)


def outgoing_pull(grad, spread, gates, capacity):
    high, rest = two_terms(grad)
    wide = dot_nn(spread, high) + dot_nn(spread, rest)
    return (slot_gates(spread, gates, capacity) * wide).astype(jnp.bfloat16)


def first_pull_kernel(capacity, picked_ref, rows_ref, spread_ref, gates_ref, grad_ref, out_ref):
    grad_ref[...] = jnp.zeros_like(grad_ref)
    for place in range(rows_ref.shape[0]):
        grad_ref[pl.ds(picked_ref[place], 1), :] = rows_ref[place : place + 1, :]
    out_ref[...] = outgoing_pull(grad_ref[...], spread_ref[...], gates_ref[...], capacity)


def first_pull(capacity, picked, rows, spread, gates):
    whole = pl.BlockSpec(memory_space=pltpu.VMEM)
    return pl.pallas_call(
        functools.partial(first_pull_kernel, capacity),
        out_shape=(
            jax.ShapeDtypeStruct((spread.shape[1], D), jnp.float32),
            jax.ShapeDtypeStruct((spread.shape[0], D), jnp.bfloat16),
        ),
        in_specs=[pl.BlockSpec(memory_space=pltpu.SMEM)] + [whole] * 3,
        out_specs=[whole] * 2,
        compiler_params=pltpu.CompilerParams(vmem_limit_bytes=48 * 1024 * 1024),
        cost_estimate=pl.CostEstimate(
            flops=4 * spread.shape[0] * spread.shape[1] * D,
            bytes_accessed=5 * 1024 * 1024,
            transcendentals=0,
        ),
    )(picked, rows, spread, gates)


def router_kernel(
    capacity, grad_ref, returned_ref, spread_back_ref, probs_ref, ffn_ref, low_ref, router_grad_ref
):
    high, rest = two_terms(grad_ref[...])
    dots = dot_nt(high, returned_ref[...]) + dot_nt(rest, returned_ref[...])
    dots = dots * spread_back_ref[...].astype(jnp.float32)
    slot_total = returned_ref.shape[0]
    slot = lax.broadcasted_iota(jnp.int32, (slot_total, LANES), 0) // capacity
    lane = lax.broadcasted_iota(jnp.int32, (slot_total, LANES), 1)
    owner = jnp.where(slot == lane, 1.0, 0.0).astype(jnp.bfloat16)
    high, rest = two_terms(dots)
    pull = dot_nn(high, owner) + dot_nn(rest, owner)
    probs = probs_ref[...]
    low = (probs * (pull - jnp.sum(probs * pull, axis=-1, keepdims=True))).astype(jnp.bfloat16)
    low_ref[...] = low
    router_grad_ref[...] = dot_tn(ffn_ref[...], low)


def router_back(capacity, grad, returned, spread_back, probs, ffn):
    whole = pl.BlockSpec(memory_space=pltpu.VMEM)
    seq_len = grad.shape[0]
    return pl.pallas_call(
        functools.partial(router_kernel, capacity),
        out_shape=(
            jax.ShapeDtypeStruct((seq_len, LANES), jnp.bfloat16),
            jax.ShapeDtypeStruct((D, LANES), jnp.float32),
        ),
        in_specs=[whole] * 5,
        out_specs=[whole] * 2,
        compiler_params=pltpu.CompilerParams(vmem_limit_bytes=48 * 1024 * 1024),
        cost_estimate=pl.CostEstimate(
            flops=4 * seq_len * returned.shape[0] * D,
            bytes_accessed=6 * 1024 * 1024,
            transcendentals=0,
        ),
    )(grad, returned, spread_back, probs, ffn)


def final_kernel(
    capacity,
    gain_row,
    picked_ref,
    middle_ref,
    gates_ref,
    returned_ref,
    spread_ref,
    spread_back_ref,
    gain_ref,
    rows_ref,
    low_ref,
):
    count = rows_ref.shape[0]
    for place in range(count):
        rows_ref[place : place + 1, :] = middle_ref[pl.ds(picked_ref[place], 1), :]
    sublane = lax.broadcasted_iota(jnp.int32, (count, LANES), 0)
    wanted = jnp.zeros((count, LANES), jnp.int32)
    for place in range(count):
        wanted = jnp.where(sublane == place, picked_ref[place], wanted)
    seq_len = middle_ref.shape[0]
    token = lax.broadcasted_iota(jnp.int32, (count, seq_len), 1)
    wanted = jnp.concatenate([wanted] * (seq_len // LANES), axis=1)
    chosen = jnp.where(token == wanted, 1.0, 0.0).astype(jnp.bfloat16)
    slots = dot_nn(chosen, spread_back_ref[...]).astype(jnp.bfloat16)
    weighted = slot_gates(spread_ref[...], gates_ref[...], capacity) * returned_ref[...].astype(
        jnp.float32
    )
    high, rest = two_terms(weighted)
    rows = rows_ref[...] + (dot_nn(slots, high) + dot_nn(slots, rest))
    rows_ref[...] = rows
    low_ref[...] = (rows * inverse_root(rows) * gain_ref[gain_row : gain_row + 1, :]).astype(
        jnp.bfloat16
    )


def final_rows_of(capacity, gain_row, picked, middle, gates, returned, spread, spread_back, gains):
    whole = pl.BlockSpec(memory_space=pltpu.VMEM)
    count = picked.shape[0]
    return pl.pallas_call(
        functools.partial(final_kernel, capacity, gain_row),
        out_shape=(
            jax.ShapeDtypeStruct((count, D), jnp.float32),
            jax.ShapeDtypeStruct((count, D), jnp.bfloat16),
        ),
        in_specs=[pl.BlockSpec(memory_space=pltpu.SMEM)] + [whole] * 6,
        out_specs=[whole] * 2,
        compiler_params=pltpu.CompilerParams(vmem_limit_bytes=48 * 1024 * 1024),
        cost_estimate=pl.CostEstimate(
            flops=1 << 28, bytes_accessed=5 * 1024 * 1024, transcendentals=0
        ),
    )(picked, middle, gates, returned, spread, spread_back, gains)


def tie(first, second):
    return lax.optimization_barrier((first, second))


def swap_pairs(row_groups, turn_plane, turn_row):
    pairs = []
    for plane in range(PLANES):
        for row in range(row_groups):
            for part in range(PLANES):
                source = (plane * row_groups + row) * PLANES + part
                target_plane = (plane + SHIFTS[part ^ turn_plane]) % PLANES
                target_row = (row + turn_row) % row_groups
                target_part = (plane // 2 + target_plane) % 2 * 2 + plane % 2
                pairs.append(
                    (source, (target_plane * row_groups + target_row) * PLANES + target_part)
                )
    return pairs


def all_turns(row_groups):
    return [(plane, row) for row in range(row_groups) for plane in range(PLANES)]


def shift_inverse(shift):
    return jnp.array(SHIFTS, jnp.int32)[shift]


def part_of_turn(turn_plane):
    me_plane = lax.axis_index("z")
    expert_plane = (lax.axis_index("y") + me_plane) % 2 * 2 + lax.axis_index("c")
    return shift_inverse((me_plane - expert_plane) % PLANES) ^ turn_plane


def piece_place(turn, row_groups):
    turn_plane, turn_row = turn
    row = (lax.axis_index("h") - turn_row) % row_groups
    return row * PLANES + part_of_turn(turn_plane)


def spread_experts(piece, row_groups):
    return [
        lax.ppermute(
            piece, ("z", "h", "y", "c"), swap_pairs(row_groups, turn_plane, turn_row)
        )
        for turn_plane, turn_row in all_turns(row_groups)
    ]


def return_expert_grads(pieces, row_groups, chosen=None):
    arrived = []
    for place, (piece, turn) in enumerate(zip(pieces, all_turns(row_groups))):
        if chosen is not None and place not in chosen:
            continue
        back = [(target, source) for source, target in swap_pairs(row_groups, *turn)]
        arrived.append(lax.ppermute(piece, ("z", "h", "y", "c"), back))
    return arrived


def scatter_sum(parts):
    total = parts[0].astype(jnp.float32)
    for part in parts[1:]:
        total = total + part.astype(jnp.float32)
    return total


def send_all(values):
    return lax.all_to_all(values, AXES, split_axis=0, concat_axis=0, tiled=True)


def send_plane(values):
    return lax.all_to_all(values, ("x", "y", "c"), split_axis=0, concat_axis=0, tiled=True)


def three_terms(values):
    first = lax.reduce_precision(values, 8, 7)
    second = lax.reduce_precision(values - first, 8, 7)
    third = lax.reduce_precision(values - first - second, 8, 7)
    return [first, second, third]

PLANE_RING = ("x", "y", "c")


def plane_partners():
    at = {name: lax.axis_index(name) for name in PLANE_RING}
    partners, groups = [None], [at["x"] * 4 + at["y"] * 2 + at["c"]]
    for turn in range(1, 8):
        flips = {"x": turn // 4, "y": turn // 2 % 2, "c": turn % 2}
        there = {name: 1 - at[name] if flips[name] else at[name] for name in PLANE_RING}
        partners.append({name: there[name] for name in PLANE_RING if flips[name]})
        groups.append(there["x"] * 4 + there["y"] * 2 + there["c"])
    return partners, groups


def part_places(part_count):
    plane = lax.axis_index("z")
    expert_plane = lax.rem(lax.axis_index("y") + plane, 2) * 2 + lax.axis_index("c")
    shift = lax.rem(plane - expert_plane + PLANES, PLANES)
    upper, lower = lax.rem(shift, 2), shift // 2
    places = []
    for turn in range(part_count):
        first = 1 - upper if turn // 2 else upper
        second = 1 - lower if turn % 2 else lower
        places.append(first * 2 + second)
    return places


def greet(partners):
    barrier = pltpu.get_barrier_semaphore()
    for partner in partners:
        pl.semaphore_signal(
            barrier, inc=1, device_id=partner, device_id_type=pl.DeviceIdType.MESH
        )
    pl.semaphore_wait(barrier, len(partners))


def push(source, target, send_sem, recv_sem, place, partner):
    copy = pltpu.make_async_remote_copy(
        src_ref=source,
        dst_ref=target,
        send_sem=send_sem.at[place],
        recv_sem=recv_sem.at[place],
        device_id=partner,
        device_id_type=pl.DeviceIdType.MESH,
    )
    copy.start()
    return copy


FAR_FIRST = (6, 7, 4, 5, 2, 3, 1)


def exchange_out(outgoing_ref, received_ref, send_sem, recv_sem, partners, groups):
    copies = {}
    for turn in FAR_FIRST:
        copies[turn] = push(
            outgoing_ref.at[groups[turn]],
            received_ref.at[turn],
            send_sem,
            recv_sem,
            turn,
            partners[turn],
        )
    received_ref[0] = outgoing_ref[groups[0]]
    return copies


def flat_rows(block):
    return block.reshape(block.shape[0] * block.shape[1], block.shape[2])


def two_blocks(ref, pair):
    return flat_rows(ref[2 * pair : 2 * pair + 2])


def put_two(ref, pair, values):
    rows = values.shape[0] // 2
    ref[2 * pair] = values[:rows]
    ref[2 * pair + 1] = values[rows:]


def forward_exchange_kernel(part_count, outgoing_ref, *refs):
    part_refs, refs = refs[:part_count], refs[part_count:]
    returned_ref, received_ref, up_ref, down_ref, produced_ref, copy_sem, send_sem, recv_sem = refs
    partners, groups = plane_partners()
    greet(partners[1:])
    copies = exchange_out(outgoing_ref, received_ref, send_sem, recv_sem, partners, groups)
    fetch_expert(part_places(part_count), part_refs, up_ref, down_ref, copy_sem)
    back = {}
    for pair in range(4):
        for turn in (2 * pair, 2 * pair + 1):
            if turn:
                copies[turn].wait_recv()
        gate_part, up_part, sigmoid = silu_parts(
            dot_nn(two_blocks(received_ref, pair), up_ref[...])
        )
        activated = (gate_part * sigmoid * up_part).astype(jnp.bfloat16)
        put_two(produced_ref, pair, dot_nn(activated, down_ref[...]).astype(jnp.bfloat16))
        for turn in (2 * pair, 2 * pair + 1):
            if turn:
                back[turn] = push(
                    produced_ref.at[turn],
                    returned_ref.at[groups[0]],
                    send_sem,
                    recv_sem,
                    8 + turn,
                    partners[turn],
                )
    returned_ref[groups[0]] = produced_ref[0]
    for turn in range(1, 8):
        copies[turn].wait_send()
        back[turn].wait()


def forward_exchange(outgoing, parts):
    whole, _, apart, scratch = expert_specs(parts)
    shape = jax.ShapeDtypeStruct(outgoing.shape, jnp.bfloat16)
    slot_total = outgoing.shape[0] * outgoing.shape[1]
    return pl.pallas_call(
        functools.partial(forward_exchange_kernel, len(parts)),
        out_shape=(shape, shape),
        in_specs=[whole] + apart,
        out_specs=[whole] * 2,
        scratch_shapes=scratch[:2]
        + [
            pltpu.VMEM(outgoing.shape, jnp.bfloat16),
            scratch[2],
            pltpu.SemaphoreType.DMA((16,)),
            pltpu.SemaphoreType.DMA((16,)),
        ],
        compiler_params=pltpu.CompilerParams(
            vmem_limit_bytes=56 * 1024 * 1024, collective_id=2, has_side_effects=True
        ),
        cost_estimate=pl.CostEstimate(
            flops=slot_total * D * F * 6, bytes_accessed=150 * 1024 * 1024, transcendentals=1 << 19
        ),
    )(outgoing, *parts)


def backward_exchange_kernel(
    part_count,
    capacity,
    outgoing_ref,
    received_ref,
    grad_ref,
    returned_ref,
    spread_back_ref,
    probs_ref,
    ffn_ref,
    *refs,
):
    part_refs, refs = refs[:part_count], refs[part_count:]
    out_refs, refs = refs[:part_count], refs[part_count:]
    (
        back_ref,
        low_ref,
        router_grad_ref,
        pull_ref,
        gate_grad_ref,
        activated_ref,
        input_grad_ref,
        up_ref,
        down_ref,
        up_grad_ref,
        down_grad_ref,
        copy_sem,
        send_sem,
        recv_sem,
    ) = refs
    partners, groups = plane_partners()
    greet(partners[1:])
    copies = exchange_out(outgoing_ref, pull_ref, send_sem, recv_sem, partners, groups)
    fetch_expert(part_places(part_count), part_refs, up_ref, down_ref, copy_sem)
    back = {}
    for pair in range(4):
        rows = slice(pair * 2 * capacity, (pair + 1) * 2 * capacity)
        gate_part, up_part, sigmoid = silu_parts(
            dot_nn(two_blocks(received_ref, pair), up_ref[...])
        )
        side = gate_part * sigmoid
        activated_ref[rows, :] = (side * up_part).astype(jnp.bfloat16)
        slope = up_part * sigmoid * (1.0 + gate_part * (1.0 - sigmoid))
        for turn in (2 * pair, 2 * pair + 1):
            if turn:
                copies[turn].wait_recv()
        pulled = dot_nt(two_blocks(pull_ref, pair), down_ref[...]).astype(jnp.bfloat16)
        pulled = pulled.astype(jnp.float32)
        gate_grad_ref[rows, :F] = (pulled * slope).astype(jnp.bfloat16)
        gate_grad_ref[rows, F:] = (pulled * side).astype(jnp.bfloat16)
        put_two(
            input_grad_ref, pair, dot_nt(gate_grad_ref[rows, :], up_ref[...]).astype(jnp.bfloat16)
        )
        for turn in (2 * pair, 2 * pair + 1):
            if turn:
                back[turn] = push(
                    input_grad_ref.at[turn],
                    back_ref.at[groups[0]],
                    send_sem,
                    recv_sem,
                    8 + turn,
                    partners[turn],
                )
        if pair == 0:
            router_kernel(
                capacity,
                grad_ref,
                returned_ref,
                spread_back_ref,
                probs_ref,
                ffn_ref,
                low_ref,
                router_grad_ref,
            )
    back_ref[groups[0]] = input_grad_ref[0]
    block = 256

    @pl.loop(0, D // block)
    def _(step):
        columns = pl.ds(pl.multiple_of(step * block, block), block)
        up_grad_ref[columns, :] = dot_tn(
            flat_rows(received_ref[:, :, columns]), gate_grad_ref[...]
        ).astype(jnp.bfloat16)

    @pl.loop(0, F // block)
    def _(step):
        columns = pl.ds(pl.multiple_of(step * block, block), block)
        down_grad_ref[columns, :] = dot_tn(
            activated_ref[:, columns], flat_rows(pull_ref[...])
        ).astype(jnp.bfloat16)

    rows = out_refs[0].shape[0]
    for out_ref, own_place in zip(out_refs, part_places(part_count)):
        place = pl.multiple_of(own_place * rows, rows)
        out_ref[:, : 2 * F] = up_grad_ref[pl.ds(place, rows), :]
        for part in range(F // rows):
            out_ref[:, 2 * F + part * rows : 2 * F + (part + 1) * rows] = down_grad_ref[
                part * rows : (part + 1) * rows, pl.ds(place, rows)
            ]
    for turn in range(1, 8):
        copies[turn].wait_send()
        back[turn].wait()


def backward_exchange(
    capacity, outgoing, received, grad, returned, spread_back, probs, ffn, parts
):
    whole, _, apart, scratch = expert_specs(parts)
    slot_total = outgoing.shape[0] * outgoing.shape[1]
    piece_rows = parts[0].shape[0]
    seq_len = grad.shape[0]
    low = jnp.bfloat16
    return pl.pallas_call(
        functools.partial(backward_exchange_kernel, len(parts), capacity),
        out_shape=[jax.ShapeDtypeStruct((piece_rows, 3 * F), low)] * len(parts)
        + [
            jax.ShapeDtypeStruct(outgoing.shape, low),
            jax.ShapeDtypeStruct((seq_len, LANES), low),
            jax.ShapeDtypeStruct((D, LANES), jnp.float32),
        ],
        in_specs=[whole] * 7 + apart,
        out_specs=[whole] * (len(parts) + 3),
        scratch_shapes=[
            pltpu.VMEM(outgoing.shape, low),
            pltpu.VMEM((slot_total, 2 * F), low),
            pltpu.VMEM((slot_total, F), low),
            pltpu.VMEM(outgoing.shape, low),
        ]
        + scratch[:2]
        + scratch[:2]
        + [
            scratch[2],
            pltpu.SemaphoreType.DMA((16,)),
            pltpu.SemaphoreType.DMA((16,)),
        ],
        compiler_params=pltpu.CompilerParams(
            vmem_limit_bytes=58 * 1024 * 1024, collective_id=3, has_side_effects=True
        ),
        cost_estimate=pl.CostEstimate(
            flops=slot_total * D * F * 18,
            bytes_accessed=180 * 1024 * 1024,
            transcendentals=1 << 19,
        ),
    )(outgoing, received, grad, returned, spread_back, probs, ffn, *parts)


RING = ("z", "x", "y", "c")


def owner_sum_kernel(
    layers,
    *refs,
):
    grads, refs = refs[:layers], refs[layers:]
    (
        out_ref,
        own_ref,
        core_ref,
        near_ref,
        joined_ref,
        turn_ref,
        last_ref,
        got_ref,
        local_sem,
        send_sem,
        recv_sem,
    ) = refs
    at = {name: lax.axis_index(name) for name in RING}
    planes = lax.axis_size("z")
    barrier = pltpu.get_barrier_semaphore()
    partners = [{name: 1 - at[name]} for name in ("c", "x", "y")]
    partners += [{"z": lax.rem(at["z"] + turn, planes)} for turn in range(1, planes)]
    for partner in partners:
        pl.semaphore_signal(
            barrier, inc=1, device_id=partner, device_id_type=pl.DeviceIdType.MESH
        )
    pl.semaphore_wait(barrier, len(partners))

    width = own_ref.shape[-1]
    half = width // 2
    per_layer = grads[0].shape[-1] // width
    chunk_count = layers * per_layer
    copies = {}

    def send(chunk_index, step, source, target, partner):
        place = chunk_index * 8 + step
        copy = pltpu.make_async_remote_copy(
            src_ref=source,
            dst_ref=target,
            send_sem=send_sem.at[place],
            recv_sem=recv_sem.at[place],
            device_id=partner,
            device_id_type=pl.DeviceIdType.MESH,
        )
        copy.start()
        copies[place] = copy

    def arrived(chunk_index, *steps):
        for step in steps:
            copies[chunk_index * 8 + step].wait()

    def source_of(chunk_index, core):
        layer, part = chunk_index // per_layer, chunk_index % per_layer
        return grads[layer].at[:, :, :, core, :, pl.ds(part * width, width)]

    def added(left, right):
        return (left.astype(jnp.float32) + right.astype(jnp.float32)).astype(jnp.bfloat16)

    local = []
    for index in range(chunk_count):
        copy = pltpu.make_async_copy(
            source_of(index, at["c"]), own_ref.at[index], local_sem.at[index]
        )
        copy.start()
        local.append(copy)
        send(index, 0, source_of(index, 1 - at["c"]), core_ref.at[index], partners[0])

    def stage_core(index):
        local[index].wait()
        arrived(index, 0)
        for plane in range(planes):
            own_ref[index, plane] = added(own_ref[index, plane], core_ref[index, plane])
        send(
            index,
            1,
            own_ref.at[index, :, 1 - at["x"], :, :, pl.ds(0, half)],
            near_ref.at[index, 0],
            partners[1],
        )
        send(
            index,
            2,
            own_ref.at[index, :, :, 1 - at["y"], :, pl.ds(half, half)],
            near_ref.at[index, 1],
            partners[2],
        )

    def stage_near(index):
        arrived(index, 1, 2)
        for plane in range(planes):
            for other in range(2):
                joined_ref[index, 0, plane, other] = added(
                    own_ref[index, plane, at["x"], other, :, :half],
                    near_ref[index, 0, plane, other],
                )
                joined_ref[index, 1, plane, other] = added(
                    own_ref[index, plane, other, at["y"], :, half:],
                    near_ref[index, 1, plane, other],
                )
        send(
            index,
            3,
            joined_ref.at[index, 0, :, 1 - at["y"]],
            turn_ref.at[index, 0],
            partners[2],
        )
        send(
            index,
            4,
            joined_ref.at[index, 1, :, 1 - at["x"]],
            turn_ref.at[index, 1],
            partners[1],
        )

    def stage_turn(index):
        arrived(index, 3, 4)
        for plane in range(planes):
            last_ref[index, plane, :, :half] = added(
                joined_ref[index, 0, plane, at["y"]], turn_ref[index, 0, plane]
            )
            last_ref[index, plane, :, half:] = added(
                joined_ref[index, 1, plane, at["x"]], turn_ref[index, 1, plane]
            )
        for turn in range(1, planes):
            send(
                index,
                4 + turn,
                last_ref.at[index, partners[2 + turn]["z"]],
                got_ref.at[index, turn - 1],
                partners[2 + turn],
            )

    def stage_planes(index):
        arrived(index, *[4 + turn for turn in range(1, planes)])
        total = last_ref[index, at["z"]].astype(jnp.float32)
        for turn in range(1, planes):
            total = total + got_ref[index, turn - 1].astype(jnp.float32)
        layer, part = index // per_layer, index % per_layer
        out_ref[layer, :, part * width : (part + 1) * width] = total

    stages = (stage_core, stage_near, stage_turn, stage_planes)
    for step in range(chunk_count + len(stages) - 1):
        for number, stage in enumerate(stages):
            if 0 <= step - number < chunk_count:
                stage(step - number)


def owner_sums(grads, width=2048):
    layers = len(grads)
    sizes = [lax.axis_size(name) for name in RING]
    rows, columns = grads[0].shape
    own_rows = rows // (sizes[0] * sizes[1] * sizes[2] * sizes[3])
    chunks = layers * columns // width
    blocks = [grad.reshape(*sizes, own_rows, columns) for grad in grads]
    half = width // 2
    low = jnp.bfloat16
    return pl.pallas_call(
        functools.partial(owner_sum_kernel, layers),
        out_shape=jax.ShapeDtypeStruct((layers, own_rows, columns), jnp.float32),
        in_specs=[pl.BlockSpec(memory_space=pl.ANY)] * layers,
        out_specs=pl.BlockSpec(memory_space=pltpu.VMEM),
        scratch_shapes=[
            pltpu.VMEM((chunks, sizes[0], 2, 2, own_rows, width), low),
            pltpu.VMEM((chunks, sizes[0], 2, 2, own_rows, width), low),
            pltpu.VMEM((chunks, 2, sizes[0], 2, own_rows, half), low),
            pltpu.VMEM((chunks, 2, sizes[0], 2, own_rows, half), low),
            pltpu.VMEM((chunks, 2, sizes[0], own_rows, half), low),
            pltpu.VMEM((chunks, sizes[0], own_rows, width), low),
            pltpu.VMEM((chunks, sizes[0] - 1, own_rows, width), low),
            pltpu.SemaphoreType.DMA((chunks,)),
            pltpu.SemaphoreType.DMA((chunks * 8,)),
            pltpu.SemaphoreType.DMA((chunks * 8,)),
        ],
        compiler_params=pltpu.CompilerParams(
            vmem_limit_bytes=56 * 1024 * 1024, collective_id=1, has_side_effects=True
        ),
        cost_estimate=pl.CostEstimate(
            flops=1 << 26, bytes_accessed=200 * 1024 * 1024, transcendentals=0
        ),
    )(*blocks)


def adam_step(weight, mean_old, square_old, gradient):
    mean_new = BETA_ONE * mean_old + (1.0 - BETA_ONE) * gradient
    square_new = BETA_TWO * square_old + (1.0 - BETA_TWO) * gradient * gradient
    bias_one = 1.0 - BETA_ONE**ADAM_STEP
    bias_two = 1.0 - BETA_TWO**ADAM_STEP
    update = -LEARN_RATE * (
        mean_new / bias_one / (jnp.sqrt(square_new / bias_two) + ADAM_EPS) + DECAY_RATE * weight
    )
    return (mean_new, square_new, update)


VOCAB_BLOCK = 2048
VOCAB_PART = 512


def embedding_kernel(
    row_ref,
    low_ref,
    high_ref,
    arrived_ref,
    word_ref,
    group_ref,
    weight_ref,
    mean_ref,
    square_ref,
    mean_out_ref,
    square_out_ref,
    update_ref,
    wide_ref,
    sorted_ref,
    turned_ref,
    total_ref,
):
    step = pl.program_id(0)
    device_count = arrived_ref.shape[0]
    token_count = sorted_ref.shape[0]
    columns = weight_ref.shape[0]
    groups = LANES // columns

    @pl.when(step == 0)
    def _():
        for part in range(wide_ref.shape[0] // device_count):
            wide_ref[part * device_count : (part + 1) * device_count, :] = arrived_ref[
                :, part * LANES : (part + 1) * LANES
            ].astype(jnp.float32)

        @pl.loop(0, token_count // 32)
        def _(block):
            start = pl.multiple_of(block * 32, 32)
            for place in range(32):
                sorted_ref[pl.ds(start + place, 1), :] = wide_ref[pl.ds(row_ref[start + place], 1), :]

        row_place = lax.broadcasted_iota(jnp.int32, (LANES, LANES), 0)
        lane = lax.broadcasted_iota(jnp.int32, (LANES, LANES), 1)
        same = jnp.where(row_place == lane, 1.0, 0.0).astype(jnp.bfloat16)

        @pl.loop(0, token_count // LANES)
        def _(block):
            rows = pl.ds(pl.multiple_of(block * LANES, LANES), LANES)
            turned = dot_nt(same, sorted_ref[rows, :].astype(jnp.bfloat16))
            group = group_ref[pl.ds(block, 1), :]
            kept = jnp.where(group == 0, turned[:columns, :], 0.0)
            for place in range(1, groups):
                kept += jnp.where(
                    group == place, turned[place * columns : (place + 1) * columns, :], 0.0
                )
            turned_ref[:, rows] = kept.astype(jnp.bfloat16)

    for part in range(VOCAB_BLOCK // VOCAB_PART):
        total_ref[...] = jnp.zeros_like(total_ref)
        place = step * (VOCAB_BLOCK // VOCAB_PART) + part
        first = place * VOCAB_PART

        @pl.loop(low_ref[place], high_ref[place])
        def _(block):
            rows = pl.ds(pl.multiple_of(block * LANES, LANES), LANES)
            word = lax.broadcasted_iota(jnp.int32, (VOCAB_PART, LANES), 0)
            hit = word == word_ref[pl.ds(block, 1), :] - first
            hit = jnp.where(hit, 1.0, 0.0).astype(jnp.bfloat16)
            total_ref[...] += dot_nt(turned_ref[:, rows], hit)

        gradient = total_ref[...]
        words = slice(part * VOCAB_PART, (part + 1) * VOCAB_PART)
        mean_new, square_new, update = adam_step(
            weight_ref[:, words], mean_ref[:, words], square_ref[:, words], gradient
        )
        mean_out_ref[:, words] = mean_new
        square_out_ref[:, words] = square_new
        update_ref[:, words] = update


def token_order(tokens, seq_len, vocabulary, groups):
    count = tokens.shape[0]
    devices = count // seq_len
    keys = lax.sort(tokens * count + jnp.arange(count, dtype=jnp.int32))
    words, origin = keys // count, keys % count
    device, place = origin // seq_len, origin % seq_len
    row = (place // groups) * devices + device
    words = words.reshape(count // LANES, LANES)
    group = (place % groups).reshape(count // LANES, LANES)
    steps = -(-vocabulary // VOCAB_BLOCK) * (VOCAB_BLOCK // VOCAB_PART)
    edges = jnp.arange(steps + 1, dtype=jnp.int32) * VOCAB_PART
    below = jnp.sum((tokens[None, :] < edges[:, None]).astype(jnp.int32), axis=1)
    low = below[:-1] // LANES
    high = (below[1:] + LANES - 1) // LANES
    high = jnp.where(below[1:] > below[:-1], high, low)
    return row, low, high, words, group


def embedding_update_of(order, arrived, weight, mean, square):
    row, low, high, words, group = order
    count = row.shape[0]
    columns, vocabulary = weight.shape
    block = pl.BlockSpec((columns, VOCAB_BLOCK), lambda step: (0, step))
    whole = pl.BlockSpec(memory_space=pltpu.VMEM)
    scalar = pl.BlockSpec(memory_space=pltpu.SMEM)
    wide = count * columns // LANES
    return pl.pallas_call(
        embedding_kernel,
        grid=(-(-vocabulary // VOCAB_BLOCK),),
        out_shape=[jax.ShapeDtypeStruct(weight.shape, jnp.float32)] * 3,
        in_specs=[scalar] * 3 + [whole] * 3 + [block] * 3,
        out_specs=[block] * 3,
        scratch_shapes=[
            pltpu.VMEM((wide, LANES), jnp.float32),
            pltpu.VMEM((count, LANES), jnp.float32),
            pltpu.VMEM((columns, count), jnp.bfloat16),
            pltpu.VMEM((columns, VOCAB_PART), jnp.float32),
        ],
        compiler_params=pltpu.CompilerParams(vmem_limit_bytes=48 * 1024 * 1024),
        cost_estimate=pl.CostEstimate(
            flops=1 << 32, bytes_accessed=50 * 1024 * 1024, transcendentals=1 << 20
        ),
    )(row, low, high, arrived, words, group, weight, mean, square)


def shards(
    tokens,
    prefix,
    routes,
    picked,
    loss_ids,
    teacher_logits,
    embedding,
    embedding_mean,
    embedding_square,
    attention,
    attention_mean,
    attention_square,
    router,
    router_mean,
    router_square,
    norm_gains,
    gains_mean,
    gains_square,
    expert_up,
    upward_mean,
    upward_square,
    expert_down,
    downward_mean,
    downward_square,
    output_table,
    table_mean,
    table_square,
):
    devices_all = lax.axis_size(AXES)
    me_all = lax.axis_index(AXES)
    row_groups = lax.axis_size("h")
    columns_x = lax.axis_size("x")
    seq_len = routes.shape[0]
    layer_count = attention.shape[0]
    experts_all = router.shape[2]
    capacity = 9 * seq_len * TOPK // (8 * experts_all)
    column_count = embedding.shape[1]
    prefix_len = prefix[0]
    slot_total = experts_all * capacity
    piece_rows = expert_up.shape[2]
    gain_count = norm_gains.shape[0]
    me_plane = lax.axis_index("z")
    member_place = jnp.arange(experts_all, dtype=jnp.int32)
    member_part = member_place % PLANES
    group_order = (
        (member_part // 2 + me_plane) % 2 * 2 + member_part % 2
    ) * columns_x + member_place // PLANES
    expert_plane = member_place // columns_x
    group_back = (
        member_place % columns_x * PLANES
        + (expert_plane // 2 + me_plane) % 2 * 2
        + expert_plane % 2
    )


    head_low = output_table.astype(jnp.bfloat16)
    vocab_local = head_low.shape[0]
    teacher_log = jax.nn.log_softmax(teacher_logits, axis=1)
    teacher_prob = jnp.exp(teacher_log)
    position_count = loss_ids.shape[0]
    teacher_mass = jnp.sum(teacher_prob, axis=1)
    coefficients = jnp.concatenate(
        [jnp.ones((position_count, 1), jnp.float32), teacher_prob], axis=1
    )
    table_low = embedding.astype(jnp.bfloat16)
    looked_up = jnp.take(table_low, tokens, axis=0, mode="clip").reshape(devices_all, seq_len * column_count)
    attention_low = []
    for layer_index in range(layer_count):
        rows_low = attention[layer_index].astype(jnp.bfloat16)
        if layer_index > 0:
            rows_low, looked_up = tie(rows_low, looked_up)
        attention_low.append(lax.all_gather(rows_low, AXES, axis=0, tiled=True))
    small_count = gain_count + layer_count * experts_all
    small = jnp.concatenate(
        [norm_gains.T, router.transpose(1, 0, 2).reshape(column_count, layer_count * experts_all)],
        axis=1,
    ).astype(jnp.bfloat16)
    small = jnp.broadcast_to(
        small.reshape(1, column_count * small_count), (devices_all, column_count * small_count)
    )
    arrived_rows = send_all(jnp.concatenate([looked_up, small], axis=1))
    expert_parts, expert_pieces = [], []
    for layer_index in range(layer_count):
        down_piece = (
            expert_down[0, layer_index]
            .reshape(F // piece_rows, piece_rows, piece_rows)
            .transpose(1, 0, 2)
            .reshape(piece_rows, F)
        )
        piece = jnp.concatenate([expert_up[0, layer_index], down_piece], axis=1).astype(
            jnp.bfloat16
        )
        expert_pieces.append(piece)
    expert_pieces[0], arrived_rows = tie(expert_pieces[0], arrived_rows)
    expert_parts.append(spread_experts(expert_pieces[0], row_groups))

    hidden = (
        arrived_rows[:, : seq_len * column_count]
        .reshape(devices_all, seq_len, column_count)
        .transpose(1, 0, 2)
        .reshape(seq_len, D)
        .astype(jnp.float32)
    )
    small_all = arrived_rows[:, seq_len * column_count :].reshape(D, small_count)
    gain_rows = jnp.pad(
        small_all[:, :gain_count].T.astype(jnp.float32), ((0, 16 - gain_count), (0, 0))
    )
    router_low = jnp.pad(
        small_all[:, gain_count:]
        .reshape(D, layer_count, experts_all)
        .transpose(1, 0, 2)[:, :, group_order],
        ((0, 0), (0, 0), (0, LANES - experts_all)),
    )

    fits_sum = [lax.axis_size(name) for name in AXES] == [PLANES, 2, 1, 2, 2]

    member = jnp.any(routes[:, :, None] == group_order[None, None, :], axis=1)
    before = jnp.dot(
        jnp.tril(jnp.ones((seq_len, seq_len), jnp.bfloat16), -1),
        member.astype(jnp.bfloat16),
        preferred_element_type=jnp.float32,
    ).astype(jnp.int32)
    spread = (
        (before.T[:, None, :] == jnp.arange(capacity, dtype=jnp.int32)[None, :, None])
        & member.T[:, None, :]
    ).astype(jnp.bfloat16)
    spread_flat = spread.reshape(slot_total, seq_len)
    spread_back = spread_flat.T
    kept = jnp.pad(
        (member & (before < capacity)).astype(jnp.float32), ((0, 0), (0, LANES - experts_all))
    )
    turns = turn_tables(seq_len)
    places = jnp.stack([piece_place(turn, row_groups) for turn in all_turns(row_groups)]).astype(
        jnp.int32
    )

    stored = []
    extra = ()
    for layer_index in range(layer_count):
        saved = forward_layer(
            layer_index,
            capacity,
            experts_all,
            prefix,
            hidden,
            extra,
            attention_low[layer_index],
            gain_rows,
            turns,
            router_low,
            kept,
            spread_flat,
            spread_back,
        )
        hidden = saved[6]
        gates, outgoing = saved[9], saved[10]
        if layer_index + 1 < layer_count:
            piece, outgoing = tie(expert_pieces[layer_index + 1], outgoing)
            expert_parts.append(spread_experts(piece, row_groups))
        blocks = outgoing.reshape(experts_all, capacity, D)
        if fits_sum:
            returned, received = forward_exchange(blocks, expert_parts[layer_index])
        else:
            received = send_plane(blocks).reshape(slot_total, D)
            produced = run_expert(places, received, expert_parts[layer_index])
            returned = send_plane(produced.reshape(experts_all, capacity, D))
        returned = returned.reshape(slot_total, D)
        if layer_index + 1 < layer_count:
            expert_parts[-1][:2], returned = tie(expert_parts[-1][:2], returned)
        stored.append((saved, received, returned))
        extra = (gates, returned)

    order = token_order(tokens, seq_len, embedding.shape[0], LANES // column_count)
    local_ids = loss_ids - me_all * vocab_local
    vocab_place = jnp.arange(vocab_local, dtype=jnp.int32)
    marked = jnp.sum(
        jnp.where(
            local_ids[:, :, None] == vocab_place[None, None, :], coefficients[:, :, None], 0.0
        ),
        axis=1,
    )
    marked_pull = jnp.dot(
        marked.astype(jnp.bfloat16), head_low, preferred_element_type=jnp.float32
    )
    own_count = position_count // devices_all

    final_gain = gain_rows[4 * layer_count]
    final_rows, final_low = final_rows_of(
        capacity,
        4 * layer_count,
        picked,
        hidden,
        *extra,
        spread_flat,
        spread_back,
        gain_rows,
    )
    all_rows = send_all(jnp.broadcast_to(final_low[None], (devices_all, own_count, D))).reshape(
        position_count, D
    )
    logits = jnp.einsum("pd,vd->pv", all_rows, head_low, preferred_element_type=jnp.float32)
    local_peak = jnp.max(logits, axis=1)
    local_exp = jnp.exp(logits - local_peak[:, None])
    local_sum = jnp.sum(local_exp, axis=1)
    local_dot = jnp.sum(marked * logits, axis=1)
    pull = jnp.dot(local_exp.astype(jnp.bfloat16), head_low, preferred_element_type=jnp.float32)
    stats = jnp.stack(
        three_terms(local_peak) + three_terms(local_sum) + three_terms(local_dot), axis=1
    )
    stats = jnp.pad(stats, ((0, 0), (0, 128 - stats.shape[1])))
    pull_sent = jnp.concatenate([pull, marked_pull, stats], axis=1).astype(jnp.bfloat16)
    pull_got = send_all(pull_sent.reshape(devices_all, own_count, 2 * D + 128)).astype(jnp.float32)
    stats_got = pull_got[:, :, 2 * D :]
    peaks = jnp.sum(stats_got[:, :, 0:3], axis=2)
    sums = jnp.sum(stats_got[:, :, 3:6], axis=2)
    dots = jnp.sum(stats_got[:, :, 6:9], axis=2)
    peak_own = jnp.max(peaks, axis=0)
    log_norm_own = peak_own + jnp.log(jnp.sum(sums * jnp.exp(peaks - peak_own), axis=0))
    mass_own = lax.dynamic_slice_in_dim(teacher_mass, me_all * own_count, own_count)
    entropy_own = lax.dynamic_slice_in_dim(
        jnp.sum(teacher_prob * teacher_log, axis=1), me_all * own_count, own_count
    )
    loss_own = (1.0 + mass_own) * log_norm_own - jnp.sum(dots, axis=0) + entropy_own
    scale_own = (1.0 + mass_own)[None, :] * jnp.exp(peaks - log_norm_own[None, :])
    marked_total = jnp.sum(pull_got[:, :, D : 2 * D], axis=0)
    final_grad = (
        jnp.sum(scale_own[:, :, None] * pull_got[:, :, :D], axis=0) - marked_total
    ) / position_count
    spread_stats = jnp.concatenate([log_norm_own, loss_own]).reshape(1, 2 * own_count)
    stats_all = send_all(jnp.broadcast_to(spread_stats, (devices_all, 2 * own_count)))
    log_norm = stats_all[:, :own_count].reshape(position_count)
    loss_value = jnp.sum(stats_all[:, own_count:]) / position_count
    grad_logits = (
        jnp.exp(logits - log_norm[:, None]) * (1.0 + teacher_mass)[:, None] - marked
    ) / position_count
    table_grad = jnp.einsum(
        "pv,pd->vd",
        grad_logits.astype(jnp.bfloat16),
        all_rows,
        preferred_element_type=jnp.float32,
    )
    rows_grad, final_gain_grad = norm_back(final_rows, final_gain, final_grad)
    grad_hidden, sent_back = first_pull(capacity, picked, rows_grad, spread_flat, extra[0])
    gain_parts = [None] * (4 * layer_count) + [final_gain_grad]
    attention_parts = [None] * layer_count
    router_parts = [None] * layer_count
    piece_parts = [None] * layer_count
    for layer_index in reversed(range(layer_count)):
        saved, received, returned = stored[layer_index]
        hidden_in, projected, queries, keys, values, attended, middle, ffn_low, probs = saved[:9]
        upper = layer_index + 1 if layer_index + 1 < layer_count else None
        blocks = sent_back.reshape(experts_all, capacity, D)
        if fits_sum:
            *grad_pieces, back_inputs, logit_low, router_parts[layer_index] = backward_exchange(
                capacity,
                blocks,
                received,
                grad_hidden,
                returned,
                spread_back,
                probs,
                ffn_low,
                expert_parts[layer_index],
            )
        else:
            output_grad = send_plane(blocks).reshape(slot_total, D)
            logit_low, router_parts[layer_index] = router_back(
                capacity, grad_hidden, returned, spread_back, probs, ffn_low
            )
            input_grad, gate_grad, activated = run_expert_back(
                places, received, output_grad, expert_parts[layer_index]
            )
            back_inputs = send_plane(input_grad.reshape(experts_all, capacity, D))
            grad_pieces = run_expert_grad(
                places, received, output_grad, gate_grad, activated, piece_rows
            )
        back_inputs = back_inputs.reshape(slot_total, D)
        if upper is not None:
            piece_parts[upper][1:], back_inputs = tie(piece_parts[upper][1:], back_inputs)
        if layer_index > 0:
            piece_parts[layer_index] = return_expert_grads(grad_pieces, row_groups)
        else:
            turns_all = len(grad_pieces)
            early = range(turns_all // 2)
            piece_parts[0] = return_expert_grads(grad_pieces, row_groups, early)
        lower = (spread_flat, stored[layer_index - 1][0][9]) if layer_index > 0 else ()
        results = backward_layer(
            layer_index,
            capacity,
            prefix,
            grad_hidden,
            back_inputs,
            logit_low,
            hidden_in,
            projected,
            queries,
            keys,
            values,
            attended,
            middle,
            attention_low[layer_index],
            gain_rows,
            turns,
            router_low,
            spread_back,
            lower,
        )
        grad_hidden, weight_grad, gain_grads = results[:3]
        gain_parts[4 * layer_index : 4 * layer_index + 4] = list(gain_grads[:4])
        if layer_index > 0:
            sent_back = results[3]
            piece_parts[layer_index][:1], sent_back = tie(piece_parts[layer_index][:1], sent_back)
        attention_parts[layer_index] = weight_grad
        if not fits_sum:
            attention_parts[layer_index] = lax.psum_scatter(
                weight_grad, AXES, scatter_dimension=0, tiled=True
            ).astype(jnp.float32)

    sending = (
        grad_hidden.astype(jnp.bfloat16)
        .reshape(seq_len, devices_all, column_count)
        .transpose(1, 0, 2)
        .reshape(devices_all, seq_len * column_count)
    )
    small_grads = jnp.concatenate(
        [jnp.stack(gain_parts, axis=1)] + [part[:, group_back] for part in router_parts], axis=1
    ).astype(jnp.bfloat16)
    arrived_grads = send_all(
        jnp.concatenate(
            [sending, small_grads.reshape(devices_all, column_count * small_count)], axis=1
        )
    )
    piece_parts[0], attention_parts = tie(piece_parts[0], attention_parts)
    if fits_sum:
        attention_parts = list(owner_sums(attention_parts[::-1], 2048))[::-1]
    grad_pieces, arrived_grads, attention_parts = lax.optimization_barrier(
        (grad_pieces, arrived_grads, attention_parts)
    )
    late = range(turns_all // 2, turns_all)
    piece_parts[0] = piece_parts[0] + return_expert_grads(grad_pieces, row_groups, late)
    embedding_next = embedding_update_of(
        order,
        arrived_grads[:, : seq_len * column_count],
        embedding.T,
        embedding_mean.T,
        embedding_square.T,
    )
    piece_parts[0], embedding_next = tie(piece_parts[0], embedding_next)
    up_parts, down_parts = [], []
    for parts in piece_parts:
        piece_grad = scatter_sum(parts)
        up_parts.append(piece_grad[:, : 2 * F])
        down_parts.append(
            piece_grad[:, 2 * F :]
            .reshape(piece_rows, F // piece_rows, piece_rows)
            .transpose(1, 0, 2)
            .reshape(F, piece_rows)
        )
    small_total = jnp.sum(
        arrived_grads[:, seq_len * column_count :].astype(jnp.float32), axis=0
    ).reshape(column_count, small_count)
    gains_grad = small_total[:, :gain_count].T
    router_grad = (
        small_total[:, gain_count:]
        .reshape(column_count, layer_count, experts_all)
        .transpose(1, 0, 2)
    )
    attention_grad = jnp.stack(attention_parts)
    upward_grad = jnp.stack(up_parts)[None]
    downward_grad = jnp.stack(down_parts)[None]
    embedding_mean_next, embedding_square_next, embedding_update = [
        part.T for part in embedding_next
    ]
    attention_mean_next, attention_square_next, attention_update = adam_step(
        attention, attention_mean, attention_square, attention_grad
    )
    router_mean_next, router_square_next, router_update = adam_step(
        router, router_mean, router_square, router_grad
    )
    gains_mean_next, gains_square_next, gains_update = adam_step(
        norm_gains, gains_mean, gains_square, gains_grad
    )
    upward_mean_next, upward_square_next, upward_update = adam_step(
        expert_up, upward_mean, upward_square, upward_grad
    )
    downward_mean_next, downward_square_next, downward_update = adam_step(
        expert_down, downward_mean, downward_square, downward_grad
    )
    table_mean_next, table_square_next, table_update = adam_step(
        output_table, table_mean, table_square, table_grad
    )
    return (
        loss_value,
        embedding_mean_next,
        embedding_square_next,
        embedding_update,
        attention_mean_next,
        attention_square_next,
        attention_update,
        router_mean_next,
        router_square_next,
        router_update,
        gains_mean_next,
        gains_square_next,
        gains_update,
        upward_mean_next,
        upward_square_next,
        upward_update,
        downward_mean_next,
        downward_square_next,
        downward_update,
        table_mean_next,
        table_square_next,
        table_update,
    )


def solution(mesh):
    expert_count, shard_count = mesh.devices.shape
    mesh = Mesh(
        mesh.devices.reshape(PLANES, expert_count // PLANES, shard_count // 4, 2, 2), AXES
    )
    return jax.shard_map(
        shards,
        mesh=mesh,
        in_specs=(
            P(),
            P(AXES),
            P(AXES, None),
            P(AXES),
            P(),
            P(),
            P(None, AXES),
            P(None, AXES),
            P(None, AXES),
            P(None, AXES, None),
            P(None, AXES, None),
            P(None, AXES, None),
            P(None, AXES, None),
            P(None, AXES, None),
            P(None, AXES, None),
            P(None, AXES),
            P(None, AXES),
            P(None, AXES),
            P(("z", "x"), None, ("h", "y", "c"), None),
            P(("z", "x"), None, ("h", "y", "c"), None),
            P(("z", "x"), None, ("h", "y", "c"), None),
            P(("z", "x"), None, None, ("h", "y", "c")),
            P(("z", "x"), None, None, ("h", "y", "c")),
            P(("z", "x"), None, None, ("h", "y", "c")),
            P(AXES, None),
            P(AXES, None),
            P(AXES, None),
        ),
        out_specs=(
            P(),
            P(None, AXES),
            P(None, AXES),
            P(None, AXES),
            P(None, AXES, None),
            P(None, AXES, None),
            P(None, AXES, None),
            P(None, AXES, None),
            P(None, AXES, None),
            P(None, AXES, None),
            P(None, AXES),
            P(None, AXES),
            P(None, AXES),
            P(("z", "x"), None, ("h", "y", "c"), None),
            P(("z", "x"), None, ("h", "y", "c"), None),
            P(("z", "x"), None, ("h", "y", "c"), None),
            P(("z", "x"), None, None, ("h", "y", "c")),
            P(("z", "x"), None, None, ("h", "y", "c")),
            P(("z", "x"), None, None, ("h", "y", "c")),
            P(AXES, None),
            P(AXES, None),
            P(AXES, None),
        ),
        check_vma=False,
    )
```

```python
import functools

import jax
import jax.numpy as jnp
from jax import lax
from jax.experimental import pallas as pl
from jax.experimental.pallas import tpu as pltpu
from jax.sharding import Mesh, PartitionSpec as P

D = 1024
HEADS = 16
HDIM = 64
F = 512
TOPK = 4
ADAM_STEP = 10


EPS_NORM = 1e-05
BETA_ONE = 0.9
BETA_TWO = 0.95
ADAM_EPS = 1e-08
LEARN_RATE = 0.01
DECAY_RATE = 0.1
ROPE_BASE = 10000.0
MASK_FILL = -1e30


AXES = ("z", "x", "h", "y", "c")
PLANES = 4
SHIFTS = (0, 2, 1, 3)
LANES = 128
CHUNKS = D // LANES


def dot_nn(left, right):
    return lax.dot_general(
        left, right, (((1,), (0,)), ((), ())), preferred_element_type=jnp.float32
    )


def dot_nt(left, right):
    return lax.dot_general(
        left, right, (((1,), (1,)), ((), ())), preferred_element_type=jnp.float32
    )


def dot_tn(left, right):
    return lax.dot_general(
        left, right, (((0,), (0,)), ((), ())), preferred_element_type=jnp.float32
    )


def inverse_root(values):
    return lax.rsqrt(jnp.mean(values * values, axis=-1, keepdims=True) + EPS_NORM)


def two_terms(values):
    high = values.astype(jnp.bfloat16)
    return high, (values - high.astype(jnp.float32)).astype(jnp.bfloat16)


def chunk(values, place):
    return values[:, place * LANES : (place + 1) * LANES]


def half_turn(values):
    lane = lax.broadcasted_iota(jnp.int32, values.shape, 1)
    ahead = pltpu.roll(values, LANES - HDIM // 2, 1)
    behind = pltpu.roll(values, HDIM // 2, 1)
    return jnp.where(lane % HDIM < HDIM // 2, ahead, behind)


def slot_gates(spread, gates, capacity):
    high, rest = two_terms(gates)
    full = dot_nn(spread, high) + dot_nn(spread, rest)
    expert = lax.broadcasted_iota(jnp.int32, full.shape, 0) // capacity
    lane = lax.broadcasted_iota(jnp.int32, full.shape, 1)
    return jnp.sum(jnp.where(lane == expert, full, 0.0), axis=1, keepdims=True)


def combine(middle, spread, spread_back, gates, returned, capacity):
    weighted = slot_gates(spread, gates, capacity) * returned.astype(jnp.float32)
    high, rest = two_terms(weighted)
    return middle + (dot_nn(spread_back, high) + dot_nn(spread_back, rest))


def masked_probs(query, key, visible):
    scores = dot_nt(query, key) * HDIM ** (-0.5)
    scores = jnp.where(visible, scores, MASK_FILL)
    weights = jnp.exp(scores - jnp.max(scores, axis=-1, keepdims=True))
    return weights / jnp.sum(weights, axis=-1, keepdims=True)


def visible_keys(prefix_ref, seq_len):
    query_place = lax.broadcasted_iota(jnp.int32, (seq_len, seq_len), 0)
    key_place = lax.broadcasted_iota(jnp.int32, (seq_len, seq_len), 1)
    return (key_place <= query_place) | (key_place < prefix_ref[0])


def head_masks(seq_len):
    lane = lax.broadcasted_iota(jnp.int32, (seq_len, LANES), 1)
    return lane < HDIM, lane >= HDIM


def fetch_weights(weight_ref, held_ref, copy_sem, layer_index, order):
    copies = {}
    for part in order:
        copies[part] = pltpu.make_async_copy(
            weight_ref.at[layer_index, :, pl.ds(part * D, D)], held_ref.at[part], copy_sem.at[part]
        )
        copies[part].start()
    return copies


def forward_kernel(
    layer_index,
    capacity,
    expert_count,
    prefix_ref,
    hidden_ref,
    *refs,
):
    if layer_index > 0:
        gates_in_ref, returned_ref, refs = refs[0], refs[1], refs[2:]
    (
        weight_ref,
        gain_ref,
        turn_ref,
        router_ref,
        kept_ref,
        spread_ref,
        spread_back_ref,
        hidden_out_ref,
        projected_ref,
        query_ref,
        key_ref,
        value_ref,
        attended_ref,
        middle_ref,
        ffn_ref,
        probs_ref,
        gates_ref,
        outgoing_ref,
        held_ref,
        copy_sem,
    ) = refs
    copies = fetch_weights(weight_ref, held_ref, copy_sem, layer_index, (0, 1, 2, 3))
    seq_len = hidden_ref.shape[0]
    hidden = hidden_ref[...]
    if layer_index > 0:
        hidden = combine(
            hidden,
            spread_ref[...],
            spread_back_ref[...],
            gates_in_ref[...],
            returned_ref[...],
            capacity,
        )
    hidden_out_ref[...] = hidden
    row = 4 * layer_index
    normed = (hidden * inverse_root(hidden) * gain_ref[row : row + 1, :]).astype(jnp.bfloat16)
    cosines, sines = turn_ref[0], turn_ref[1]
    for part, out_ref in ((0, query_ref), (1, key_ref)):
        columns = slice(part * D, (part + 1) * D)
        copies[part].wait()
        projected = dot_nn(normed, held_ref[part])
        projected_ref[:, columns] = projected
        scaled = projected * inverse_root(projected) * gain_ref[row + 1 + part : row + 2 + part, :]
        for place in range(CHUNKS):
            block = chunk(scaled, place)
            out_ref[:, place * LANES : (place + 1) * LANES] = (
                block * cosines + half_turn(block) * sines
            ).astype(jnp.bfloat16)
    copies[2].wait()
    value_ref[...] = dot_nn(normed, held_ref[2]).astype(jnp.bfloat16)
    visible = visible_keys(prefix_ref, seq_len)
    masks = head_masks(seq_len)
    zero = jnp.zeros((), jnp.bfloat16)
    for place in range(CHUNKS):
        columns = slice(place * LANES, (place + 1) * LANES)
        query, key, value = query_ref[:, columns], key_ref[:, columns], value_ref[:, columns]
        total = None
        for mask in masks:
            probs = masked_probs(query, jnp.where(mask, key, zero), visible).astype(jnp.bfloat16)
            term = dot_nn(probs, jnp.where(mask, value, zero))
            total = term if total is None else total + term
        attended_ref[:, columns] = total.astype(jnp.bfloat16)
    copies[3].wait()
    middle = hidden + dot_nn(attended_ref[...], held_ref[3])
    middle_ref[...] = middle
    ffn = (middle * inverse_root(middle) * gain_ref[row + 3 : row + 4, :]).astype(jnp.bfloat16)
    ffn_ref[...] = ffn
    outgoing_ref[...] = dot_nn(spread_ref[...], ffn).astype(jnp.bfloat16)
    logits = dot_nn(ffn, router_ref[layer_index])
    lane = lax.broadcasted_iota(jnp.int32, logits.shape, 1)
    logits = jnp.where(lane < expert_count, logits, MASK_FILL)
    weights = jnp.exp(logits - jnp.max(logits, axis=-1, keepdims=True))
    probs = weights / jnp.sum(weights, axis=-1, keepdims=True)
    probs_ref[...] = probs
    gates_ref[...] = probs * kept_ref[...]


def forward_layer(
    layer_index,
    capacity,
    expert_count,
    prefix,
    hidden,
    extra,
    weights,
    gains,
    turns,
    router,
    kept,
    spread,
    spread_back,
):
    seq_len = hidden.shape[0]
    whole = pl.BlockSpec(memory_space=pltpu.VMEM)
    wide = jax.ShapeDtypeStruct((seq_len, D), jnp.float32)
    low = jax.ShapeDtypeStruct((seq_len, D), jnp.bfloat16)
    small = jax.ShapeDtypeStruct((seq_len, LANES), jnp.float32)
    return pl.pallas_call(
        functools.partial(forward_kernel, layer_index, capacity, expert_count),
        out_shape=(
            wide,
            jax.ShapeDtypeStruct((seq_len, 2 * D), jnp.float32),
            low,
            low,
            low,
            low,
            wide,
            low,
            small,
            small,
            jax.ShapeDtypeStruct((spread.shape[0], D), jnp.bfloat16),
        ),
        in_specs=[pl.BlockSpec(memory_space=pltpu.SMEM), whole]
        + [whole] * len(extra)
        + [pl.BlockSpec(memory_space=pl.ANY)]
        + [whole] * 6,
        out_specs=[whole] * 11,
        scratch_shapes=[
            pltpu.VMEM((4, D, D), jnp.bfloat16),
            pltpu.SemaphoreType.DMA((4,)),
        ],
        compiler_params=pltpu.CompilerParams(vmem_limit_bytes=60 * 1024 * 1024),
        cost_estimate=pl.CostEstimate(
            flops=4 * seq_len * D * D * 3, bytes_accessed=24 * 1024 * 1024, transcendentals=1 << 20
        ),
    )(prefix, hidden, *extra, weights, gains, turns, router, kept, spread, spread_back)


def norm_pull(values, gain, upstream):
    root = inverse_root(values)
    scaled = values * root
    weighted = upstream * gain
    mean = jnp.mean(weighted * scaled, axis=-1, keepdims=True)
    return root * (weighted - scaled * mean), jnp.sum(upstream * scaled, axis=0, keepdims=True)


def backward_kernel(
    layer_index,
    capacity,
    prefix_ref,
    grad_ref,
    back_ref,
    logit_ref,
    hidden_ref,
    projected_ref,
    query_ref,
    key_ref,
    value_ref,
    attended_ref,
    middle_ref,
    weight_ref,
    gain_ref,
    turn_ref,
    router_ref,
    spread_back_ref,
    *refs,
):
    if layer_index > 0:
        spread_ref, gates_ref, refs = refs[0], refs[1], refs[2:]
        outgoing_ref, refs = refs[3], refs[:3] + refs[4:]
    grad_out_ref, weight_grad_ref, gain_grad_ref, pull_ref, key_pull_ref, held_ref, copy_sem = refs
    copies = fetch_weights(weight_ref, held_ref, copy_sem, layer_index, (3, 2, 0, 1))
    seq_len = hidden_ref.shape[0]
    row = 4 * layer_index
    ffn_grad = dot_nn(spread_back_ref[...], back_ref[...]) + dot_nt(
        logit_ref[...], router_ref[layer_index]
    )
    middle_grad, gain_three = norm_pull(
        middle_ref[...], gain_ref[row + 3 : row + 4, :], ffn_grad
    )
    grad_middle = grad_ref[...] + middle_grad
    grad_out_ref[...] = grad_middle
    branch = grad_middle.astype(jnp.bfloat16)
    weight_grad_ref[:, 3 * D :] = dot_tn(attended_ref[...], branch).astype(jnp.bfloat16)
    copies[3].wait()
    pull_ref[...] = dot_nt(branch, held_ref[3]).astype(jnp.bfloat16)
    visible = visible_keys(prefix_ref, seq_len)
    masks = head_masks(seq_len)
    zero = jnp.zeros((), jnp.bfloat16)
    cosines, sines = turn_ref[0], turn_ref[1]
    factor = HDIM ** (-0.5)
    hidden = hidden_ref[...]
    normed = (hidden * inverse_root(hidden) * gain_ref[row : row + 1, :]).astype(jnp.bfloat16)
    for place in range(CHUNKS):
        columns = slice(place * LANES, (place + 1) * LANES)
        query, key, value = query_ref[:, columns], key_ref[:, columns], value_ref[:, columns]
        pull = pull_ref[:, columns]
        totals = [None, None, None]
        for mask in masks:
            key_half = jnp.where(mask, key, zero)
            probs = masked_probs(query, key_half, visible)
            pulled = dot_nt(pull, jnp.where(mask, value, zero))
            inner = jnp.sum(probs * pulled, axis=-1, keepdims=True)
            score_grad = (probs * (pulled - inner)).astype(jnp.bfloat16)
            terms = (
                dot_nn(score_grad, key_half),
                dot_tn(score_grad, jnp.where(mask, query, zero)),
                dot_tn(probs.astype(jnp.bfloat16), jnp.where(mask, pull, zero)),
            )
            totals = [b if a is None else a + b for a, b in zip(totals, terms)]
        for part, target_ref in ((0, key_pull_ref.at[0]), (1, key_pull_ref.at[1])):
            turned = (totals[part] * factor).astype(jnp.bfloat16).astype(jnp.float32)
            target_ref[:, columns] = turned * cosines - half_turn(turned) * sines
        pull_ref[:, columns] = totals[2].astype(jnp.bfloat16)
    gain_rows = []
    value_pull = pull_ref[...]
    copies[2].wait()
    back = dot_nt(value_pull, held_ref[2])
    weight_grad_ref[:, 2 * D : 3 * D] = dot_tn(normed, value_pull).astype(jnp.bfloat16)
    for part in range(2):
        columns = slice(part * D, (part + 1) * D)
        input_pull, gain_row = norm_pull(
            projected_ref[:, columns],
            gain_ref[row + 1 + part : row + 2 + part, :],
            key_pull_ref[part],
        )
        gain_rows.append(gain_row)
        low_pull = input_pull.astype(jnp.bfloat16)
        weight_grad_ref[:, columns] = dot_tn(normed, low_pull).astype(jnp.bfloat16)
        copies[part].wait()
        back = back + dot_nt(low_pull, held_ref[part])
    hidden_grad, gain_zero = norm_pull(hidden, gain_ref[row : row + 1, :], back)
    grad_out = grad_out_ref[...] + hidden_grad
    grad_out_ref[...] = grad_out
    if layer_index > 0:
        outgoing_ref[...] = outgoing_pull(grad_out, spread_ref[...], gates_ref[...], capacity)
    gain_grad_ref[...] = jnp.concatenate(
        [gain_zero] + gain_rows + [gain_three, jnp.zeros((4, D), jnp.float32)], axis=0
    )


def backward_layer(
    layer_index,
    capacity,
    prefix,
    grad,
    back_inputs,
    logit_low,
    hidden,
    projected,
    queries,
    keys,
    values,
    attended,
    middle,
    weights,
    gains,
    turns,
    router,
    spread_back,
    extra,
):
    seq_len = hidden.shape[0]
    whole = pl.BlockSpec(memory_space=pltpu.VMEM)
    out_shape = [
        jax.ShapeDtypeStruct((seq_len, D), jnp.float32),
        jax.ShapeDtypeStruct((D, 4 * D), jnp.bfloat16),
        jax.ShapeDtypeStruct((8, D), jnp.float32),
    ]
    if layer_index > 0:
        out_shape.append(jax.ShapeDtypeStruct((spread_back.shape[1], D), jnp.bfloat16))
    return pl.pallas_call(
        functools.partial(backward_kernel, layer_index, capacity),
        out_shape=out_shape,
        in_specs=[pl.BlockSpec(memory_space=pltpu.SMEM)]
        + [whole] * 10
        + [pl.BlockSpec(memory_space=pl.ANY)]
        + [whole] * (4 + len(extra)),
        out_specs=[whole] * len(out_shape),
        scratch_shapes=[
            pltpu.VMEM((seq_len, D), jnp.bfloat16),
            pltpu.VMEM((2, seq_len, D), jnp.float32),
            pltpu.VMEM((4, D, D), jnp.bfloat16),
            pltpu.SemaphoreType.DMA((4,)),
        ],
        compiler_params=pltpu.CompilerParams(vmem_limit_bytes=60 * 1024 * 1024),
        cost_estimate=pl.CostEstimate(
            flops=8 * seq_len * D * D * 3, bytes_accessed=32 * 1024 * 1024, transcendentals=1 << 20
        ),
    )(
        prefix,
        grad,
        back_inputs,
        logit_low,
        hidden,
        projected,
        queries,
        keys,
        values,
        attended,
        middle,
        weights,
        gains,
        turns,
        router,
        spread_back,
        *extra,
    )


def turn_tables(seq_len):
    position = jnp.arange(seq_len, dtype=jnp.float32)[:, None]
    frequency = ROPE_BASE ** (-jnp.arange(HDIM // 2, dtype=jnp.float32) * 2.0 / HDIM)
    angles = position * frequency[None, :]
    cosines, sines = jnp.cos(angles), jnp.sin(angles)
    return jnp.stack(
        [
            jnp.concatenate([cosines] * 4, axis=1),
            jnp.concatenate([-sines, sines, -sines, sines], axis=1),
        ]
    )


def silu_parts(gate_up):
    gate_part, up_part = gate_up[:, :F], gate_up[:, F:]
    sigmoid = 1.0 / (1.0 + jnp.exp(-gate_part))
    return gate_part, up_part, sigmoid


def fetch_expert(places, part_refs, up_ref, down_ref, copy_sem):
    copies = []
    rows = part_refs[0].shape[0]
    for turn, part_ref in enumerate(part_refs):
        place = pl.multiple_of(places[turn] * rows, rows)
        copies.append(
            pltpu.make_async_copy(
                part_ref.at[:, pl.ds(0, 2 * F)],
                up_ref.at[pl.ds(place, rows), :],
                copy_sem.at[len(copies)],
            )
        )
        for block in range(F // rows):
            copies.append(
                pltpu.make_async_copy(
                    part_ref.at[:, pl.ds(2 * F + block * rows, rows)],
                    down_ref.at[pl.ds(block * rows, rows), pl.ds(place, rows)],
                    copy_sem.at[len(copies)],
                )
            )
    for copy in copies:
        copy.start()
    for copy in copies:
        copy.wait()


def expert_kernel(part_count, row_block, place_ref, received_ref, *refs):
    part_refs, (produced_ref, up_ref, down_ref, copy_sem) = refs[:part_count], refs[part_count:]
    fetch_expert(place_ref, part_refs, up_ref, down_ref, copy_sem)

    @pl.loop(0, received_ref.shape[0] // row_block)
    def _(step):
        rows = pl.ds(pl.multiple_of(step * row_block, row_block), row_block)
        gate_part, up_part, sigmoid = silu_parts(dot_nn(received_ref[rows, :], up_ref[...]))
        activated = (gate_part * sigmoid * up_part).astype(jnp.bfloat16)
        produced_ref[rows, :] = dot_nn(activated, down_ref[...]).astype(jnp.bfloat16)


def expert_specs(parts):
    rows = parts[0].shape[0]
    whole = pl.BlockSpec(memory_space=pltpu.VMEM)
    specs = [pl.BlockSpec(memory_space=pltpu.SMEM)]
    apart = [pl.BlockSpec(memory_space=pl.ANY)] * len(parts)
    scratch = [
        pltpu.VMEM((D, 2 * F), jnp.bfloat16),
        pltpu.VMEM((F, D), jnp.bfloat16),
        pltpu.SemaphoreType.DMA((len(parts) * (1 + F // rows),)),
    ]
    return whole, specs, apart, scratch


def run_expert(places, received, parts):
    whole, specs, apart, scratch = expert_specs(parts)
    slot_total = received.shape[0]
    return pl.pallas_call(
        functools.partial(expert_kernel, len(parts), slot_total // 4),
        out_shape=jax.ShapeDtypeStruct((slot_total, D), jnp.bfloat16),
        in_specs=specs + [whole] + apart,
        out_specs=whole,
        scratch_shapes=scratch,
        compiler_params=pltpu.CompilerParams(vmem_limit_bytes=56 * 1024 * 1024),
        cost_estimate=pl.CostEstimate(
            flops=slot_total * D * F * 6, bytes_accessed=8 * 1024 * 1024, transcendentals=1 << 19
        ),
    )(places, received, *parts)


def expert_back_kernel(part_count, row_block, place_ref, received_ref, pull_ref, *refs):
    part_refs, refs = refs[:part_count], refs[part_count:]
    input_grad_ref, gate_grad_ref, activated_ref, up_ref, down_ref, copy_sem = refs
    fetch_expert(place_ref, part_refs, up_ref, down_ref, copy_sem)

    @pl.loop(0, received_ref.shape[0] // row_block)
    def _(step):
        rows = pl.ds(pl.multiple_of(step * row_block, row_block), row_block)
        gate_part, up_part, sigmoid = silu_parts(dot_nn(received_ref[rows, :], up_ref[...]))
        side = gate_part * sigmoid
        activated_ref[rows, :] = (side * up_part).astype(jnp.bfloat16)
        pulled = dot_nt(pull_ref[rows, :], down_ref[...]).astype(jnp.bfloat16)
        pulled = pulled.astype(jnp.float32)
        gate_side = pulled * up_part * sigmoid * (1.0 + gate_part * (1.0 - sigmoid))
        gate_grad_ref[rows, :F] = gate_side.astype(jnp.bfloat16)
        gate_grad_ref[rows, F:] = (pulled * side).astype(jnp.bfloat16)
        input_grad_ref[rows, :] = dot_nt(gate_grad_ref[rows, :], up_ref[...]).astype(jnp.bfloat16)


def run_expert_back(places, received, pull, parts):
    whole, specs, apart, scratch = expert_specs(parts)
    slot_total = received.shape[0]
    return pl.pallas_call(
        functools.partial(expert_back_kernel, len(parts), slot_total // 4),
        out_shape=(
            jax.ShapeDtypeStruct((slot_total, D), jnp.bfloat16),
            jax.ShapeDtypeStruct((slot_total, 2 * F), jnp.bfloat16),
            jax.ShapeDtypeStruct((slot_total, F), jnp.bfloat16),
        ),
        in_specs=specs + [whole] * 2 + apart,
        out_specs=[whole] * 3,
        scratch_shapes=scratch,
        compiler_params=pltpu.CompilerParams(vmem_limit_bytes=56 * 1024 * 1024),
        cost_estimate=pl.CostEstimate(
            flops=slot_total * D * F * 12, bytes_accessed=12 * 1024 * 1024, transcendentals=1 << 19
        ),
    )(places, received, pull, *parts)


def expert_grad_kernel(
    part_count, place_ref, received_ref, pull_ref, gate_grad_ref, activated_ref, *refs
):
    out_refs, (up_ref, down_ref) = refs[:part_count], refs[part_count:]
    block = 256

    @pl.loop(0, D // block)
    def _(step):
        columns = pl.ds(pl.multiple_of(step * block, block), block)
        up_ref[columns, :] = dot_tn(received_ref[:, columns], gate_grad_ref[...]).astype(
            jnp.bfloat16
        )

    @pl.loop(0, F // block)
    def _(step):
        columns = pl.ds(pl.multiple_of(step * block, block), block)
        down_ref[columns, :] = dot_tn(activated_ref[:, columns], pull_ref[...]).astype(
            jnp.bfloat16
        )

    rows = out_refs[0].shape[0]
    for turn, out_ref in enumerate(out_refs):
        place = pl.multiple_of(place_ref[turn] * rows, rows)
        out_ref[:, : 2 * F] = up_ref[pl.ds(place, rows), :]
        for part in range(F // rows):
            out_ref[:, 2 * F + part * rows : 2 * F + (part + 1) * rows] = down_ref[
                part * rows : (part + 1) * rows, pl.ds(place, rows)
            ]


def run_expert_grad(places, received, pull, gate_grad, activated, piece_rows):
    whole = pl.BlockSpec(memory_space=pltpu.VMEM)
    part_count = D // piece_rows
    slot_total = received.shape[0]
    return pl.pallas_call(
        functools.partial(expert_grad_kernel, part_count),
        out_shape=[jax.ShapeDtypeStruct((piece_rows, 3 * F), jnp.bfloat16)] * part_count,
        in_specs=[pl.BlockSpec(memory_space=pltpu.SMEM)] + [whole] * 4,
        out_specs=[whole] * part_count,
        scratch_shapes=[
            pltpu.VMEM((D, 2 * F), jnp.bfloat16),
            pltpu.VMEM((F, D), jnp.bfloat16),
        ],
        compiler_params=pltpu.CompilerParams(vmem_limit_bytes=56 * 1024 * 1024),
        cost_estimate=pl.CostEstimate(
            flops=slot_total * D * F * 6, bytes_accessed=12 * 1024 * 1024, transcendentals=0
        ),
    )(places, received, pull, gate_grad, activated)


def outgoing_pull(grad, spread, gates, capacity):
    high, rest = two_terms(grad)
    wide = dot_nn(spread, high) + dot_nn(spread, rest)
    return (slot_gates(spread, gates, capacity) * wide).astype(jnp.bfloat16)


def first_pull_kernel(
    capacity,
    gain_row,
    position_count,
    picked_ref,
    got_ref,
    own_ref,
    rows_ref,
    gain_ref,
    spread_ref,
    gates_ref,
    grad_ref,
    out_ref,
    gain_grad_ref,
    stat_ref,
):
    stats = got_ref[:, :, 2 * D :].astype(jnp.float32)

    def joined(place):
        return sum(stats[:, :, place + term : place + term + 1] for term in range(3))

    peaks, sums, dots = joined(0), joined(3), joined(6)
    peak = jnp.max(peaks, axis=0)
    log_norm = peak + jnp.log(jnp.sum(sums * jnp.exp(peaks - peak[None]), axis=0))
    mass, entropy = own_ref[:, 0:1], own_ref[:, 1:2]
    loss = (1.0 + mass) * log_norm - jnp.sum(dots, axis=0) + entropy
    scale = (1.0 + mass)[None] * jnp.exp(peaks - log_norm[None])
    total = jnp.zeros(rows_ref.shape, jnp.float32)
    for device in range(got_ref.shape[0]):
        total += scale[device] * got_ref[device, :, :D].astype(jnp.float32)
        total -= got_ref[device, :, D : 2 * D].astype(jnp.float32)
    rows_grad, gain_grad = norm_pull(
        rows_ref[...], gain_ref[gain_row : gain_row + 1, :], total / position_count
    )
    gain_grad_ref[...] = gain_grad
    lane = lax.broadcasted_iota(jnp.int32, stat_ref.shape, 1)
    stat_ref[...] = jnp.where(lane == 0, log_norm, jnp.where(lane == 1, loss, 0.0))
    grad_ref[...] = jnp.zeros_like(grad_ref)
    for place in range(rows_ref.shape[0]):
        grad_ref[pl.ds(picked_ref[place], 1), :] = rows_grad[place : place + 1, :]
    out_ref[...] = outgoing_pull(grad_ref[...], spread_ref[...], gates_ref[...], capacity)


def first_pull(capacity, gain_row, position_count, picked, got, own, rows, gains, spread, gates):
    whole = pl.BlockSpec(memory_space=pltpu.VMEM)
    return pl.pallas_call(
        functools.partial(first_pull_kernel, capacity, gain_row, position_count),
        out_shape=(
            jax.ShapeDtypeStruct((spread.shape[1], D), jnp.float32),
            jax.ShapeDtypeStruct((spread.shape[0], D), jnp.bfloat16),
            jax.ShapeDtypeStruct((1, D), jnp.float32),
            jax.ShapeDtypeStruct(own.shape, jnp.float32),
        ),
        in_specs=[pl.BlockSpec(memory_space=pltpu.SMEM)] + [whole] * 6,
        out_specs=[whole] * 4,
        compiler_params=pltpu.CompilerParams(vmem_limit_bytes=48 * 1024 * 1024),
        cost_estimate=pl.CostEstimate(
            flops=4 * spread.shape[0] * spread.shape[1] * D,
            bytes_accessed=6 * 1024 * 1024,
            transcendentals=0,
        ),
    )(picked, got, own, rows, gains, spread, gates)


def router_kernel(
    capacity, grad_ref, returned_ref, spread_back_ref, probs_ref, ffn_ref, low_ref, router_grad_ref
):
    high, rest = two_terms(grad_ref[...])
    dots = dot_nt(high, returned_ref[...]) + dot_nt(rest, returned_ref[...])
    dots = dots * spread_back_ref[...].astype(jnp.float32)
    slot_total = returned_ref.shape[0]
    slot = lax.broadcasted_iota(jnp.int32, (slot_total, LANES), 0) // capacity
    lane = lax.broadcasted_iota(jnp.int32, (slot_total, LANES), 1)
    owner = jnp.where(slot == lane, 1.0, 0.0).astype(jnp.bfloat16)
    high, rest = two_terms(dots)
    pull = dot_nn(high, owner) + dot_nn(rest, owner)
    probs = probs_ref[...]
    low = (probs * (pull - jnp.sum(probs * pull, axis=-1, keepdims=True))).astype(jnp.bfloat16)
    low_ref[...] = low
    router_grad_ref[...] = dot_tn(ffn_ref[...], low)


def router_back(capacity, grad, returned, spread_back, probs, ffn):
    whole = pl.BlockSpec(memory_space=pltpu.VMEM)
    seq_len = grad.shape[0]
    return pl.pallas_call(
        functools.partial(router_kernel, capacity),
        out_shape=(
            jax.ShapeDtypeStruct((seq_len, LANES), jnp.bfloat16),
            jax.ShapeDtypeStruct((D, LANES), jnp.float32),
        ),
        in_specs=[whole] * 5,
        out_specs=[whole] * 2,
        compiler_params=pltpu.CompilerParams(vmem_limit_bytes=48 * 1024 * 1024),
        cost_estimate=pl.CostEstimate(
            flops=4 * seq_len * returned.shape[0] * D,
            bytes_accessed=6 * 1024 * 1024,
            transcendentals=0,
        ),
    )(grad, returned, spread_back, probs, ffn)


def final_kernel(
    capacity,
    gain_row,
    picked_ref,
    middle_ref,
    gates_ref,
    returned_ref,
    spread_ref,
    spread_back_ref,
    gain_ref,
    rows_ref,
    low_ref,
):
    count = rows_ref.shape[0]
    for place in range(count):
        rows_ref[place : place + 1, :] = middle_ref[pl.ds(picked_ref[place], 1), :]
    sublane = lax.broadcasted_iota(jnp.int32, (count, LANES), 0)
    wanted = jnp.zeros((count, LANES), jnp.int32)
    for place in range(count):
        wanted = jnp.where(sublane == place, picked_ref[place], wanted)
    seq_len = middle_ref.shape[0]
    token = lax.broadcasted_iota(jnp.int32, (count, seq_len), 1)
    wanted = jnp.concatenate([wanted] * (seq_len // LANES), axis=1)
    chosen = jnp.where(token == wanted, 1.0, 0.0).astype(jnp.bfloat16)
    slots = dot_nn(chosen, spread_back_ref[...]).astype(jnp.bfloat16)
    weighted = slot_gates(spread_ref[...], gates_ref[...], capacity) * returned_ref[...].astype(
        jnp.float32
    )
    high, rest = two_terms(weighted)
    rows = rows_ref[...] + (dot_nn(slots, high) + dot_nn(slots, rest))
    rows_ref[...] = rows
    low_ref[...] = (rows * inverse_root(rows) * gain_ref[gain_row : gain_row + 1, :]).astype(
        jnp.bfloat16
    )


def final_rows_of(capacity, gain_row, picked, middle, gates, returned, spread, spread_back, gains):
    whole = pl.BlockSpec(memory_space=pltpu.VMEM)
    count = picked.shape[0]
    return pl.pallas_call(
        functools.partial(final_kernel, capacity, gain_row),
        out_shape=(
            jax.ShapeDtypeStruct((count, D), jnp.float32),
            jax.ShapeDtypeStruct((count, D), jnp.bfloat16),
        ),
        in_specs=[pl.BlockSpec(memory_space=pltpu.SMEM)] + [whole] * 6,
        out_specs=[whole] * 2,
        compiler_params=pltpu.CompilerParams(vmem_limit_bytes=48 * 1024 * 1024),
        cost_estimate=pl.CostEstimate(
            flops=1 << 28, bytes_accessed=5 * 1024 * 1024, transcendentals=0
        ),
    )(picked, middle, gates, returned, spread, spread_back, gains)


def tie(first, second):
    return lax.optimization_barrier((first, second))


def swap_pairs(row_groups, turn_plane, turn_row):
    pairs = []
    for plane in range(PLANES):
        for row in range(row_groups):
            for part in range(PLANES):
                source = (plane * row_groups + row) * PLANES + part
                target_plane = (plane + SHIFTS[part ^ turn_plane]) % PLANES
                target_row = (row + turn_row) % row_groups
                target_part = (plane // 2 + target_plane) % 2 * 2 + plane % 2
                pairs.append(
                    (source, (target_plane * row_groups + target_row) * PLANES + target_part)
                )
    return pairs


def all_turns(row_groups):
    return [(plane, row) for row in range(row_groups) for plane in range(PLANES)]


def shift_inverse(shift):
    return jnp.array(SHIFTS, jnp.int32)[shift]


def part_of_turn(turn_plane):
    me_plane = lax.axis_index("z")
    expert_plane = (lax.axis_index("y") + me_plane) % 2 * 2 + lax.axis_index("c")
    return shift_inverse((me_plane - expert_plane) % PLANES) ^ turn_plane


def piece_place(turn, row_groups):
    turn_plane, turn_row = turn
    row = (lax.axis_index("h") - turn_row) % row_groups
    return row * PLANES + part_of_turn(turn_plane)


def spread_experts(piece, row_groups):
    return [
        lax.ppermute(
            piece, ("z", "h", "y", "c"), swap_pairs(row_groups, turn_plane, turn_row)
        )
        for turn_plane, turn_row in all_turns(row_groups)
    ]


def return_expert_grads(pieces, row_groups, chosen=None):
    arrived = []
    for place, (piece, turn) in enumerate(zip(pieces, all_turns(row_groups))):
        if chosen is not None and place not in chosen:
            continue
        back = [(target, source) for source, target in swap_pairs(row_groups, *turn)]
        arrived.append(lax.ppermute(piece, ("z", "h", "y", "c"), back))
    return arrived


def scatter_sum(parts):
    total = parts[0].astype(jnp.float32)
    for part in parts[1:]:
        total = total + part.astype(jnp.float32)
    return total


def send_all(values):
    return lax.all_to_all(values, AXES, split_axis=0, concat_axis=0, tiled=True)


def send_plane(values):
    return lax.all_to_all(values, ("x", "y", "c"), split_axis=0, concat_axis=0, tiled=True)


def three_terms(values):
    first = lax.reduce_precision(values, 8, 7)
    second = lax.reduce_precision(values - first, 8, 7)
    third = lax.reduce_precision(values - first - second, 8, 7)
    return [first, second, third]

PLANE_RING = ("x", "y", "c")


def plane_partners():
    at = {name: lax.axis_index(name) for name in PLANE_RING}
    partners, groups = [None], [at["x"] * 4 + at["y"] * 2 + at["c"]]
    for turn in range(1, 8):
        flips = {"x": turn // 4, "y": turn // 2 % 2, "c": turn % 2}
        there = {name: 1 - at[name] if flips[name] else at[name] for name in PLANE_RING}
        partners.append({name: there[name] for name in PLANE_RING if flips[name]})
        groups.append(there["x"] * 4 + there["y"] * 2 + there["c"])
    return partners, groups


def part_places(part_count):
    plane = lax.axis_index("z")
    expert_plane = lax.rem(lax.axis_index("y") + plane, 2) * 2 + lax.axis_index("c")
    shift = lax.rem(plane - expert_plane + PLANES, PLANES)
    upper, lower = lax.rem(shift, 2), shift // 2
    places = []
    for turn in range(part_count):
        first = 1 - upper if turn // 2 else upper
        second = 1 - lower if turn % 2 else lower
        places.append(first * 2 + second)
    return places


def swap_routes():
    z, y, c = (lax.axis_index(name) for name in ("z", "y", "c"))
    expert_plane = lax.rem(y + z, 2) * 2 + c
    shift_in = lax.rem(z - expert_plane + PLANES, PLANES)
    routes = []
    for turn in range(PLANES):
        upper = 1 - y if turn // 2 else y
        lower = 1 - c if turn % 2 else c
        plane = lax.rem(z + lower * 2 + upper, PLANES)
        target = {"z": plane, "y": lax.rem(z // 2 + plane, 2), "c": lax.rem(z, 2)}
        first, second = lax.rem(shift_in, 2), shift_in // 2
        source = {
            "z": expert_plane,
            "y": 1 - first if turn // 2 else first,
            "c": 1 - second if turn % 2 else second,
        }
        own = (target["z"] == z) & (target["y"] == y) & (target["c"] == c)
        routes.append((target, source, own))
    return routes


def swap_copies(route, turn, held_ref, slot_ref, sems, backward):
    target, source, _ = route
    send_sem, recv_sem, local_sem = sems
    away = pltpu.make_async_remote_copy(
        src_ref=held_ref,
        dst_ref=slot_ref,
        send_sem=send_sem.at[turn],
        recv_sem=recv_sem.at[turn],
        device_id=source if backward else target,
        device_id_type=pl.DeviceIdType.MESH,
    )
    return away, pltpu.make_async_copy(held_ref, slot_ref, local_sem.at[turn])


def swap_start(routes, held_refs, slot_refs, sems, backward):
    for turn, route in enumerate(routes):
        away, stay = swap_copies(route, turn, held_refs[turn], slot_refs[turn], sems, backward)
        pl.when(jnp.logical_not(route[2]))(away.start)
        pl.when(route[2])(stay.start)


def swap_wait(routes, held_refs, slot_refs, sems, backward):
    for turn, route in enumerate(routes):
        away, stay = swap_copies(route, turn, held_refs[turn], slot_refs[turn], sems, backward)
        pl.when(jnp.logical_not(route[2]))(away.wait)
        pl.when(route[2])(stay.wait)


def greet(partners, routes=()):
    barrier = pltpu.get_barrier_semaphore()

    def hello(partner):
        pl.semaphore_signal(
            barrier, inc=1, device_id=partner, device_id_type=pl.DeviceIdType.MESH
        )

    for partner in partners:
        hello(partner)
    for target, source, own in routes:

        @pl.when(jnp.logical_not(own))
        def _(target=target, source=source):
            hello(target)
            hello(source)

    count = len(partners)
    for _, _, own in routes:
        count = count + jnp.where(own, 0, 2)
    pl.semaphore_wait(barrier, count)


def swap_scratch(count):
    return [pltpu.SemaphoreType.DMA((PLANES,))] * (3 * count)


def push(source, target, send_sem, recv_sem, place, partner):
    copy = pltpu.make_async_remote_copy(
        src_ref=source,
        dst_ref=target,
        send_sem=send_sem.at[place],
        recv_sem=recv_sem.at[place],
        device_id=partner,
        device_id_type=pl.DeviceIdType.MESH,
    )
    copy.start()
    return copy


FAR_FIRST = (6, 7, 4, 5, 2, 3, 1)


def exchange_out(outgoing_ref, received_ref, send_sem, recv_sem, partners, groups):
    copies = {}
    for turn in FAR_FIRST:
        copies[turn] = push(
            outgoing_ref.at[groups[turn]],
            received_ref.at[turn],
            send_sem,
            recv_sem,
            turn,
            partners[turn],
        )
    received_ref[0] = outgoing_ref[groups[0]]
    return copies


def flat_rows(block):
    return block.reshape(block.shape[0] * block.shape[1], block.shape[2])


def two_blocks(ref, pair):
    return flat_rows(ref[2 * pair : 2 * pair + 2])


def put_two(ref, pair, values):
    rows = values.shape[0] // 2
    ref[2 * pair] = values[:rows]
    ref[2 * pair + 1] = values[rows:]


def forward_exchange_kernel(spread_count, outgoing_ref, *refs):
    routes = ()
    if spread_count:
        routes = swap_routes()
        pieces, refs = refs[:spread_count], refs[spread_count:]
        returned_ref, received_ref = refs[:2]
        slots, refs = refs[2 : 2 + spread_count * PLANES], refs[2 + spread_count * PLANES :]
        sems, refs = refs[-3 * spread_count :], refs[: -3 * spread_count]
        swaps = [
            (
                routes,
                [piece] * PLANES,
                slots[place * PLANES : (place + 1) * PLANES],
                sems[3 * place : 3 * place + 3],
                False,
            )
            for place, piece in enumerate(pieces)
        ]
        part_refs = slots[:PLANES]
    else:
        part_refs, refs = refs[:PLANES], refs[PLANES:]
        returned_ref, received_ref = refs[:2]
        swaps, refs = [], refs[2:]
    up_ref, down_ref, produced_ref, copy_sem, send_sem, recv_sem = refs
    partners, groups = plane_partners()
    greet(partners[1:], routes)
    for swap in swaps[:1]:
        swap_start(*swap)
    copies = exchange_out(outgoing_ref, received_ref, send_sem, recv_sem, partners, groups)
    for swap in swaps[:1]:
        swap_wait(*swap)
    for swap in swaps[1:]:
        swap_start(*swap)
    fetch_expert(part_places(PLANES), part_refs, up_ref, down_ref, copy_sem)
    back = {}
    for pair in range(4):
        for turn in (2 * pair, 2 * pair + 1):
            if turn:
                copies[turn].wait_recv()
        gate_part, up_part, sigmoid = silu_parts(
            dot_nn(two_blocks(received_ref, pair), up_ref[...])
        )
        activated = (gate_part * sigmoid * up_part).astype(jnp.bfloat16)
        put_two(produced_ref, pair, dot_nn(activated, down_ref[...]).astype(jnp.bfloat16))
        for turn in (2 * pair, 2 * pair + 1):
            if turn:
                back[turn] = push(
                    produced_ref.at[turn],
                    returned_ref.at[groups[0]],
                    send_sem,
                    recv_sem,
                    8 + turn,
                    partners[turn],
                )
    returned_ref[groups[0]] = produced_ref[0]
    for turn in range(1, 8):
        copies[turn].wait_send()
        back[turn].wait()
    for swap in swaps[1:]:
        swap_wait(*swap)


def forward_exchange(outgoing, parts, pieces=()):
    whole = pl.BlockSpec(memory_space=pltpu.VMEM)
    apart = [pl.BlockSpec(memory_space=pl.ANY)]
    sources = list(pieces) if pieces else list(parts)
    rows = sources[0].shape[0]
    shape = jax.ShapeDtypeStruct(outgoing.shape, jnp.bfloat16)
    slot_total = outgoing.shape[0] * outgoing.shape[1]
    slots = [
        jax.ShapeDtypeStruct(piece.shape, piece.dtype) for piece in pieces for _ in range(PLANES)
    ]
    return pl.pallas_call(
        functools.partial(forward_exchange_kernel, len(pieces)),
        out_shape=[shape, shape] + slots,
        in_specs=[whole] + apart * len(sources),
        out_specs=[whole] * 2 + apart * len(slots),
        scratch_shapes=[
            pltpu.VMEM((D, 2 * F), jnp.bfloat16),
            pltpu.VMEM((F, D), jnp.bfloat16),
            pltpu.VMEM(outgoing.shape, jnp.bfloat16),
            pltpu.SemaphoreType.DMA((PLANES * (1 + F // rows),)),
            pltpu.SemaphoreType.DMA((16,)),
            pltpu.SemaphoreType.DMA((16,)),
        ]
        + swap_scratch(len(pieces)),
        compiler_params=pltpu.CompilerParams(
            vmem_limit_bytes=56 * 1024 * 1024,
            collective_id=5 if pieces else 2,
            has_side_effects=True,
        ),
        cost_estimate=pl.CostEstimate(
            flops=slot_total * D * F * 6, bytes_accessed=150 * 1024 * 1024, transcendentals=1 << 19
        ),
    )(outgoing, *sources)


def backward_exchange_kernel(
    part_count,
    capacity,
    outgoing_ref,
    received_ref,
    grad_ref,
    returned_ref,
    spread_back_ref,
    probs_ref,
    ffn_ref,
    *refs,
):
    part_refs, refs = refs[:part_count], refs[part_count:]
    out_refs, refs = refs[:part_count], refs[part_count:]
    (
        back_ref,
        low_ref,
        router_grad_ref,
        pull_ref,
        gate_grad_ref,
        activated_ref,
        input_grad_ref,
        up_ref,
        down_ref,
        up_grad_ref,
        down_grad_ref,
        copy_sem,
        send_sem,
        recv_sem,
    ) = refs
    partners, groups = plane_partners()
    greet(partners[1:])
    copies = exchange_out(outgoing_ref, pull_ref, send_sem, recv_sem, partners, groups)
    fetch_expert(part_places(part_count), part_refs, up_ref, down_ref, copy_sem)
    back = {}
    for pair in range(4):
        rows = slice(pair * 2 * capacity, (pair + 1) * 2 * capacity)
        gate_part, up_part, sigmoid = silu_parts(
            dot_nn(two_blocks(received_ref, pair), up_ref[...])
        )
        side = gate_part * sigmoid
        activated_ref[rows, :] = (side * up_part).astype(jnp.bfloat16)
        slope = up_part * sigmoid * (1.0 + gate_part * (1.0 - sigmoid))
        for turn in (2 * pair, 2 * pair + 1):
            if turn:
                copies[turn].wait_recv()
        pulled = dot_nt(two_blocks(pull_ref, pair), down_ref[...]).astype(jnp.bfloat16)
        pulled = pulled.astype(jnp.float32)
        gate_grad_ref[rows, :F] = (pulled * slope).astype(jnp.bfloat16)
        gate_grad_ref[rows, F:] = (pulled * side).astype(jnp.bfloat16)
        put_two(
            input_grad_ref, pair, dot_nt(gate_grad_ref[rows, :], up_ref[...]).astype(jnp.bfloat16)
        )
        for turn in (2 * pair, 2 * pair + 1):
            if turn:
                back[turn] = push(
                    input_grad_ref.at[turn],
                    back_ref.at[groups[0]],
                    send_sem,
                    recv_sem,
                    8 + turn,
                    partners[turn],
                )
        if pair == 0:
            router_kernel(
                capacity,
                grad_ref,
                returned_ref,
                spread_back_ref,
                probs_ref,
                ffn_ref,
                low_ref,
                router_grad_ref,
            )
    back_ref[groups[0]] = input_grad_ref[0]
    block = 256

    @pl.loop(0, D // block)
    def _(step):
        columns = pl.ds(pl.multiple_of(step * block, block), block)
        up_grad_ref[columns, :] = dot_tn(
            flat_rows(received_ref[:, :, columns]), gate_grad_ref[...]
        ).astype(jnp.bfloat16)

    @pl.loop(0, F // block)
    def _(step):
        columns = pl.ds(pl.multiple_of(step * block, block), block)
        down_grad_ref[columns, :] = dot_tn(
            activated_ref[:, columns], flat_rows(pull_ref[...])
        ).astype(jnp.bfloat16)

    rows = out_refs[0].shape[0]
    for out_ref, own_place in zip(out_refs, part_places(part_count)):
        place = pl.multiple_of(own_place * rows, rows)
        out_ref[:, : 2 * F] = up_grad_ref[pl.ds(place, rows), :]
        for part in range(F // rows):
            out_ref[:, 2 * F + part * rows : 2 * F + (part + 1) * rows] = down_grad_ref[
                part * rows : (part + 1) * rows, pl.ds(place, rows)
            ]
    for turn in range(1, 8):
        copies[turn].wait_send()
        back[turn].wait()


def backward_exchange(
    capacity, outgoing, received, grad, returned, spread_back, probs, ffn, parts
):
    whole, _, apart, scratch = expert_specs(parts)
    slot_total = outgoing.shape[0] * outgoing.shape[1]
    piece_rows = parts[0].shape[0]
    seq_len = grad.shape[0]
    low = jnp.bfloat16
    return pl.pallas_call(
        functools.partial(backward_exchange_kernel, len(parts), capacity),
        out_shape=[jax.ShapeDtypeStruct((piece_rows, 3 * F), low)] * len(parts)
        + [
            jax.ShapeDtypeStruct(outgoing.shape, low),
            jax.ShapeDtypeStruct((seq_len, LANES), low),
            jax.ShapeDtypeStruct((D, LANES), jnp.float32),
        ],
        in_specs=[whole] * 7 + apart,
        out_specs=[whole] * (len(parts) + 3),
        scratch_shapes=[
            pltpu.VMEM(outgoing.shape, low),
            pltpu.VMEM((slot_total, 2 * F), low),
            pltpu.VMEM((slot_total, F), low),
            pltpu.VMEM(outgoing.shape, low),
        ]
        + scratch[:2]
        + scratch[:2]
        + [
            scratch[2],
            pltpu.SemaphoreType.DMA((16,)),
            pltpu.SemaphoreType.DMA((16,)),
        ],
        compiler_params=pltpu.CompilerParams(
            vmem_limit_bytes=58 * 1024 * 1024, collective_id=3, has_side_effects=True
        ),
        cost_estimate=pl.CostEstimate(
            flops=slot_total * D * F * 18,
            bytes_accessed=180 * 1024 * 1024,
            transcendentals=1 << 19,
        ),
    )(outgoing, received, grad, returned, spread_back, probs, ffn, *parts)


RING = ("z", "x", "y", "c")


def owner_sum_kernel(
    layers,
    *refs,
):
    grads, refs = refs[:layers], refs[layers:]
    (
        out_ref,
        own_ref,
        core_ref,
        near_ref,
        joined_ref,
        turn_ref,
        last_ref,
        got_ref,
        local_sem,
        send_sem,
        recv_sem,
    ) = refs
    at = {name: lax.axis_index(name) for name in RING}
    planes = lax.axis_size("z")
    barrier = pltpu.get_barrier_semaphore()
    partners = [{name: 1 - at[name]} for name in ("c", "x", "y")]
    partners += [{"z": lax.rem(at["z"] + turn, planes)} for turn in range(1, planes)]
    for partner in partners:
        pl.semaphore_signal(
            barrier, inc=1, device_id=partner, device_id_type=pl.DeviceIdType.MESH
        )
    pl.semaphore_wait(barrier, len(partners))

    width = own_ref.shape[-1]
    half = width // 2
    per_layer = grads[0].shape[-1] // width
    chunk_count = layers * per_layer
    copies = {}

    def send(chunk_index, step, source, target, partner):
        place = chunk_index * 8 + step
        copy = pltpu.make_async_remote_copy(
            src_ref=source,
            dst_ref=target,
            send_sem=send_sem.at[place],
            recv_sem=recv_sem.at[place],
            device_id=partner,
            device_id_type=pl.DeviceIdType.MESH,
        )
        copy.start()
        copies[place] = copy

    def arrived(chunk_index, *steps):
        for step in steps:
            copies[chunk_index * 8 + step].wait()

    def source_of(chunk_index, core):
        layer, part = chunk_index // per_layer, chunk_index % per_layer
        return grads[layer].at[:, :, :, core, :, pl.ds(part * width, width)]

    def added(left, right):
        return (left.astype(jnp.float32) + right.astype(jnp.float32)).astype(jnp.bfloat16)

    local = []
    for index in range(chunk_count):
        copy = pltpu.make_async_copy(
            source_of(index, at["c"]), own_ref.at[index], local_sem.at[index]
        )
        copy.start()
        local.append(copy)
        send(index, 0, source_of(index, 1 - at["c"]), core_ref.at[index], partners[0])

    def stage_core(index):
        local[index].wait()
        arrived(index, 0)
        for plane in range(planes):
            own_ref[index, plane] = added(own_ref[index, plane], core_ref[index, plane])
        send(
            index,
            1,
            own_ref.at[index, :, 1 - at["x"], :, :, pl.ds(0, half)],
            near_ref.at[index, 0],
            partners[1],
        )
        send(
            index,
            2,
            own_ref.at[index, :, :, 1 - at["y"], :, pl.ds(half, half)],
            near_ref.at[index, 1],
            partners[2],
        )

    def stage_near(index):
        arrived(index, 1, 2)
        for plane in range(planes):
            for other in range(2):
                joined_ref[index, 0, plane, other] = added(
                    own_ref[index, plane, at["x"], other, :, :half],
                    near_ref[index, 0, plane, other],
                )
                joined_ref[index, 1, plane, other] = added(
                    own_ref[index, plane, other, at["y"], :, half:],
                    near_ref[index, 1, plane, other],
                )
        send(
            index,
            3,
            joined_ref.at[index, 0, :, 1 - at["y"]],
            turn_ref.at[index, 0],
            partners[2],
        )
        send(
            index,
            4,
            joined_ref.at[index, 1, :, 1 - at["x"]],
            turn_ref.at[index, 1],
            partners[1],
        )

    def stage_turn(index):
        arrived(index, 3, 4)
        for plane in range(planes):
            last_ref[index, plane, :, :half] = added(
                joined_ref[index, 0, plane, at["y"]], turn_ref[index, 0, plane]
            )
            last_ref[index, plane, :, half:] = added(
                joined_ref[index, 1, plane, at["x"]], turn_ref[index, 1, plane]
            )
        for turn in range(1, planes):
            send(
                index,
                4 + turn,
                last_ref.at[index, partners[2 + turn]["z"]],
                got_ref.at[index, turn - 1],
                partners[2 + turn],
            )

    def stage_planes(index):
        arrived(index, *[4 + turn for turn in range(1, planes)])
        total = last_ref[index, at["z"]].astype(jnp.float32)
        for turn in range(1, planes):
            total = total + got_ref[index, turn - 1].astype(jnp.float32)
        layer, part = index // per_layer, index % per_layer
        out_ref[layer, :, part * width : (part + 1) * width] = total

    stages = (stage_core, stage_near, stage_turn, stage_planes)
    for step in range(chunk_count + len(stages) - 1):
        for number, stage in enumerate(stages):
            if 0 <= step - number < chunk_count:
                stage(step - number)


def owner_sums(grads, width=2048):
    layers = len(grads)
    sizes = [lax.axis_size(name) for name in RING]
    rows, columns = grads[0].shape
    own_rows = rows // (sizes[0] * sizes[1] * sizes[2] * sizes[3])
    chunks = layers * columns // width
    blocks = [grad.reshape(*sizes, own_rows, columns) for grad in grads]
    half = width // 2
    low = jnp.bfloat16
    return pl.pallas_call(
        functools.partial(owner_sum_kernel, layers),
        out_shape=jax.ShapeDtypeStruct((layers, own_rows, columns), jnp.float32),
        in_specs=[pl.BlockSpec(memory_space=pl.ANY)] * layers,
        out_specs=pl.BlockSpec(memory_space=pltpu.VMEM),
        scratch_shapes=[
            pltpu.VMEM((chunks, sizes[0], 2, 2, own_rows, width), low),
            pltpu.VMEM((chunks, sizes[0], 2, 2, own_rows, width), low),
            pltpu.VMEM((chunks, 2, sizes[0], 2, own_rows, half), low),
            pltpu.VMEM((chunks, 2, sizes[0], 2, own_rows, half), low),
            pltpu.VMEM((chunks, 2, sizes[0], own_rows, half), low),
            pltpu.VMEM((chunks, sizes[0], own_rows, width), low),
            pltpu.VMEM((chunks, sizes[0] - 1, own_rows, width), low),
            pltpu.SemaphoreType.DMA((chunks,)),
            pltpu.SemaphoreType.DMA((chunks * 8,)),
            pltpu.SemaphoreType.DMA((chunks * 8,)),
        ],
        compiler_params=pltpu.CompilerParams(
            vmem_limit_bytes=56 * 1024 * 1024, collective_id=1, has_side_effects=True
        ),
        cost_estimate=pl.CostEstimate(
            flops=1 << 26, bytes_accessed=200 * 1024 * 1024, transcendentals=0
        ),
    )(*blocks)


def adam_step(weight, mean_old, square_old, gradient):
    mean_new = BETA_ONE * mean_old + (1.0 - BETA_ONE) * gradient
    square_new = BETA_TWO * square_old + (1.0 - BETA_TWO) * gradient * gradient
    bias_one = 1.0 - BETA_ONE**ADAM_STEP
    bias_two = 1.0 - BETA_TWO**ADAM_STEP
    update = -LEARN_RATE * (
        mean_new / bias_one / (jnp.sqrt(square_new / bias_two) + ADAM_EPS) + DECAY_RATE * weight
    )
    return (mean_new, square_new, update)


VOCAB_BLOCK = 2048
VOCAB_PART = 512


def embedding_kernel(
    row_ref,
    low_ref,
    high_ref,
    arrived_ref,
    word_ref,
    group_ref,
    weight_ref,
    mean_ref,
    square_ref,
    mean_out_ref,
    square_out_ref,
    update_ref,
    wide_ref,
    sorted_ref,
    turned_ref,
    total_ref,
):
    step = pl.program_id(0)
    device_count = arrived_ref.shape[0]
    token_count = sorted_ref.shape[0]
    columns = weight_ref.shape[0]
    groups = LANES // columns

    @pl.when(step == 0)
    def _():
        for part in range(wide_ref.shape[0] // device_count):
            wide_ref[part * device_count : (part + 1) * device_count, :] = arrived_ref[
                :, part * LANES : (part + 1) * LANES
            ].astype(jnp.float32)

        @pl.loop(0, token_count // 32)
        def _(block):
            start = pl.multiple_of(block * 32, 32)
            for place in range(32):
                sorted_ref[pl.ds(start + place, 1), :] = wide_ref[pl.ds(row_ref[start + place], 1), :]

        row_place = lax.broadcasted_iota(jnp.int32, (LANES, LANES), 0)
        lane = lax.broadcasted_iota(jnp.int32, (LANES, LANES), 1)
        same = jnp.where(row_place == lane, 1.0, 0.0).astype(jnp.bfloat16)

        @pl.loop(0, token_count // LANES)
        def _(block):
            rows = pl.ds(pl.multiple_of(block * LANES, LANES), LANES)
            turned = dot_nt(same, sorted_ref[rows, :].astype(jnp.bfloat16))
            group = group_ref[pl.ds(block, 1), :]
            kept = jnp.where(group == 0, turned[:columns, :], 0.0)
            for place in range(1, groups):
                kept += jnp.where(
                    group == place, turned[place * columns : (place + 1) * columns, :], 0.0
                )
            turned_ref[:, rows] = kept.astype(jnp.bfloat16)

    for part in range(VOCAB_BLOCK // VOCAB_PART):
        total_ref[...] = jnp.zeros_like(total_ref)
        place = step * (VOCAB_BLOCK // VOCAB_PART) + part
        first = place * VOCAB_PART

        @pl.loop(low_ref[place], high_ref[place])
        def _(block):
            rows = pl.ds(pl.multiple_of(block * LANES, LANES), LANES)
            word = lax.broadcasted_iota(jnp.int32, (VOCAB_PART, LANES), 0)
            hit = word == word_ref[pl.ds(block, 1), :] - first
            hit = jnp.where(hit, 1.0, 0.0).astype(jnp.bfloat16)
            total_ref[...] += dot_nt(turned_ref[:, rows], hit)

        gradient = total_ref[...]
        words = slice(part * VOCAB_PART, (part + 1) * VOCAB_PART)
        mean_new, square_new, update = adam_step(
            weight_ref[:, words], mean_ref[:, words], square_ref[:, words], gradient
        )
        mean_out_ref[:, words] = mean_new
        square_out_ref[:, words] = square_new
        update_ref[:, words] = update


def token_order(tokens, seq_len, vocabulary, groups):
    count = tokens.shape[0]
    devices = count // seq_len
    keys = lax.sort(tokens * count + jnp.arange(count, dtype=jnp.int32))
    words, origin = keys // count, keys % count
    device, place = origin // seq_len, origin % seq_len
    row = (place // groups) * devices + device
    words = words.reshape(count // LANES, LANES)
    group = (place % groups).reshape(count // LANES, LANES)
    steps = -(-vocabulary // VOCAB_BLOCK) * (VOCAB_BLOCK // VOCAB_PART)
    edges = jnp.arange(steps + 1, dtype=jnp.int32) * VOCAB_PART
    below = jnp.sum((tokens[None, :] < edges[:, None]).astype(jnp.int32), axis=1)
    low = below[:-1] // LANES
    high = (below[1:] + LANES - 1) // LANES
    high = jnp.where(below[1:] > below[:-1], high, low)
    return row, low, high, words, group


def embedding_update_of(order, arrived, weight, mean, square):
    row, low, high, words, group = order
    count = row.shape[0]
    columns, vocabulary = weight.shape
    block = pl.BlockSpec((columns, VOCAB_BLOCK), lambda step: (0, step))
    whole = pl.BlockSpec(memory_space=pltpu.VMEM)
    scalar = pl.BlockSpec(memory_space=pltpu.SMEM)
    wide = count * columns // LANES
    return pl.pallas_call(
        embedding_kernel,
        grid=(-(-vocabulary // VOCAB_BLOCK),),
        out_shape=[jax.ShapeDtypeStruct(weight.shape, jnp.float32)] * 3,
        in_specs=[scalar] * 3 + [whole] * 3 + [block] * 3,
        out_specs=[block] * 3,
        scratch_shapes=[
            pltpu.VMEM((wide, LANES), jnp.float32),
            pltpu.VMEM((count, LANES), jnp.float32),
            pltpu.VMEM((columns, count), jnp.bfloat16),
            pltpu.VMEM((columns, VOCAB_PART), jnp.float32),
        ],
        compiler_params=pltpu.CompilerParams(vmem_limit_bytes=48 * 1024 * 1024),
        cost_estimate=pl.CostEstimate(
            flops=1 << 32, bytes_accessed=50 * 1024 * 1024, transcendentals=1 << 20
        ),
    )(row, low, high, arrived, words, group, weight, mean, square)


def shards(
    tokens,
    prefix,
    routes,
    picked,
    loss_ids,
    teacher_logits,
    embedding,
    embedding_mean,
    embedding_square,
    attention,
    attention_mean,
    attention_square,
    router,
    router_mean,
    router_square,
    norm_gains,
    gains_mean,
    gains_square,
    expert_up,
    upward_mean,
    upward_square,
    expert_down,
    downward_mean,
    downward_square,
    output_table,
    table_mean,
    table_square,
):
    devices_all = lax.axis_size(AXES)
    me_all = lax.axis_index(AXES)
    row_groups = lax.axis_size("h")
    columns_x = lax.axis_size("x")
    seq_len = routes.shape[0]
    layer_count = attention.shape[0]
    experts_all = router.shape[2]
    capacity = 9 * seq_len * TOPK // (8 * experts_all)
    column_count = embedding.shape[1]
    prefix_len = prefix[0]
    slot_total = experts_all * capacity
    piece_rows = expert_up.shape[2]
    gain_count = norm_gains.shape[0]
    me_plane = lax.axis_index("z")
    member_place = jnp.arange(experts_all, dtype=jnp.int32)
    member_part = member_place % PLANES
    group_order = (
        (member_part // 2 + me_plane) % 2 * 2 + member_part % 2
    ) * columns_x + member_place // PLANES
    expert_plane = member_place // columns_x
    group_back = (
        member_place % columns_x * PLANES
        + (expert_plane // 2 + me_plane) % 2 * 2
        + expert_plane % 2
    )


    head_low = output_table.astype(jnp.bfloat16)
    vocab_local = head_low.shape[0]
    teacher_log = jax.nn.log_softmax(teacher_logits, axis=1)
    teacher_prob = jnp.exp(teacher_log)
    position_count = loss_ids.shape[0]
    teacher_mass = jnp.sum(teacher_prob, axis=1)
    coefficients = jnp.concatenate(
        [jnp.ones((position_count, 1), jnp.float32), teacher_prob], axis=1
    )
    table_low = embedding.astype(jnp.bfloat16)
    looked_up = jnp.take(table_low, tokens, axis=0, mode="clip").reshape(devices_all, seq_len * column_count)
    attention_low = lax.all_gather(attention.astype(jnp.bfloat16), AXES, axis=1, tiled=True)
    small_count = gain_count + layer_count * experts_all
    small = jnp.concatenate(
        [norm_gains.T, router.transpose(1, 0, 2).reshape(column_count, layer_count * experts_all)],
        axis=1,
    ).astype(jnp.bfloat16)
    small = jnp.broadcast_to(
        small.reshape(1, column_count * small_count), (devices_all, column_count * small_count)
    )
    arrived_rows = send_all(jnp.concatenate([looked_up, small], axis=1))
    fits_sum = [lax.axis_size(name) for name in AXES] == [PLANES, 2, 1, 2, 2]

    expert_parts, expert_pieces = [], []
    for layer_index in range(layer_count):
        down_piece = (
            expert_down[0, layer_index]
            .reshape(F // piece_rows, piece_rows, piece_rows)
            .transpose(1, 0, 2)
            .reshape(piece_rows, F)
        )
        piece = jnp.concatenate([expert_up[0, layer_index], down_piece], axis=1).astype(
            jnp.bfloat16
        )
        expert_pieces.append(piece)
    if not fits_sum:
        expert_parts.append(spread_experts(expert_pieces[0], row_groups))

    hidden = (
        arrived_rows[:, : seq_len * column_count]
        .reshape(devices_all, seq_len, column_count)
        .transpose(1, 0, 2)
        .reshape(seq_len, D)
        .astype(jnp.float32)
    )
    small_all = arrived_rows[:, seq_len * column_count :].reshape(D, small_count)
    gain_rows = jnp.pad(
        small_all[:, :gain_count].T.astype(jnp.float32), ((0, 16 - gain_count), (0, 0))
    )
    router_low = jnp.pad(
        small_all[:, gain_count:]
        .reshape(D, layer_count, experts_all)
        .transpose(1, 0, 2)[:, :, group_order],
        ((0, 0), (0, 0), (0, LANES - experts_all)),
    )

    member = jnp.any(routes[:, :, None] == group_order[None, None, :], axis=1)
    before = jnp.dot(
        jnp.tril(jnp.ones((seq_len, seq_len), jnp.bfloat16), -1),
        member.astype(jnp.bfloat16),
        preferred_element_type=jnp.float32,
    ).astype(jnp.int32)
    spread = (
        (before.T[:, None, :] == jnp.arange(capacity, dtype=jnp.int32)[None, :, None])
        & member.T[:, None, :]
    ).astype(jnp.bfloat16)
    spread_flat = spread.reshape(slot_total, seq_len)
    spread_back = spread_flat.T
    kept = jnp.pad(
        (member & (before < capacity)).astype(jnp.float32), ((0, 0), (0, LANES - experts_all))
    )
    turns = turn_tables(seq_len)
    places = jnp.stack([piece_place(turn, row_groups) for turn in all_turns(row_groups)]).astype(
        jnp.int32
    )

    stored = []
    extra = ()
    for layer_index in range(layer_count):
        saved = forward_layer(
            layer_index,
            capacity,
            experts_all,
            prefix,
            hidden,
            extra,
            attention_low,
            gain_rows,
            turns,
            router_low,
            kept,
            spread_flat,
            spread_back,
        )
        hidden = saved[6]
        gates, outgoing = saved[9], saved[10]
        blocks = outgoing.reshape(experts_all, capacity, D)
        if fits_sum:
            here = expert_parts[layer_index] if layer_index < len(expert_parts) else ()
            ahead = () if here else expert_pieces[layer_index : layer_index + 2]
            returned, received, *arrived = forward_exchange(blocks, here, ahead)
            for place in range(len(ahead)):
                expert_parts.append(arrived[place * PLANES : (place + 1) * PLANES])
        else:
            for piece in expert_pieces[layer_index + 1 : layer_index + 2]:
                expert_parts.append(spread_experts(piece, row_groups))
            received = send_plane(blocks).reshape(slot_total, D)
            produced = run_expert(places, received, expert_parts[layer_index])
            returned = send_plane(produced.reshape(experts_all, capacity, D))
        returned = returned.reshape(slot_total, D)
        stored.append((saved, received, returned))
        extra = (gates, returned)

    order = token_order(tokens, seq_len, embedding.shape[0], LANES // column_count)
    local_ids = loss_ids - me_all * vocab_local
    vocab_place = jnp.arange(vocab_local, dtype=jnp.int32)
    marked = jnp.sum(
        jnp.where(
            local_ids[:, :, None] == vocab_place[None, None, :], coefficients[:, :, None], 0.0
        ),
        axis=1,
    )
    marked_pull = jnp.dot(
        marked.astype(jnp.bfloat16), head_low, preferred_element_type=jnp.float32
    )
    own_count = position_count // devices_all

    final_rows, final_low = final_rows_of(
        capacity,
        4 * layer_count,
        picked,
        hidden,
        *extra,
        spread_flat,
        spread_back,
        gain_rows,
    )
    all_rows = send_all(jnp.broadcast_to(final_low[None], (devices_all, own_count, D))).reshape(
        position_count, D
    )
    logits = jnp.einsum("pd,vd->pv", all_rows, head_low, preferred_element_type=jnp.float32)
    local_peak = jnp.max(logits, axis=1)
    local_exp = jnp.exp(logits - local_peak[:, None])
    local_sum = jnp.sum(local_exp, axis=1)
    local_dot = jnp.sum(marked * logits, axis=1)
    pull = jnp.dot(local_exp.astype(jnp.bfloat16), head_low, preferred_element_type=jnp.float32)
    stats = jnp.stack(
        three_terms(local_peak) + three_terms(local_sum) + three_terms(local_dot), axis=1
    )
    stats = jnp.pad(stats, ((0, 0), (0, 128 - stats.shape[1])))
    pull_sent = jnp.concatenate([pull, marked_pull, stats], axis=1).astype(jnp.bfloat16)
    pull_got = send_all(pull_sent.reshape(devices_all, own_count, 2 * D + LANES))
    entropy = jnp.sum(teacher_prob * teacher_log, axis=1)
    own = lax.dynamic_slice_in_dim(
        jnp.pad(jnp.stack([teacher_mass, entropy], axis=1), ((0, 0), (0, LANES - 2))),
        me_all * own_count,
        own_count,
    )
    grad_hidden, sent_back, final_gain_grad, own_stats = first_pull(
        capacity,
        4 * layer_count,
        position_count,
        picked,
        pull_got,
        own,
        final_rows,
        gain_rows,
        spread_flat,
        extra[0],
    )
    final_gain_grad = final_gain_grad[0]
    gain_parts = [None] * (4 * layer_count) + [final_gain_grad]
    attention_parts = [None] * layer_count
    router_parts = [None] * layer_count
    piece_parts = [None] * layer_count
    for layer_index in reversed(range(layer_count)):
        saved, received, returned = stored[layer_index]
        hidden_in, projected, queries, keys, values, attended, middle, ffn_low, probs = saved[:9]
        upper = layer_index + 1 if layer_index + 1 < layer_count else None
        blocks = sent_back.reshape(experts_all, capacity, D)
        if fits_sum:
            *grad_pieces, back_inputs, logit_low, router_parts[layer_index] = backward_exchange(
                capacity,
                blocks,
                received,
                grad_hidden,
                returned,
                spread_back,
                probs,
                ffn_low,
                expert_parts[layer_index],
            )
        else:
            output_grad = send_plane(blocks).reshape(slot_total, D)
            logit_low, router_parts[layer_index] = router_back(
                capacity, grad_hidden, returned, spread_back, probs, ffn_low
            )
            input_grad, gate_grad, activated = run_expert_back(
                places, received, output_grad, expert_parts[layer_index]
            )
            back_inputs = send_plane(input_grad.reshape(experts_all, capacity, D))
            grad_pieces = run_expert_grad(
                places, received, output_grad, gate_grad, activated, piece_rows
            )
        back_inputs = back_inputs.reshape(slot_total, D)
        if upper is None:
            own_stats, back_inputs = tie(own_stats, back_inputs)
        if upper is not None:
            piece_parts[upper][1:], back_inputs = tie(piece_parts[upper][1:], back_inputs)
        if layer_index > 0:
            piece_parts[layer_index] = return_expert_grads(grad_pieces, row_groups)
        else:
            turns_all = len(grad_pieces)
            piece_parts[0] = []
        lower = (spread_flat, stored[layer_index - 1][0][9]) if layer_index > 0 else ()
        results = backward_layer(
            layer_index,
            capacity,
            prefix,
            grad_hidden,
            back_inputs,
            logit_low,
            hidden_in,
            projected,
            queries,
            keys,
            values,
            attended,
            middle,
            attention_low,
            gain_rows,
            turns,
            router_low,
            spread_back,
            lower,
        )
        grad_hidden, weight_grad, gain_grads = results[:3]
        gain_parts[4 * layer_index : 4 * layer_index + 4] = list(gain_grads[:4])
        if layer_index > 0:
            sent_back = results[3]
            piece_parts[layer_index][:1], sent_back = tie(piece_parts[layer_index][:1], sent_back)
        attention_parts[layer_index] = weight_grad
        if not fits_sum:
            attention_parts[layer_index] = lax.psum_scatter(
                weight_grad, AXES, scatter_dimension=0, tiled=True
            ).astype(jnp.float32)

    log_norm_own, loss_own = own_stats[:, 0], own_stats[:, 1]
    spread_stats = jnp.concatenate([log_norm_own, loss_own]).reshape(1, 2 * own_count)
    stats_all = send_all(jnp.broadcast_to(spread_stats, (devices_all, 2 * own_count)))
    log_norm = stats_all[:, :own_count].reshape(position_count)
    loss_value = jnp.sum(stats_all[:, own_count:]) / position_count
    grad_logits = (
        jnp.exp(logits - log_norm[:, None]) * (1.0 + teacher_mass)[:, None] - marked
    ) / position_count
    table_grad = jnp.einsum(
        "pv,pd->vd",
        grad_logits.astype(jnp.bfloat16),
        all_rows,
        preferred_element_type=jnp.float32,
    )

    sending = (
        grad_hidden.astype(jnp.bfloat16)
        .reshape(seq_len, devices_all, column_count)
        .transpose(1, 0, 2)
        .reshape(devices_all, seq_len * column_count)
    )
    small_grads = jnp.concatenate(
        [jnp.stack(gain_parts, axis=1)] + [part[:, group_back] for part in router_parts], axis=1
    ).astype(jnp.bfloat16)
    arrived_grads = send_all(
        jnp.concatenate(
            [sending, small_grads.reshape(devices_all, column_count * small_count)], axis=1
        )
    )
    if fits_sum:
        attention_parts = list(owner_sums(attention_parts[::-1], 2048))[::-1]
    grad_pieces, arrived_grads, attention_parts = lax.optimization_barrier(
        (grad_pieces, arrived_grads, attention_parts)
    )
    late = range(turns_all)
    piece_parts[0] = piece_parts[0] + return_expert_grads(grad_pieces, row_groups, late)
    embedding_next = embedding_update_of(
        order,
        arrived_grads[:, : seq_len * column_count],
        embedding.T,
        embedding_mean.T,
        embedding_square.T,
    )
    piece_parts[0], embedding_next = tie(piece_parts[0], embedding_next)
    up_parts, down_parts = [], []
    for parts in piece_parts:
        piece_grad = scatter_sum(parts)
        up_parts.append(piece_grad[:, : 2 * F])
        down_parts.append(
            piece_grad[:, 2 * F :]
            .reshape(piece_rows, F // piece_rows, piece_rows)
            .transpose(1, 0, 2)
            .reshape(F, piece_rows)
        )
    small_total = jnp.sum(
        arrived_grads[:, seq_len * column_count :].astype(jnp.float32), axis=0
    ).reshape(column_count, small_count)
    gains_grad = small_total[:, :gain_count].T
    router_grad = (
        small_total[:, gain_count:]
        .reshape(column_count, layer_count, experts_all)
        .transpose(1, 0, 2)
    )
    attention_grad = jnp.stack(attention_parts)
    upward_grad = jnp.stack(up_parts)[None]
    downward_grad = jnp.stack(down_parts)[None]
    embedding_mean_next, embedding_square_next, embedding_update = [
        part.T for part in embedding_next
    ]
    attention_mean_next, attention_square_next, attention_update = adam_step(
        attention, attention_mean, attention_square, attention_grad
    )
    router_mean_next, router_square_next, router_update = adam_step(
        router, router_mean, router_square, router_grad
    )
    gains_mean_next, gains_square_next, gains_update = adam_step(
        norm_gains, gains_mean, gains_square, gains_grad
    )
    upward_mean_next, upward_square_next, upward_update = adam_step(
        expert_up, upward_mean, upward_square, upward_grad
    )
    downward_mean_next, downward_square_next, downward_update = adam_step(
        expert_down, downward_mean, downward_square, downward_grad
    )
    table_mean_next, table_square_next, table_update = adam_step(
        output_table, table_mean, table_square, table_grad
    )
    return (
        loss_value,
        embedding_mean_next,
        embedding_square_next,
        embedding_update,
        attention_mean_next,
        attention_square_next,
        attention_update,
        router_mean_next,
        router_square_next,
        router_update,
        gains_mean_next,
        gains_square_next,
        gains_update,
        upward_mean_next,
        upward_square_next,
        upward_update,
        downward_mean_next,
        downward_square_next,
        downward_update,
        table_mean_next,
        table_square_next,
        table_update,
    )


def solution(mesh):
    expert_count, shard_count = mesh.devices.shape
    mesh = Mesh(
        mesh.devices.reshape(PLANES, expert_count // PLANES, shard_count // 4, 2, 2), AXES
    )
    return jax.shard_map(
        shards,
        mesh=mesh,
        in_specs=(
            P(),
            P(AXES),
            P(AXES, None),
            P(AXES),
            P(),
            P(),
            P(None, AXES),
            P(None, AXES),
            P(None, AXES),
            P(None, AXES, None),
            P(None, AXES, None),
            P(None, AXES, None),
            P(None, AXES, None),
            P(None, AXES, None),
            P(None, AXES, None),
            P(None, AXES),
            P(None, AXES),
            P(None, AXES),
            P(("z", "x"), None, ("h", "y", "c"), None),
            P(("z", "x"), None, ("h", "y", "c"), None),
            P(("z", "x"), None, ("h", "y", "c"), None),
            P(("z", "x"), None, None, ("h", "y", "c")),
            P(("z", "x"), None, None, ("h", "y", "c")),
            P(("z", "x"), None, None, ("h", "y", "c")),
            P(AXES, None),
            P(AXES, None),
            P(AXES, None),
        ),
        out_specs=(
            P(),
            P(None, AXES),
            P(None, AXES),
            P(None, AXES),
            P(None, AXES, None),
            P(None, AXES, None),
            P(None, AXES, None),
            P(None, AXES, None),
            P(None, AXES, None),
            P(None, AXES, None),
            P(None, AXES),
            P(None, AXES),
            P(None, AXES),
            P(("z", "x"), None, ("h", "y", "c"), None),
            P(("z", "x"), None, ("h", "y", "c"), None),
            P(("z", "x"), None, ("h", "y", "c"), None),
            P(("z", "x"), None, None, ("h", "y", "c")),
            P(("z", "x"), None, None, ("h", "y", "c")),
            P(("z", "x"), None, None, ("h", "y", "c")),
            P(AXES, None),
            P(AXES, None),
            P(AXES, None),
        ),
        check_vma=False,
    )
```

```python
import functools

import jax
import jax.numpy as jnp
from jax import lax
from jax.experimental import pallas as pl
from jax.experimental.pallas import tpu as pltpu
from jax.sharding import Mesh, PartitionSpec as P

D = 1024
HEADS = 16
HDIM = 64
F = 512
TOPK = 4
ADAM_STEP = 10


EPS_NORM = 1e-05
BETA_ONE = 0.9
BETA_TWO = 0.95
ADAM_EPS = 1e-08
LEARN_RATE = 0.01
DECAY_RATE = 0.1
ROPE_BASE = 10000.0
MASK_FILL = -1e30


AXES = ("z", "x", "h", "y", "c")
PLANES = 4
SHIFTS = (0, 2, 1, 3)
LANES = 128
CHUNKS = D // LANES


def dot_nn(left, right):
    return lax.dot_general(
        left, right, (((1,), (0,)), ((), ())), preferred_element_type=jnp.float32
    )


def dot_nt(left, right):
    return lax.dot_general(
        left, right, (((1,), (1,)), ((), ())), preferred_element_type=jnp.float32
    )


def dot_tn(left, right):
    return lax.dot_general(
        left, right, (((0,), (0,)), ((), ())), preferred_element_type=jnp.float32
    )


def inverse_root(values):
    return lax.rsqrt(jnp.mean(values * values, axis=-1, keepdims=True) + EPS_NORM)


def two_terms(values):
    high = values.astype(jnp.bfloat16)
    return high, (values - high.astype(jnp.float32)).astype(jnp.bfloat16)


def chunk(values, place):
    return values[:, place * LANES : (place + 1) * LANES]


def half_turn(values):
    lane = lax.broadcasted_iota(jnp.int32, values.shape, 1)
    ahead = pltpu.roll(values, LANES - HDIM // 2, 1)
    behind = pltpu.roll(values, HDIM // 2, 1)
    return jnp.where(lane % HDIM < HDIM // 2, ahead, behind)


def slot_gates(spread, gates, capacity):
    high, rest = two_terms(gates)
    full = dot_nn(spread, high) + dot_nn(spread, rest)
    expert = lax.broadcasted_iota(jnp.int32, full.shape, 0) // capacity
    lane = lax.broadcasted_iota(jnp.int32, full.shape, 1)
    return jnp.sum(jnp.where(lane == expert, full, 0.0), axis=1, keepdims=True)


def combine(middle, spread, spread_back, gates, returned, capacity):
    weighted = slot_gates(spread, gates, capacity) * returned.astype(jnp.float32)
    high, rest = two_terms(weighted)
    return middle + (dot_nn(spread_back, high) + dot_nn(spread_back, rest))


def masked_probs(query, key, visible):
    scores = dot_nt(query, key) * HDIM ** (-0.5)
    scores = jnp.where(visible, scores, MASK_FILL)
    weights = jnp.exp(scores - jnp.max(scores, axis=-1, keepdims=True))
    return weights / jnp.sum(weights, axis=-1, keepdims=True)


def visible_keys(prefix_ref, seq_len):
    query_place = lax.broadcasted_iota(jnp.int32, (seq_len, seq_len), 0)
    key_place = lax.broadcasted_iota(jnp.int32, (seq_len, seq_len), 1)
    return (key_place <= query_place) | (key_place < prefix_ref[0])


def head_masks(seq_len):
    lane = lax.broadcasted_iota(jnp.int32, (seq_len, LANES), 1)
    return lane < HDIM, lane >= HDIM


def fetch_weights(weight_ref, held_ref, copy_sem, layer_index, order):
    copies = {}
    for part in order:
        copies[part] = pltpu.make_async_copy(
            weight_ref.at[layer_index, :, pl.ds(part * D, D)], held_ref.at[part], copy_sem.at[part]
        )
        copies[part].start()
    return copies


def forward_kernel(
    layer_index,
    capacity,
    expert_count,
    prefix_ref,
    hidden_ref,
    *refs,
):
    if layer_index > 0:
        gates_in_ref, returned_ref, refs = refs[0], refs[1], refs[2:]
    (
        weight_ref,
        gain_ref,
        turn_ref,
        router_ref,
        kept_ref,
        spread_ref,
        spread_back_ref,
        hidden_out_ref,
        projected_ref,
        query_ref,
        key_ref,
        value_ref,
        attended_ref,
        middle_ref,
        ffn_ref,
        probs_ref,
        gates_ref,
        outgoing_ref,
        held_ref,
        copy_sem,
    ) = refs
    copies = fetch_weights(weight_ref, held_ref, copy_sem, layer_index, (0, 1, 2, 3))
    seq_len = hidden_ref.shape[0]
    hidden = hidden_ref[...]
    if layer_index > 0:
        hidden = combine(
            hidden,
            spread_ref[...],
            spread_back_ref[...],
            gates_in_ref[...],
            returned_ref[...],
            capacity,
        )
    hidden_out_ref[...] = hidden
    row = 4 * layer_index
    normed = (hidden * inverse_root(hidden) * gain_ref[row : row + 1, :]).astype(jnp.bfloat16)
    cosines, sines = turn_ref[0], turn_ref[1]
    for part, out_ref in ((0, query_ref), (1, key_ref)):
        columns = slice(part * D, (part + 1) * D)
        copies[part].wait()
        projected = dot_nn(normed, held_ref[part])
        projected_ref[:, columns] = projected
        scaled = projected * inverse_root(projected) * gain_ref[row + 1 + part : row + 2 + part, :]
        for place in range(CHUNKS):
            block = chunk(scaled, place)
            out_ref[:, place * LANES : (place + 1) * LANES] = (
                block * cosines + half_turn(block) * sines
            ).astype(jnp.bfloat16)
    copies[2].wait()
    value_ref[...] = dot_nn(normed, held_ref[2]).astype(jnp.bfloat16)
    visible = visible_keys(prefix_ref, seq_len)
    masks = head_masks(seq_len)
    zero = jnp.zeros((), jnp.bfloat16)
    for place in range(CHUNKS):
        columns = slice(place * LANES, (place + 1) * LANES)
        query, key, value = query_ref[:, columns], key_ref[:, columns], value_ref[:, columns]
        total = None
        for mask in masks:
            probs = masked_probs(query, jnp.where(mask, key, zero), visible).astype(jnp.bfloat16)
            term = dot_nn(probs, jnp.where(mask, value, zero))
            total = term if total is None else total + term
        attended_ref[:, columns] = total.astype(jnp.bfloat16)
    copies[3].wait()
    middle = hidden + dot_nn(attended_ref[...], held_ref[3])
    middle_ref[...] = middle
    ffn = (middle * inverse_root(middle) * gain_ref[row + 3 : row + 4, :]).astype(jnp.bfloat16)
    ffn_ref[...] = ffn
    outgoing_ref[...] = dot_nn(spread_ref[...], ffn).astype(jnp.bfloat16)
    logits = dot_nn(ffn, router_ref[layer_index])
    lane = lax.broadcasted_iota(jnp.int32, logits.shape, 1)
    logits = jnp.where(lane < expert_count, logits, MASK_FILL)
    weights = jnp.exp(logits - jnp.max(logits, axis=-1, keepdims=True))
    probs = weights / jnp.sum(weights, axis=-1, keepdims=True)
    probs_ref[...] = probs
    gates_ref[...] = probs * kept_ref[...]


def forward_layer(
    layer_index,
    capacity,
    expert_count,
    prefix,
    hidden,
    extra,
    weights,
    gains,
    turns,
    router,
    kept,
    spread,
    spread_back,
):
    seq_len = hidden.shape[0]
    whole = pl.BlockSpec(memory_space=pltpu.VMEM)
    wide = jax.ShapeDtypeStruct((seq_len, D), jnp.float32)
    low = jax.ShapeDtypeStruct((seq_len, D), jnp.bfloat16)
    small = jax.ShapeDtypeStruct((seq_len, LANES), jnp.float32)
    return pl.pallas_call(
        functools.partial(forward_kernel, layer_index, capacity, expert_count),
        out_shape=(
            wide,
            jax.ShapeDtypeStruct((seq_len, 2 * D), jnp.float32),
            low,
            low,
            low,
            low,
            wide,
            low,
            small,
            small,
            jax.ShapeDtypeStruct((spread.shape[0], D), jnp.bfloat16),
        ),
        in_specs=[pl.BlockSpec(memory_space=pltpu.SMEM), whole]
        + [whole] * len(extra)
        + [pl.BlockSpec(memory_space=pl.ANY)]
        + [whole] * 6,
        out_specs=[whole] * 11,
        scratch_shapes=[
            pltpu.VMEM((4, D, D), jnp.bfloat16),
            pltpu.SemaphoreType.DMA((4,)),
        ],
        compiler_params=pltpu.CompilerParams(vmem_limit_bytes=60 * 1024 * 1024),
        cost_estimate=pl.CostEstimate(
            flops=4 * seq_len * D * D * 3, bytes_accessed=24 * 1024 * 1024, transcendentals=1 << 20
        ),
    )(prefix, hidden, *extra, weights, gains, turns, router, kept, spread, spread_back)


def norm_pull(values, gain, upstream):
    root = inverse_root(values)
    scaled = values * root
    weighted = upstream * gain
    mean = jnp.mean(weighted * scaled, axis=-1, keepdims=True)
    return root * (weighted - scaled * mean), jnp.sum(upstream * scaled, axis=0, keepdims=True)


def backward_kernel(
    layer_index,
    capacity,
    prefix_ref,
    grad_ref,
    back_ref,
    logit_ref,
    hidden_ref,
    projected_ref,
    query_ref,
    key_ref,
    value_ref,
    attended_ref,
    middle_ref,
    weight_ref,
    gain_ref,
    turn_ref,
    router_ref,
    spread_back_ref,
    *refs,
):
    if layer_index > 0:
        spread_ref, gates_ref, refs = refs[0], refs[1], refs[2:]
        outgoing_ref, refs = refs[3], refs[:3] + refs[4:]
    grad_out_ref, weight_grad_ref, gain_grad_ref, pull_ref, key_pull_ref, held_ref, copy_sem = refs
    copies = fetch_weights(weight_ref, held_ref, copy_sem, layer_index, (3, 2, 0, 1))
    seq_len = hidden_ref.shape[0]
    row = 4 * layer_index
    ffn_grad = dot_nn(spread_back_ref[...], back_ref[...]) + dot_nt(
        logit_ref[...], router_ref[layer_index]
    )
    middle_grad, gain_three = norm_pull(
        middle_ref[...], gain_ref[row + 3 : row + 4, :], ffn_grad
    )
    grad_middle = grad_ref[...] + middle_grad
    grad_out_ref[...] = grad_middle
    branch = grad_middle.astype(jnp.bfloat16)
    weight_grad_ref[:, 3 * D :] = dot_tn(attended_ref[...], branch).astype(jnp.bfloat16)
    copies[3].wait()
    pull_ref[...] = dot_nt(branch, held_ref[3]).astype(jnp.bfloat16)
    visible = visible_keys(prefix_ref, seq_len)
    masks = head_masks(seq_len)
    zero = jnp.zeros((), jnp.bfloat16)
    cosines, sines = turn_ref[0], turn_ref[1]
    factor = HDIM ** (-0.5)
    hidden = hidden_ref[...]
    normed = (hidden * inverse_root(hidden) * gain_ref[row : row + 1, :]).astype(jnp.bfloat16)
    for place in range(CHUNKS):
        columns = slice(place * LANES, (place + 1) * LANES)
        query, key, value = query_ref[:, columns], key_ref[:, columns], value_ref[:, columns]
        pull = pull_ref[:, columns]
        totals = [None, None, None]
        for mask in masks:
            key_half = jnp.where(mask, key, zero)
            probs = masked_probs(query, key_half, visible)
            pulled = dot_nt(pull, jnp.where(mask, value, zero))
            inner = jnp.sum(probs * pulled, axis=-1, keepdims=True)
            score_grad = (probs * (pulled - inner)).astype(jnp.bfloat16)
            terms = (
                dot_nn(score_grad, key_half),
                dot_tn(score_grad, jnp.where(mask, query, zero)),
                dot_tn(probs.astype(jnp.bfloat16), jnp.where(mask, pull, zero)),
            )
            totals = [b if a is None else a + b for a, b in zip(totals, terms)]
        for part, target_ref in ((0, key_pull_ref.at[0]), (1, key_pull_ref.at[1])):
            turned = (totals[part] * factor).astype(jnp.bfloat16).astype(jnp.float32)
            target_ref[:, columns] = turned * cosines - half_turn(turned) * sines
        pull_ref[:, columns] = totals[2].astype(jnp.bfloat16)
    gain_rows = []
    value_pull = pull_ref[...]
    copies[2].wait()
    back = dot_nt(value_pull, held_ref[2])
    weight_grad_ref[:, 2 * D : 3 * D] = dot_tn(normed, value_pull).astype(jnp.bfloat16)
    for part in range(2):
        columns = slice(part * D, (part + 1) * D)
        input_pull, gain_row = norm_pull(
            projected_ref[:, columns],
            gain_ref[row + 1 + part : row + 2 + part, :],
            key_pull_ref[part],
        )
        gain_rows.append(gain_row)
        low_pull = input_pull.astype(jnp.bfloat16)
        weight_grad_ref[:, columns] = dot_tn(normed, low_pull).astype(jnp.bfloat16)
        copies[part].wait()
        back = back + dot_nt(low_pull, held_ref[part])
    hidden_grad, gain_zero = norm_pull(hidden, gain_ref[row : row + 1, :], back)
    grad_out = grad_out_ref[...] + hidden_grad
    grad_out_ref[...] = grad_out
    if layer_index > 0:
        outgoing_ref[...] = outgoing_pull(grad_out, spread_ref[...], gates_ref[...], capacity)
    gain_grad_ref[...] = jnp.concatenate(
        [gain_zero] + gain_rows + [gain_three, jnp.zeros((4, D), jnp.float32)], axis=0
    )


def backward_layer(
    layer_index,
    capacity,
    prefix,
    grad,
    back_inputs,
    logit_low,
    hidden,
    projected,
    queries,
    keys,
    values,
    attended,
    middle,
    weights,
    gains,
    turns,
    router,
    spread_back,
    extra,
):
    seq_len = hidden.shape[0]
    whole = pl.BlockSpec(memory_space=pltpu.VMEM)
    out_shape = [
        jax.ShapeDtypeStruct((seq_len, D), jnp.float32),
        jax.ShapeDtypeStruct((D, 4 * D), jnp.bfloat16),
        jax.ShapeDtypeStruct((8, D), jnp.float32),
    ]
    if layer_index > 0:
        out_shape.append(jax.ShapeDtypeStruct((spread_back.shape[1], D), jnp.bfloat16))
    return pl.pallas_call(
        functools.partial(backward_kernel, layer_index, capacity),
        out_shape=out_shape,
        in_specs=[pl.BlockSpec(memory_space=pltpu.SMEM)]
        + [whole] * 10
        + [pl.BlockSpec(memory_space=pl.ANY)]
        + [whole] * (4 + len(extra)),
        out_specs=[whole] * len(out_shape),
        scratch_shapes=[
            pltpu.VMEM((seq_len, D), jnp.bfloat16),
            pltpu.VMEM((2, seq_len, D), jnp.float32),
            pltpu.VMEM((4, D, D), jnp.bfloat16),
            pltpu.SemaphoreType.DMA((4,)),
        ],
        compiler_params=pltpu.CompilerParams(vmem_limit_bytes=60 * 1024 * 1024),
        cost_estimate=pl.CostEstimate(
            flops=8 * seq_len * D * D * 3, bytes_accessed=32 * 1024 * 1024, transcendentals=1 << 20
        ),
    )(
        prefix,
        grad,
        back_inputs,
        logit_low,
        hidden,
        projected,
        queries,
        keys,
        values,
        attended,
        middle,
        weights,
        gains,
        turns,
        router,
        spread_back,
        *extra,
    )


def turn_tables(seq_len):
    position = jnp.arange(seq_len, dtype=jnp.float32)[:, None]
    frequency = ROPE_BASE ** (-jnp.arange(HDIM // 2, dtype=jnp.float32) * 2.0 / HDIM)
    angles = position * frequency[None, :]
    cosines, sines = jnp.cos(angles), jnp.sin(angles)
    return jnp.stack(
        [
            jnp.concatenate([cosines] * 4, axis=1),
            jnp.concatenate([-sines, sines, -sines, sines], axis=1),
        ]
    )


def silu_parts(gate_up):
    gate_part, up_part = gate_up[:, :F], gate_up[:, F:]
    sigmoid = 1.0 / (1.0 + jnp.exp(-gate_part))
    return gate_part, up_part, sigmoid


def fetch_expert(places, part_refs, up_ref, down_ref, copy_sem):
    copies = []
    rows = part_refs[0].shape[0]
    for turn, part_ref in enumerate(part_refs):
        place = pl.multiple_of(places[turn] * rows, rows)
        copies.append(
            pltpu.make_async_copy(
                part_ref.at[:, pl.ds(0, 2 * F)],
                up_ref.at[pl.ds(place, rows), :],
                copy_sem.at[len(copies)],
            )
        )
        for block in range(F // rows):
            copies.append(
                pltpu.make_async_copy(
                    part_ref.at[:, pl.ds(2 * F + block * rows, rows)],
                    down_ref.at[pl.ds(block * rows, rows), pl.ds(place, rows)],
                    copy_sem.at[len(copies)],
                )
            )
    for copy in copies:
        copy.start()
    for copy in copies:
        copy.wait()


def expert_kernel(part_count, row_block, place_ref, received_ref, *refs):
    part_refs, (produced_ref, up_ref, down_ref, copy_sem) = refs[:part_count], refs[part_count:]
    fetch_expert(place_ref, part_refs, up_ref, down_ref, copy_sem)

    @pl.loop(0, received_ref.shape[0] // row_block)
    def _(step):
        rows = pl.ds(pl.multiple_of(step * row_block, row_block), row_block)
        gate_part, up_part, sigmoid = silu_parts(dot_nn(received_ref[rows, :], up_ref[...]))
        activated = (gate_part * sigmoid * up_part).astype(jnp.bfloat16)
        produced_ref[rows, :] = dot_nn(activated, down_ref[...]).astype(jnp.bfloat16)


def expert_specs(parts):
    rows = parts[0].shape[0]
    whole = pl.BlockSpec(memory_space=pltpu.VMEM)
    specs = [pl.BlockSpec(memory_space=pltpu.SMEM)]
    apart = [pl.BlockSpec(memory_space=pl.ANY)] * len(parts)
    scratch = [
        pltpu.VMEM((D, 2 * F), jnp.bfloat16),
        pltpu.VMEM((F, D), jnp.bfloat16),
        pltpu.SemaphoreType.DMA((len(parts) * (1 + F // rows),)),
    ]
    return whole, specs, apart, scratch


def run_expert(places, received, parts):
    whole, specs, apart, scratch = expert_specs(parts)
    slot_total = received.shape[0]
    return pl.pallas_call(
        functools.partial(expert_kernel, len(parts), slot_total // 4),
        out_shape=jax.ShapeDtypeStruct((slot_total, D), jnp.bfloat16),
        in_specs=specs + [whole] + apart,
        out_specs=whole,
        scratch_shapes=scratch,
        compiler_params=pltpu.CompilerParams(vmem_limit_bytes=56 * 1024 * 1024),
        cost_estimate=pl.CostEstimate(
            flops=slot_total * D * F * 6, bytes_accessed=8 * 1024 * 1024, transcendentals=1 << 19
        ),
    )(places, received, *parts)


def expert_back_kernel(part_count, row_block, place_ref, received_ref, pull_ref, *refs):
    part_refs, refs = refs[:part_count], refs[part_count:]
    input_grad_ref, gate_grad_ref, activated_ref, up_ref, down_ref, copy_sem = refs
    fetch_expert(place_ref, part_refs, up_ref, down_ref, copy_sem)

    @pl.loop(0, received_ref.shape[0] // row_block)
    def _(step):
        rows = pl.ds(pl.multiple_of(step * row_block, row_block), row_block)
        gate_part, up_part, sigmoid = silu_parts(dot_nn(received_ref[rows, :], up_ref[...]))
        side = gate_part * sigmoid
        activated_ref[rows, :] = (side * up_part).astype(jnp.bfloat16)
        pulled = dot_nt(pull_ref[rows, :], down_ref[...]).astype(jnp.bfloat16)
        pulled = pulled.astype(jnp.float32)
        gate_side = pulled * up_part * sigmoid * (1.0 + gate_part * (1.0 - sigmoid))
        gate_grad_ref[rows, :F] = gate_side.astype(jnp.bfloat16)
        gate_grad_ref[rows, F:] = (pulled * side).astype(jnp.bfloat16)
        input_grad_ref[rows, :] = dot_nt(gate_grad_ref[rows, :], up_ref[...]).astype(jnp.bfloat16)


def run_expert_back(places, received, pull, parts):
    whole, specs, apart, scratch = expert_specs(parts)
    slot_total = received.shape[0]
    return pl.pallas_call(
        functools.partial(expert_back_kernel, len(parts), slot_total // 4),
        out_shape=(
            jax.ShapeDtypeStruct((slot_total, D), jnp.bfloat16),
            jax.ShapeDtypeStruct((slot_total, 2 * F), jnp.bfloat16),
            jax.ShapeDtypeStruct((slot_total, F), jnp.bfloat16),
        ),
        in_specs=specs + [whole] * 2 + apart,
        out_specs=[whole] * 3,
        scratch_shapes=scratch,
        compiler_params=pltpu.CompilerParams(vmem_limit_bytes=56 * 1024 * 1024),
        cost_estimate=pl.CostEstimate(
            flops=slot_total * D * F * 12, bytes_accessed=12 * 1024 * 1024, transcendentals=1 << 19
        ),
    )(places, received, pull, *parts)


def expert_grad_kernel(
    part_count, place_ref, received_ref, pull_ref, gate_grad_ref, activated_ref, *refs
):
    out_refs, (up_ref, down_ref) = refs[:part_count], refs[part_count:]
    block = 256

    @pl.loop(0, D // block)
    def _(step):
        columns = pl.ds(pl.multiple_of(step * block, block), block)
        up_ref[columns, :] = dot_tn(received_ref[:, columns], gate_grad_ref[...]).astype(
            jnp.bfloat16
        )

    @pl.loop(0, F // block)
    def _(step):
        columns = pl.ds(pl.multiple_of(step * block, block), block)
        down_ref[columns, :] = dot_tn(activated_ref[:, columns], pull_ref[...]).astype(
            jnp.bfloat16
        )

    rows = out_refs[0].shape[0]
    for turn, out_ref in enumerate(out_refs):
        place = pl.multiple_of(place_ref[turn] * rows, rows)
        out_ref[:, : 2 * F] = up_ref[pl.ds(place, rows), :]
        for part in range(F // rows):
            out_ref[:, 2 * F + part * rows : 2 * F + (part + 1) * rows] = down_ref[
                part * rows : (part + 1) * rows, pl.ds(place, rows)
            ]


def run_expert_grad(places, received, pull, gate_grad, activated, piece_rows):
    whole = pl.BlockSpec(memory_space=pltpu.VMEM)
    part_count = D // piece_rows
    slot_total = received.shape[0]
    return pl.pallas_call(
        functools.partial(expert_grad_kernel, part_count),
        out_shape=[jax.ShapeDtypeStruct((piece_rows, 3 * F), jnp.bfloat16)] * part_count,
        in_specs=[pl.BlockSpec(memory_space=pltpu.SMEM)] + [whole] * 4,
        out_specs=[whole] * part_count,
        scratch_shapes=[
            pltpu.VMEM((D, 2 * F), jnp.bfloat16),
            pltpu.VMEM((F, D), jnp.bfloat16),
        ],
        compiler_params=pltpu.CompilerParams(vmem_limit_bytes=56 * 1024 * 1024),
        cost_estimate=pl.CostEstimate(
            flops=slot_total * D * F * 6, bytes_accessed=12 * 1024 * 1024, transcendentals=0
        ),
    )(places, received, pull, gate_grad, activated)


def outgoing_pull(grad, spread, gates, capacity):
    high, rest = two_terms(grad)
    wide = dot_nn(spread, high) + dot_nn(spread, rest)
    return (slot_gates(spread, gates, capacity) * wide).astype(jnp.bfloat16)


def first_pull_kernel(
    capacity,
    gain_row,
    position_count,
    picked_ref,
    got_ref,
    own_ref,
    rows_ref,
    gain_ref,
    spread_ref,
    gates_ref,
    grad_ref,
    out_ref,
    gain_grad_ref,
    stat_ref,
):
    stats = got_ref[:, :, 2 * D :].astype(jnp.float32)

    def joined(place):
        return sum(stats[:, :, place + term : place + term + 1] for term in range(3))

    peaks, sums, dots = joined(0), joined(3), joined(6)
    peak = jnp.max(peaks, axis=0)
    log_norm = peak + jnp.log(jnp.sum(sums * jnp.exp(peaks - peak[None]), axis=0))
    mass, entropy = own_ref[:, 0:1], own_ref[:, 1:2]
    loss = (1.0 + mass) * log_norm - jnp.sum(dots, axis=0) + entropy
    scale = (1.0 + mass)[None] * jnp.exp(peaks - log_norm[None])
    total = jnp.zeros(rows_ref.shape, jnp.float32)
    for device in range(got_ref.shape[0]):
        total += scale[device] * got_ref[device, :, :D].astype(jnp.float32)
        total -= got_ref[device, :, D : 2 * D].astype(jnp.float32)
    rows_grad, gain_grad = norm_pull(
        rows_ref[...], gain_ref[gain_row : gain_row + 1, :], total / position_count
    )
    gain_grad_ref[...] = gain_grad
    lane = lax.broadcasted_iota(jnp.int32, stat_ref.shape, 1)
    stat_ref[...] = jnp.where(lane == 0, log_norm, jnp.where(lane == 1, loss, 0.0))
    grad_ref[...] = jnp.zeros_like(grad_ref)
    for place in range(rows_ref.shape[0]):
        grad_ref[pl.ds(picked_ref[place], 1), :] = rows_grad[place : place + 1, :]
    out_ref[...] = outgoing_pull(grad_ref[...], spread_ref[...], gates_ref[...], capacity)


def first_pull(capacity, gain_row, position_count, picked, got, own, rows, gains, spread, gates):
    whole = pl.BlockSpec(memory_space=pltpu.VMEM)
    return pl.pallas_call(
        functools.partial(first_pull_kernel, capacity, gain_row, position_count),
        out_shape=(
            jax.ShapeDtypeStruct((spread.shape[1], D), jnp.float32),
            jax.ShapeDtypeStruct((spread.shape[0], D), jnp.bfloat16),
            jax.ShapeDtypeStruct((1, D), jnp.float32),
            jax.ShapeDtypeStruct(own.shape, jnp.float32),
        ),
        in_specs=[pl.BlockSpec(memory_space=pltpu.SMEM)] + [whole] * 6,
        out_specs=[whole] * 4,
        compiler_params=pltpu.CompilerParams(vmem_limit_bytes=48 * 1024 * 1024),
        cost_estimate=pl.CostEstimate(
            flops=4 * spread.shape[0] * spread.shape[1] * D,
            bytes_accessed=6 * 1024 * 1024,
            transcendentals=0,
        ),
    )(picked, got, own, rows, gains, spread, gates)


def router_kernel(
    capacity, grad_ref, returned_ref, spread_back_ref, probs_ref, ffn_ref, low_ref, router_grad_ref
):
    high, rest = two_terms(grad_ref[...])
    dots = dot_nt(high, returned_ref[...]) + dot_nt(rest, returned_ref[...])
    dots = dots * spread_back_ref[...].astype(jnp.float32)
    slot_total = returned_ref.shape[0]
    slot = lax.broadcasted_iota(jnp.int32, (slot_total, LANES), 0) // capacity
    lane = lax.broadcasted_iota(jnp.int32, (slot_total, LANES), 1)
    owner = jnp.where(slot == lane, 1.0, 0.0).astype(jnp.bfloat16)
    high, rest = two_terms(dots)
    pull = dot_nn(high, owner) + dot_nn(rest, owner)
    probs = probs_ref[...]
    low = (probs * (pull - jnp.sum(probs * pull, axis=-1, keepdims=True))).astype(jnp.bfloat16)
    low_ref[...] = low
    router_grad_ref[...] = dot_tn(ffn_ref[...], low)


def router_back(capacity, grad, returned, spread_back, probs, ffn):
    whole = pl.BlockSpec(memory_space=pltpu.VMEM)
    seq_len = grad.shape[0]
    return pl.pallas_call(
        functools.partial(router_kernel, capacity),
        out_shape=(
            jax.ShapeDtypeStruct((seq_len, LANES), jnp.bfloat16),
            jax.ShapeDtypeStruct((D, LANES), jnp.float32),
        ),
        in_specs=[whole] * 5,
        out_specs=[whole] * 2,
        compiler_params=pltpu.CompilerParams(vmem_limit_bytes=48 * 1024 * 1024),
        cost_estimate=pl.CostEstimate(
            flops=4 * seq_len * returned.shape[0] * D,
            bytes_accessed=6 * 1024 * 1024,
            transcendentals=0,
        ),
    )(grad, returned, spread_back, probs, ffn)


def final_kernel(
    capacity,
    gain_row,
    picked_ref,
    middle_ref,
    gates_ref,
    returned_ref,
    spread_ref,
    spread_back_ref,
    gain_ref,
    rows_ref,
    low_ref,
):
    count = rows_ref.shape[0]
    for place in range(count):
        rows_ref[place : place + 1, :] = middle_ref[pl.ds(picked_ref[place], 1), :]
    sublane = lax.broadcasted_iota(jnp.int32, (count, LANES), 0)
    wanted = jnp.zeros((count, LANES), jnp.int32)
    for place in range(count):
        wanted = jnp.where(sublane == place, picked_ref[place], wanted)
    seq_len = middle_ref.shape[0]
    token = lax.broadcasted_iota(jnp.int32, (count, seq_len), 1)
    wanted = jnp.concatenate([wanted] * (seq_len // LANES), axis=1)
    chosen = jnp.where(token == wanted, 1.0, 0.0).astype(jnp.bfloat16)
    slots = dot_nn(chosen, spread_back_ref[...]).astype(jnp.bfloat16)
    weighted = slot_gates(spread_ref[...], gates_ref[...], capacity) * returned_ref[...].astype(
        jnp.float32
    )
    high, rest = two_terms(weighted)
    rows = rows_ref[...] + (dot_nn(slots, high) + dot_nn(slots, rest))
    rows_ref[...] = rows
    low_ref[...] = (rows * inverse_root(rows) * gain_ref[gain_row : gain_row + 1, :]).astype(
        jnp.bfloat16
    )


def final_rows_of(capacity, gain_row, picked, middle, gates, returned, spread, spread_back, gains):
    whole = pl.BlockSpec(memory_space=pltpu.VMEM)
    count = picked.shape[0]
    return pl.pallas_call(
        functools.partial(final_kernel, capacity, gain_row),
        out_shape=(
            jax.ShapeDtypeStruct((count, D), jnp.float32),
            jax.ShapeDtypeStruct((count, D), jnp.bfloat16),
        ),
        in_specs=[pl.BlockSpec(memory_space=pltpu.SMEM)] + [whole] * 6,
        out_specs=[whole] * 2,
        compiler_params=pltpu.CompilerParams(vmem_limit_bytes=48 * 1024 * 1024),
        cost_estimate=pl.CostEstimate(
            flops=1 << 28, bytes_accessed=5 * 1024 * 1024, transcendentals=0
        ),
    )(picked, middle, gates, returned, spread, spread_back, gains)


def tie(first, second):
    return lax.optimization_barrier((first, second))


def swap_pairs(row_groups, turn_plane, turn_row):
    pairs = []
    for plane in range(PLANES):
        for row in range(row_groups):
            for part in range(PLANES):
                source = (plane * row_groups + row) * PLANES + part
                target_plane = (plane + SHIFTS[part ^ turn_plane]) % PLANES
                target_row = (row + turn_row) % row_groups
                target_part = (plane // 2 + target_plane) % 2 * 2 + plane % 2
                pairs.append(
                    (source, (target_plane * row_groups + target_row) * PLANES + target_part)
                )
    return pairs


def all_turns(row_groups):
    return [(plane, row) for row in range(row_groups) for plane in range(PLANES)]


def shift_inverse(shift):
    return jnp.array(SHIFTS, jnp.int32)[shift]


def part_of_turn(turn_plane):
    me_plane = lax.axis_index("z")
    expert_plane = (lax.axis_index("y") + me_plane) % 2 * 2 + lax.axis_index("c")
    return shift_inverse((me_plane - expert_plane) % PLANES) ^ turn_plane


def piece_place(turn, row_groups):
    turn_plane, turn_row = turn
    row = (lax.axis_index("h") - turn_row) % row_groups
    return row * PLANES + part_of_turn(turn_plane)


def spread_experts(piece, row_groups):
    return [
        lax.ppermute(
            piece, ("z", "h", "y", "c"), swap_pairs(row_groups, turn_plane, turn_row)
        )
        for turn_plane, turn_row in all_turns(row_groups)
    ]


def return_expert_grads(pieces, row_groups, chosen=None):
    arrived = []
    for place, (piece, turn) in enumerate(zip(pieces, all_turns(row_groups))):
        if chosen is not None and place not in chosen:
            continue
        back = [(target, source) for source, target in swap_pairs(row_groups, *turn)]
        arrived.append(lax.ppermute(piece, ("z", "h", "y", "c"), back))
    return arrived


def scatter_sum(parts):
    total = parts[0].astype(jnp.float32)
    for part in parts[1:]:
        total = total + part.astype(jnp.float32)
    return total


def send_all(values):
    return lax.all_to_all(values, AXES, split_axis=0, concat_axis=0, tiled=True)


def send_plane(values):
    return lax.all_to_all(values, ("x", "y", "c"), split_axis=0, concat_axis=0, tiled=True)


def three_terms(values):
    first = lax.reduce_precision(values, 8, 7)
    second = lax.reduce_precision(values - first, 8, 7)
    third = lax.reduce_precision(values - first - second, 8, 7)
    return [first, second, third]

PLANE_RING = ("x", "y", "c")


def plane_partners():
    at = {name: lax.axis_index(name) for name in PLANE_RING}
    partners, groups = [None], [at["x"] * 4 + at["y"] * 2 + at["c"]]
    for turn in range(1, 8):
        flips = {"x": turn // 4, "y": turn // 2 % 2, "c": turn % 2}
        there = {name: 1 - at[name] if flips[name] else at[name] for name in PLANE_RING}
        partners.append({name: there[name] for name in PLANE_RING if flips[name]})
        groups.append(there["x"] * 4 + there["y"] * 2 + there["c"])
    return partners, groups


def part_places(part_count):
    plane = lax.axis_index("z")
    expert_plane = lax.rem(lax.axis_index("y") + plane, 2) * 2 + lax.axis_index("c")
    shift = lax.rem(plane - expert_plane + PLANES, PLANES)
    upper, lower = lax.rem(shift, 2), shift // 2
    places = []
    for turn in range(part_count):
        first = 1 - upper if turn // 2 else upper
        second = 1 - lower if turn % 2 else lower
        places.append(first * 2 + second)
    return places


def swap_routes():
    z, y, c = (lax.axis_index(name) for name in ("z", "y", "c"))
    expert_plane = lax.rem(y + z, 2) * 2 + c
    shift_in = lax.rem(z - expert_plane + PLANES, PLANES)
    routes = []
    for turn in range(PLANES):
        upper = 1 - y if turn // 2 else y
        lower = 1 - c if turn % 2 else c
        plane = lax.rem(z + lower * 2 + upper, PLANES)
        target = {"z": plane, "y": lax.rem(z // 2 + plane, 2), "c": lax.rem(z, 2)}
        first, second = lax.rem(shift_in, 2), shift_in // 2
        source = {
            "z": expert_plane,
            "y": 1 - first if turn // 2 else first,
            "c": 1 - second if turn % 2 else second,
        }
        own = (target["z"] == z) & (target["y"] == y) & (target["c"] == c)
        routes.append((target, source, own))
    return routes


def swap_copies(route, turn, held_ref, slot_ref, sems, backward):
    target, source, _ = route
    send_sem, recv_sem, local_sem = sems
    away = pltpu.make_async_remote_copy(
        src_ref=held_ref,
        dst_ref=slot_ref,
        send_sem=send_sem.at[turn],
        recv_sem=recv_sem.at[turn],
        device_id=source if backward else target,
        device_id_type=pl.DeviceIdType.MESH,
    )
    return away, pltpu.make_async_copy(held_ref, slot_ref, local_sem.at[turn])


def swap_start(routes, held_refs, slot_refs, sems, backward):
    for turn, route in enumerate(routes):
        away, stay = swap_copies(route, turn, held_refs[turn], slot_refs[turn], sems, backward)
        pl.when(jnp.logical_not(route[2]))(away.start)
        pl.when(route[2])(stay.start)


def swap_wait(routes, held_refs, slot_refs, sems, backward):
    for turn, route in enumerate(routes):
        away, stay = swap_copies(route, turn, held_refs[turn], slot_refs[turn], sems, backward)
        pl.when(jnp.logical_not(route[2]))(away.wait)
        pl.when(route[2])(stay.wait)


def greet(partners, routes=()):
    barrier = pltpu.get_barrier_semaphore()

    def hello(partner):
        pl.semaphore_signal(
            barrier, inc=1, device_id=partner, device_id_type=pl.DeviceIdType.MESH
        )

    for partner in partners:
        hello(partner)
    for target, source, own in routes:

        @pl.when(jnp.logical_not(own))
        def _(target=target, source=source):
            hello(target)
            hello(source)

    count = len(partners)
    for _, _, own in routes:
        count = count + jnp.where(own, 0, 2)
    pl.semaphore_wait(barrier, count)


def swap_scratch(count):
    return [pltpu.SemaphoreType.DMA((PLANES,))] * (3 * count)


def push(source, target, send_sem, recv_sem, place, partner):
    copy = pltpu.make_async_remote_copy(
        src_ref=source,
        dst_ref=target,
        send_sem=send_sem.at[place],
        recv_sem=recv_sem.at[place],
        device_id=partner,
        device_id_type=pl.DeviceIdType.MESH,
    )
    copy.start()
    return copy


FAR_FIRST = (6, 7, 4, 5, 2, 3, 1)


def exchange_out(outgoing_ref, received_ref, send_sem, recv_sem, partners, groups):
    copies = {}
    for turn in FAR_FIRST:
        copies[turn] = push(
            outgoing_ref.at[groups[turn]],
            received_ref.at[turn],
            send_sem,
            recv_sem,
            turn,
            partners[turn],
        )
    received_ref[0] = outgoing_ref[groups[0]]
    return copies


def flat_rows(block):
    return block.reshape(block.shape[0] * block.shape[1], block.shape[2])


def two_blocks(ref, pair):
    return flat_rows(ref[2 * pair : 2 * pair + 2])


def put_two(ref, pair, values):
    rows = values.shape[0] // 2
    ref[2 * pair] = values[:rows]
    ref[2 * pair + 1] = values[rows:]


def forward_exchange_kernel(spread_count, outgoing_ref, *refs):
    routes = ()
    if spread_count:
        routes = swap_routes()
        pieces, refs = refs[:spread_count], refs[spread_count:]
        returned_ref, received_ref = refs[:2]
        slots, refs = refs[2 : 2 + spread_count * PLANES], refs[2 + spread_count * PLANES :]
        sems, refs = refs[-3 * spread_count :], refs[: -3 * spread_count]
        swaps = [
            (
                routes,
                [piece] * PLANES,
                slots[place * PLANES : (place + 1) * PLANES],
                sems[3 * place : 3 * place + 3],
                False,
            )
            for place, piece in enumerate(pieces)
        ]
        part_refs = slots[:PLANES]
    else:
        part_refs, refs = refs[:PLANES], refs[PLANES:]
        returned_ref, received_ref = refs[:2]
        swaps, refs = [], refs[2:]
    up_ref, down_ref, produced_ref, copy_sem, send_sem, recv_sem = refs
    partners, groups = plane_partners()
    greet(partners[1:], routes)
    for swap in swaps[:1]:
        swap_start(*swap)
    copies = exchange_out(outgoing_ref, received_ref, send_sem, recv_sem, partners, groups)
    for swap in swaps[:1]:
        swap_wait(*swap)
    for swap in swaps[1:]:
        swap_start(*swap)
    fetch_expert(part_places(PLANES), part_refs, up_ref, down_ref, copy_sem)
    back = {}
    for pair in (0, 3, 2, 1):
        for turn in (2 * pair, 2 * pair + 1):
            if turn:
                copies[turn].wait_recv()
        gate_part, up_part, sigmoid = silu_parts(
            dot_nn(two_blocks(received_ref, pair), up_ref[...])
        )
        activated = (gate_part * sigmoid * up_part).astype(jnp.bfloat16)
        put_two(produced_ref, pair, dot_nn(activated, down_ref[...]).astype(jnp.bfloat16))
        for turn in (2 * pair, 2 * pair + 1):
            if turn:
                back[turn] = push(
                    produced_ref.at[turn],
                    returned_ref.at[groups[0]],
                    send_sem,
                    recv_sem,
                    8 + turn,
                    partners[turn],
                )
    returned_ref[groups[0]] = produced_ref[0]
    for turn in range(1, 8):
        copies[turn].wait_send()
        back[turn].wait()
    for swap in swaps[1:]:
        swap_wait(*swap)


def forward_exchange(outgoing, parts, pieces=()):
    whole = pl.BlockSpec(memory_space=pltpu.VMEM)
    apart = [pl.BlockSpec(memory_space=pl.ANY)]
    sources = list(pieces) if pieces else list(parts)
    rows = sources[0].shape[0]
    shape = jax.ShapeDtypeStruct(outgoing.shape, jnp.bfloat16)
    slot_total = outgoing.shape[0] * outgoing.shape[1]
    slots = [
        jax.ShapeDtypeStruct(piece.shape, piece.dtype) for piece in pieces for _ in range(PLANES)
    ]
    return pl.pallas_call(
        functools.partial(forward_exchange_kernel, len(pieces)),
        out_shape=[shape, shape] + slots,
        in_specs=[whole] + apart * len(sources),
        out_specs=[whole] * 2 + apart * len(slots),
        scratch_shapes=[
            pltpu.VMEM((D, 2 * F), jnp.bfloat16),
            pltpu.VMEM((F, D), jnp.bfloat16),
            pltpu.VMEM(outgoing.shape, jnp.bfloat16),
            pltpu.SemaphoreType.DMA((PLANES * (1 + F // rows),)),
            pltpu.SemaphoreType.DMA((16,)),
            pltpu.SemaphoreType.DMA((16,)),
        ]
        + swap_scratch(len(pieces)),
        compiler_params=pltpu.CompilerParams(
            vmem_limit_bytes=56 * 1024 * 1024,
            collective_id=5 if pieces else 2,
            has_side_effects=True,
        ),
        cost_estimate=pl.CostEstimate(
            flops=slot_total * D * F * 6, bytes_accessed=150 * 1024 * 1024, transcendentals=1 << 19
        ),
    )(outgoing, *sources)


def backward_exchange_kernel(
    part_count,
    capacity,
    outgoing_ref,
    received_ref,
    grad_ref,
    returned_ref,
    spread_back_ref,
    probs_ref,
    ffn_ref,
    *refs,
):
    part_refs, refs = refs[:part_count], refs[part_count:]
    out_refs, refs = refs[:part_count], refs[part_count:]
    (
        back_ref,
        low_ref,
        router_grad_ref,
        pull_ref,
        gate_grad_ref,
        activated_ref,
        input_grad_ref,
        up_ref,
        down_ref,
        up_grad_ref,
        down_grad_ref,
        copy_sem,
        send_sem,
        recv_sem,
    ) = refs
    partners, groups = plane_partners()
    greet(partners[1:])
    copies = exchange_out(outgoing_ref, pull_ref, send_sem, recv_sem, partners, groups)
    fetch_expert(part_places(part_count), part_refs, up_ref, down_ref, copy_sem)
    back = {}
    for pair in (0, 3, 2, 1):
        rows = slice(pair * 2 * capacity, (pair + 1) * 2 * capacity)
        gate_part, up_part, sigmoid = silu_parts(
            dot_nn(two_blocks(received_ref, pair), up_ref[...])
        )
        side = gate_part * sigmoid
        activated_ref[rows, :] = (side * up_part).astype(jnp.bfloat16)
        slope = up_part * sigmoid * (1.0 + gate_part * (1.0 - sigmoid))
        for turn in (2 * pair, 2 * pair + 1):
            if turn:
                copies[turn].wait_recv()
        pulled = dot_nt(two_blocks(pull_ref, pair), down_ref[...]).astype(jnp.bfloat16)
        pulled = pulled.astype(jnp.float32)
        gate_grad_ref[rows, :F] = (pulled * slope).astype(jnp.bfloat16)
        gate_grad_ref[rows, F:] = (pulled * side).astype(jnp.bfloat16)
        put_two(
            input_grad_ref, pair, dot_nt(gate_grad_ref[rows, :], up_ref[...]).astype(jnp.bfloat16)
        )
        for turn in (2 * pair, 2 * pair + 1):
            if turn:
                back[turn] = push(
                    input_grad_ref.at[turn],
                    back_ref.at[groups[0]],
                    send_sem,
                    recv_sem,
                    8 + turn,
                    partners[turn],
                )
        if pair == 0:
            router_kernel(
                capacity,
                grad_ref,
                returned_ref,
                spread_back_ref,
                probs_ref,
                ffn_ref,
                low_ref,
                router_grad_ref,
            )
    back_ref[groups[0]] = input_grad_ref[0]
    block = 256

    @pl.loop(0, D // block)
    def _(step):
        columns = pl.ds(pl.multiple_of(step * block, block), block)
        up_grad_ref[columns, :] = dot_tn(
            flat_rows(received_ref[:, :, columns]), gate_grad_ref[...]
        ).astype(jnp.bfloat16)

    @pl.loop(0, F // block)
    def _(step):
        columns = pl.ds(pl.multiple_of(step * block, block), block)
        down_grad_ref[columns, :] = dot_tn(
            activated_ref[:, columns], flat_rows(pull_ref[...])
        ).astype(jnp.bfloat16)

    rows = out_refs[0].shape[0]
    for out_ref, own_place in zip(out_refs, part_places(part_count)):
        place = pl.multiple_of(own_place * rows, rows)
        out_ref[:, : 2 * F] = up_grad_ref[pl.ds(place, rows), :]
        for part in range(F // rows):
            out_ref[:, 2 * F + part * rows : 2 * F + (part + 1) * rows] = down_grad_ref[
                part * rows : (part + 1) * rows, pl.ds(place, rows)
            ]
    for turn in range(1, 8):
        copies[turn].wait_send()
        back[turn].wait()


def backward_exchange(
    capacity, outgoing, received, grad, returned, spread_back, probs, ffn, parts
):
    whole, _, apart, scratch = expert_specs(parts)
    slot_total = outgoing.shape[0] * outgoing.shape[1]
    piece_rows = parts[0].shape[0]
    seq_len = grad.shape[0]
    low = jnp.bfloat16
    return pl.pallas_call(
        functools.partial(backward_exchange_kernel, len(parts), capacity),
        out_shape=[jax.ShapeDtypeStruct((piece_rows, 3 * F), low)] * len(parts)
        + [
            jax.ShapeDtypeStruct(outgoing.shape, low),
            jax.ShapeDtypeStruct((seq_len, LANES), low),
            jax.ShapeDtypeStruct((D, LANES), jnp.float32),
        ],
        in_specs=[whole] * 7 + apart,
        out_specs=[whole] * (len(parts) + 3),
        scratch_shapes=[
            pltpu.VMEM(outgoing.shape, low),
            pltpu.VMEM((slot_total, 2 * F), low),
            pltpu.VMEM((slot_total, F), low),
            pltpu.VMEM(outgoing.shape, low),
        ]
        + scratch[:2]
        + scratch[:2]
        + [
            scratch[2],
            pltpu.SemaphoreType.DMA((16,)),
            pltpu.SemaphoreType.DMA((16,)),
        ],
        compiler_params=pltpu.CompilerParams(
            vmem_limit_bytes=58 * 1024 * 1024, collective_id=3, has_side_effects=True
        ),
        cost_estimate=pl.CostEstimate(
            flops=slot_total * D * F * 18,
            bytes_accessed=180 * 1024 * 1024,
            transcendentals=1 << 19,
        ),
    )(outgoing, received, grad, returned, spread_back, probs, ffn, *parts)


RING = ("z", "x", "y", "c")


def owner_sum_kernel(
    layers,
    *refs,
):
    grads, refs = refs[:layers], refs[layers:]
    (
        out_ref,
        own_ref,
        core_ref,
        near_ref,
        joined_ref,
        turn_ref,
        last_ref,
        got_ref,
        local_sem,
        send_sem,
        recv_sem,
    ) = refs
    at = {name: lax.axis_index(name) for name in RING}
    planes = lax.axis_size("z")
    barrier = pltpu.get_barrier_semaphore()
    partners = [{name: 1 - at[name]} for name in ("c", "x", "y")]
    partners += [{"z": lax.rem(at["z"] + turn, planes)} for turn in range(1, planes)]
    for partner in partners:
        pl.semaphore_signal(
            barrier, inc=1, device_id=partner, device_id_type=pl.DeviceIdType.MESH
        )
    pl.semaphore_wait(barrier, len(partners))

    width = own_ref.shape[-1]
    half = width // 2
    per_layer = grads[0].shape[-1] // width
    chunk_count = layers * per_layer
    copies = {}

    def send(chunk_index, step, source, target, partner):
        place = chunk_index * 8 + step
        copy = pltpu.make_async_remote_copy(
            src_ref=source,
            dst_ref=target,
            send_sem=send_sem.at[place],
            recv_sem=recv_sem.at[place],
            device_id=partner,
            device_id_type=pl.DeviceIdType.MESH,
        )
        copy.start()
        copies[place] = copy

    def arrived(chunk_index, *steps):
        for step in steps:
            copies[chunk_index * 8 + step].wait()

    def source_of(chunk_index, core):
        layer, part = chunk_index // per_layer, chunk_index % per_layer
        return grads[layer].at[:, :, :, core, :, pl.ds(part * width, width)]

    def added(left, right):
        return (left.astype(jnp.float32) + right.astype(jnp.float32)).astype(jnp.bfloat16)

    local = []
    for index in range(chunk_count):
        copy = pltpu.make_async_copy(
            source_of(index, at["c"]), own_ref.at[index], local_sem.at[index]
        )
        copy.start()
        local.append(copy)
        send(index, 0, source_of(index, 1 - at["c"]), core_ref.at[index], partners[0])

    def stage_core(index):
        local[index].wait()
        arrived(index, 0)
        for plane in range(planes):
            own_ref[index, plane] = added(own_ref[index, plane], core_ref[index, plane])
        send(
            index,
            1,
            own_ref.at[index, :, 1 - at["x"], :, :, pl.ds(0, half)],
            near_ref.at[index, 0],
            partners[1],
        )
        send(
            index,
            2,
            own_ref.at[index, :, :, 1 - at["y"], :, pl.ds(half, half)],
            near_ref.at[index, 1],
            partners[2],
        )

    def stage_near(index):
        arrived(index, 1, 2)
        for plane in range(planes):
            for other in range(2):
                joined_ref[index, 0, plane, other] = added(
                    own_ref[index, plane, at["x"], other, :, :half],
                    near_ref[index, 0, plane, other],
                )
                joined_ref[index, 1, plane, other] = added(
                    own_ref[index, plane, other, at["y"], :, half:],
                    near_ref[index, 1, plane, other],
                )
        send(
            index,
            3,
            joined_ref.at[index, 0, :, 1 - at["y"]],
            turn_ref.at[index, 0],
            partners[2],
        )
        send(
            index,
            4,
            joined_ref.at[index, 1, :, 1 - at["x"]],
            turn_ref.at[index, 1],
            partners[1],
        )

    def stage_turn(index):
        arrived(index, 3, 4)
        for plane in range(planes):
            last_ref[index, plane, :, :half] = added(
                joined_ref[index, 0, plane, at["y"]], turn_ref[index, 0, plane]
            )
            last_ref[index, plane, :, half:] = added(
                joined_ref[index, 1, plane, at["x"]], turn_ref[index, 1, plane]
            )
        for turn in range(1, planes):
            send(
                index,
                4 + turn,
                last_ref.at[index, partners[2 + turn]["z"]],
                got_ref.at[index, turn - 1],
                partners[2 + turn],
            )

    def stage_planes(index):
        arrived(index, *[4 + turn for turn in range(1, planes)])
        total = last_ref[index, at["z"]].astype(jnp.float32)
        for turn in range(1, planes):
            total = total + got_ref[index, turn - 1].astype(jnp.float32)
        layer, part = index // per_layer, index % per_layer
        out_ref[layer, :, part * width : (part + 1) * width] = total

    stages = (stage_core, stage_near, stage_turn, stage_planes)
    for step in range(chunk_count + len(stages) - 1):
        for number, stage in enumerate(stages):
            if 0 <= step - number < chunk_count:
                stage(step - number)


def owner_sums(grads, width=2048):
    layers = len(grads)
    sizes = [lax.axis_size(name) for name in RING]
    rows, columns = grads[0].shape
    own_rows = rows // (sizes[0] * sizes[1] * sizes[2] * sizes[3])
    chunks = layers * columns // width
    blocks = [grad.reshape(*sizes, own_rows, columns) for grad in grads]
    half = width // 2
    low = jnp.bfloat16
    return pl.pallas_call(
        functools.partial(owner_sum_kernel, layers),
        out_shape=jax.ShapeDtypeStruct((layers, own_rows, columns), jnp.float32),
        in_specs=[pl.BlockSpec(memory_space=pl.ANY)] * layers,
        out_specs=pl.BlockSpec(memory_space=pltpu.VMEM),
        scratch_shapes=[
            pltpu.VMEM((chunks, sizes[0], 2, 2, own_rows, width), low),
            pltpu.VMEM((chunks, sizes[0], 2, 2, own_rows, width), low),
            pltpu.VMEM((chunks, 2, sizes[0], 2, own_rows, half), low),
            pltpu.VMEM((chunks, 2, sizes[0], 2, own_rows, half), low),
            pltpu.VMEM((chunks, 2, sizes[0], own_rows, half), low),
            pltpu.VMEM((chunks, sizes[0], own_rows, width), low),
            pltpu.VMEM((chunks, sizes[0] - 1, own_rows, width), low),
            pltpu.SemaphoreType.DMA((chunks,)),
            pltpu.SemaphoreType.DMA((chunks * 8,)),
            pltpu.SemaphoreType.DMA((chunks * 8,)),
        ],
        compiler_params=pltpu.CompilerParams(
            vmem_limit_bytes=56 * 1024 * 1024, collective_id=1, has_side_effects=True
        ),
        cost_estimate=pl.CostEstimate(
            flops=1 << 26, bytes_accessed=200 * 1024 * 1024, transcendentals=0
        ),
    )(*blocks)


def adam_step(weight, mean_old, square_old, gradient):
    mean_new = BETA_ONE * mean_old + (1.0 - BETA_ONE) * gradient
    square_new = BETA_TWO * square_old + (1.0 - BETA_TWO) * gradient * gradient
    bias_one = 1.0 - BETA_ONE**ADAM_STEP
    bias_two = 1.0 - BETA_TWO**ADAM_STEP
    update = -LEARN_RATE * (
        mean_new / bias_one / (jnp.sqrt(square_new / bias_two) + ADAM_EPS) + DECAY_RATE * weight
    )
    return (mean_new, square_new, update)


VOCAB_BLOCK = 2048
VOCAB_PART = 512


def embedding_kernel(
    row_ref,
    low_ref,
    high_ref,
    arrived_ref,
    word_ref,
    group_ref,
    weight_ref,
    mean_ref,
    square_ref,
    mean_out_ref,
    square_out_ref,
    update_ref,
    wide_ref,
    sorted_ref,
    turned_ref,
    total_ref,
):
    step = pl.program_id(0)
    device_count = arrived_ref.shape[0]
    token_count = sorted_ref.shape[0]
    columns = weight_ref.shape[0]
    groups = LANES // columns

    @pl.when(step == 0)
    def _():
        for part in range(wide_ref.shape[0] // device_count):
            wide_ref[part * device_count : (part + 1) * device_count, :] = arrived_ref[
                :, part * LANES : (part + 1) * LANES
            ].astype(jnp.float32)

        @pl.loop(0, token_count // 32)
        def _(block):
            start = pl.multiple_of(block * 32, 32)
            for place in range(32):
                sorted_ref[pl.ds(start + place, 1), :] = wide_ref[pl.ds(row_ref[start + place], 1), :]

        row_place = lax.broadcasted_iota(jnp.int32, (LANES, LANES), 0)
        lane = lax.broadcasted_iota(jnp.int32, (LANES, LANES), 1)
        same = jnp.where(row_place == lane, 1.0, 0.0).astype(jnp.bfloat16)

        @pl.loop(0, token_count // LANES)
        def _(block):
            rows = pl.ds(pl.multiple_of(block * LANES, LANES), LANES)
            turned = dot_nt(same, sorted_ref[rows, :].astype(jnp.bfloat16))
            group = group_ref[pl.ds(block, 1), :]
            kept = jnp.where(group == 0, turned[:columns, :], 0.0)
            for place in range(1, groups):
                kept += jnp.where(
                    group == place, turned[place * columns : (place + 1) * columns, :], 0.0
                )
            turned_ref[:, rows] = kept.astype(jnp.bfloat16)

    for part in range(VOCAB_BLOCK // VOCAB_PART):
        total_ref[...] = jnp.zeros_like(total_ref)
        place = step * (VOCAB_BLOCK // VOCAB_PART) + part
        first = place * VOCAB_PART

        @pl.loop(low_ref[place], high_ref[place])
        def _(block):
            rows = pl.ds(pl.multiple_of(block * LANES, LANES), LANES)
            word = lax.broadcasted_iota(jnp.int32, (VOCAB_PART, LANES), 0)
            hit = word == word_ref[pl.ds(block, 1), :] - first
            hit = jnp.where(hit, 1.0, 0.0).astype(jnp.bfloat16)
            total_ref[...] += dot_nt(turned_ref[:, rows], hit)

        gradient = total_ref[...]
        words = slice(part * VOCAB_PART, (part + 1) * VOCAB_PART)
        mean_new, square_new, update = adam_step(
            weight_ref[:, words], mean_ref[:, words], square_ref[:, words], gradient
        )
        mean_out_ref[:, words] = mean_new
        square_out_ref[:, words] = square_new
        update_ref[:, words] = update


def token_order(tokens, seq_len, vocabulary, groups):
    count = tokens.shape[0]
    devices = count // seq_len
    keys = lax.sort(tokens * count + jnp.arange(count, dtype=jnp.int32))
    words, origin = keys // count, keys % count
    device, place = origin // seq_len, origin % seq_len
    row = (place // groups) * devices + device
    words = words.reshape(count // LANES, LANES)
    group = (place % groups).reshape(count // LANES, LANES)
    steps = -(-vocabulary // VOCAB_BLOCK) * (VOCAB_BLOCK // VOCAB_PART)
    edges = jnp.arange(steps + 1, dtype=jnp.int32) * VOCAB_PART
    below = jnp.sum((tokens[None, :] < edges[:, None]).astype(jnp.int32), axis=1)
    low = below[:-1] // LANES
    high = (below[1:] + LANES - 1) // LANES
    high = jnp.where(below[1:] > below[:-1], high, low)
    return row, low, high, words, group


def embedding_update_of(order, arrived, weight, mean, square):
    row, low, high, words, group = order
    count = row.shape[0]
    columns, vocabulary = weight.shape
    block = pl.BlockSpec((columns, VOCAB_BLOCK), lambda step: (0, step))
    whole = pl.BlockSpec(memory_space=pltpu.VMEM)
    scalar = pl.BlockSpec(memory_space=pltpu.SMEM)
    wide = count * columns // LANES
    return pl.pallas_call(
        embedding_kernel,
        grid=(-(-vocabulary // VOCAB_BLOCK),),
        out_shape=[jax.ShapeDtypeStruct(weight.shape, jnp.float32)] * 3,
        in_specs=[scalar] * 3 + [whole] * 3 + [block] * 3,
        out_specs=[block] * 3,
        scratch_shapes=[
            pltpu.VMEM((wide, LANES), jnp.float32),
            pltpu.VMEM((count, LANES), jnp.float32),
            pltpu.VMEM((columns, count), jnp.bfloat16),
            pltpu.VMEM((columns, VOCAB_PART), jnp.float32),
        ],
        compiler_params=pltpu.CompilerParams(vmem_limit_bytes=48 * 1024 * 1024),
        cost_estimate=pl.CostEstimate(
            flops=1 << 32, bytes_accessed=50 * 1024 * 1024, transcendentals=1 << 20
        ),
    )(row, low, high, arrived, words, group, weight, mean, square)


def shards(
    tokens,
    prefix,
    routes,
    picked,
    loss_ids,
    teacher_logits,
    embedding,
    embedding_mean,
    embedding_square,
    attention,
    attention_mean,
    attention_square,
    router,
    router_mean,
    router_square,
    norm_gains,
    gains_mean,
    gains_square,
    expert_up,
    upward_mean,
    upward_square,
    expert_down,
    downward_mean,
    downward_square,
    output_table,
    table_mean,
    table_square,
):
    devices_all = lax.axis_size(AXES)
    me_all = lax.axis_index(AXES)
    row_groups = lax.axis_size("h")
    columns_x = lax.axis_size("x")
    seq_len = routes.shape[0]
    layer_count = attention.shape[0]
    experts_all = router.shape[2]
    capacity = 9 * seq_len * TOPK // (8 * experts_all)
    column_count = embedding.shape[1]
    prefix_len = prefix[0]
    slot_total = experts_all * capacity
    piece_rows = expert_up.shape[2]
    gain_count = norm_gains.shape[0]
    me_plane = lax.axis_index("z")
    member_place = jnp.arange(experts_all, dtype=jnp.int32)
    member_part = member_place % PLANES
    group_order = (
        (member_part // 2 + me_plane) % 2 * 2 + member_part % 2
    ) * columns_x + member_place // PLANES
    expert_plane = member_place // columns_x
    group_back = (
        member_place % columns_x * PLANES
        + (expert_plane // 2 + me_plane) % 2 * 2
        + expert_plane % 2
    )


    head_low = output_table.astype(jnp.bfloat16)
    vocab_local = head_low.shape[0]
    teacher_log = jax.nn.log_softmax(teacher_logits, axis=1)
    teacher_prob = jnp.exp(teacher_log)
    position_count = loss_ids.shape[0]
    teacher_mass = jnp.sum(teacher_prob, axis=1)
    coefficients = jnp.concatenate(
        [jnp.ones((position_count, 1), jnp.float32), teacher_prob], axis=1
    )
    table_low = embedding.astype(jnp.bfloat16)
    looked_up = jnp.take(table_low, tokens, axis=0, mode="clip").reshape(devices_all, seq_len * column_count)
    attention_low = lax.all_gather(attention.astype(jnp.bfloat16), AXES, axis=1, tiled=True)
    small_count = gain_count + layer_count * experts_all
    small = jnp.concatenate(
        [norm_gains.T, router.transpose(1, 0, 2).reshape(column_count, layer_count * experts_all)],
        axis=1,
    ).astype(jnp.bfloat16)
    small = jnp.broadcast_to(
        small.reshape(1, column_count * small_count), (devices_all, column_count * small_count)
    )
    arrived_rows = send_all(jnp.concatenate([looked_up, small], axis=1))
    fits_sum = [lax.axis_size(name) for name in AXES] == [PLANES, 2, 1, 2, 2]

    expert_parts, expert_pieces = [], []
    for layer_index in range(layer_count):
        down_piece = (
            expert_down[0, layer_index]
            .reshape(F // piece_rows, piece_rows, piece_rows)
            .transpose(1, 0, 2)
            .reshape(piece_rows, F)
        )
        piece = jnp.concatenate([expert_up[0, layer_index], down_piece], axis=1).astype(
            jnp.bfloat16
        )
        expert_pieces.append(piece)
    if not fits_sum:
        expert_parts.append(spread_experts(expert_pieces[0], row_groups))

    hidden = (
        arrived_rows[:, : seq_len * column_count]
        .reshape(devices_all, seq_len, column_count)
        .transpose(1, 0, 2)
        .reshape(seq_len, D)
        .astype(jnp.float32)
    )
    small_all = arrived_rows[:, seq_len * column_count :].reshape(D, small_count)
    gain_rows = jnp.pad(
        small_all[:, :gain_count].T.astype(jnp.float32), ((0, 16 - gain_count), (0, 0))
    )
    router_low = jnp.pad(
        small_all[:, gain_count:]
        .reshape(D, layer_count, experts_all)
        .transpose(1, 0, 2)[:, :, group_order],
        ((0, 0), (0, 0), (0, LANES - experts_all)),
    )

    member = jnp.any(routes[:, :, None] == group_order[None, None, :], axis=1)
    before = jnp.dot(
        jnp.tril(jnp.ones((seq_len, seq_len), jnp.bfloat16), -1),
        member.astype(jnp.bfloat16),
        preferred_element_type=jnp.float32,
    ).astype(jnp.int32)
    spread = (
        (before.T[:, None, :] == jnp.arange(capacity, dtype=jnp.int32)[None, :, None])
        & member.T[:, None, :]
    ).astype(jnp.bfloat16)
    spread_flat = spread.reshape(slot_total, seq_len)
    spread_back = spread_flat.T
    kept = jnp.pad(
        (member & (before < capacity)).astype(jnp.float32), ((0, 0), (0, LANES - experts_all))
    )
    turns = turn_tables(seq_len)
    places = jnp.stack([piece_place(turn, row_groups) for turn in all_turns(row_groups)]).astype(
        jnp.int32
    )

    stored = []
    extra = ()
    for layer_index in range(layer_count):
        saved = forward_layer(
            layer_index,
            capacity,
            experts_all,
            prefix,
            hidden,
            extra,
            attention_low,
            gain_rows,
            turns,
            router_low,
            kept,
            spread_flat,
            spread_back,
        )
        hidden = saved[6]
        gates, outgoing = saved[9], saved[10]
        blocks = outgoing.reshape(experts_all, capacity, D)
        if fits_sum:
            here = expert_parts[layer_index] if layer_index < len(expert_parts) else ()
            ahead = () if here else expert_pieces[layer_index : layer_index + 2]
            returned, received, *arrived = forward_exchange(blocks, here, ahead)
            for place in range(len(ahead)):
                expert_parts.append(arrived[place * PLANES : (place + 1) * PLANES])
        else:
            for piece in expert_pieces[layer_index + 1 : layer_index + 2]:
                expert_parts.append(spread_experts(piece, row_groups))
            received = send_plane(blocks).reshape(slot_total, D)
            produced = run_expert(places, received, expert_parts[layer_index])
            returned = send_plane(produced.reshape(experts_all, capacity, D))
        returned = returned.reshape(slot_total, D)
        stored.append((saved, received, returned))
        extra = (gates, returned)

    order = token_order(tokens, seq_len, embedding.shape[0], LANES // column_count)
    local_ids = loss_ids - me_all * vocab_local
    vocab_place = jnp.arange(vocab_local, dtype=jnp.int32)
    marked = jnp.sum(
        jnp.where(
            local_ids[:, :, None] == vocab_place[None, None, :], coefficients[:, :, None], 0.0
        ),
        axis=1,
    )
    marked_pull = jnp.dot(
        marked.astype(jnp.bfloat16), head_low, preferred_element_type=jnp.float32
    )
    own_count = position_count // devices_all

    final_rows, final_low = final_rows_of(
        capacity,
        4 * layer_count,
        picked,
        hidden,
        *extra,
        spread_flat,
        spread_back,
        gain_rows,
    )
    all_rows = send_all(jnp.broadcast_to(final_low[None], (devices_all, own_count, D))).reshape(
        position_count, D
    )
    logits = jnp.einsum("pd,vd->pv", all_rows, head_low, preferred_element_type=jnp.float32)
    local_peak = jnp.max(logits, axis=1)
    local_exp = jnp.exp(logits - local_peak[:, None])
    local_sum = jnp.sum(local_exp, axis=1)
    local_dot = jnp.sum(marked * logits, axis=1)
    pull = jnp.dot(local_exp.astype(jnp.bfloat16), head_low, preferred_element_type=jnp.float32)
    stats = jnp.stack(
        three_terms(local_peak) + three_terms(local_sum) + three_terms(local_dot), axis=1
    )
    stats = jnp.pad(stats, ((0, 0), (0, 128 - stats.shape[1])))
    pull_sent = jnp.concatenate([pull, marked_pull, stats], axis=1).astype(jnp.bfloat16)
    pull_got = send_all(pull_sent.reshape(devices_all, own_count, 2 * D + LANES))
    entropy = jnp.sum(teacher_prob * teacher_log, axis=1)
    own = lax.dynamic_slice_in_dim(
        jnp.pad(jnp.stack([teacher_mass, entropy], axis=1), ((0, 0), (0, LANES - 2))),
        me_all * own_count,
        own_count,
    )
    grad_hidden, sent_back, final_gain_grad, own_stats = first_pull(
        capacity,
        4 * layer_count,
        position_count,
        picked,
        pull_got,
        own,
        final_rows,
        gain_rows,
        spread_flat,
        extra[0],
    )
    final_gain_grad = final_gain_grad[0]
    gain_parts = [None] * (4 * layer_count) + [final_gain_grad]
    attention_parts = [None] * layer_count
    router_parts = [None] * layer_count
    piece_parts = [None] * layer_count
    for layer_index in reversed(range(layer_count)):
        saved, received, returned = stored[layer_index]
        hidden_in, projected, queries, keys, values, attended, middle, ffn_low, probs = saved[:9]
        upper = layer_index + 1 if layer_index + 1 < layer_count else None
        blocks = sent_back.reshape(experts_all, capacity, D)
        if fits_sum:
            *grad_pieces, back_inputs, logit_low, router_parts[layer_index] = backward_exchange(
                capacity,
                blocks,
                received,
                grad_hidden,
                returned,
                spread_back,
                probs,
                ffn_low,
                expert_parts[layer_index],
            )
        else:
            output_grad = send_plane(blocks).reshape(slot_total, D)
            logit_low, router_parts[layer_index] = router_back(
                capacity, grad_hidden, returned, spread_back, probs, ffn_low
            )
            input_grad, gate_grad, activated = run_expert_back(
                places, received, output_grad, expert_parts[layer_index]
            )
            back_inputs = send_plane(input_grad.reshape(experts_all, capacity, D))
            grad_pieces = run_expert_grad(
                places, received, output_grad, gate_grad, activated, piece_rows
            )
        back_inputs = back_inputs.reshape(slot_total, D)
        if upper is None:
            own_stats, back_inputs = tie(own_stats, back_inputs)
        if upper is not None:
            piece_parts[upper][1:], back_inputs = tie(piece_parts[upper][1:], back_inputs)
        if layer_index > 0:
            piece_parts[layer_index] = return_expert_grads(grad_pieces, row_groups)
        else:
            turns_all = len(grad_pieces)
            piece_parts[0] = []
        lower = (spread_flat, stored[layer_index - 1][0][9]) if layer_index > 0 else ()
        results = backward_layer(
            layer_index,
            capacity,
            prefix,
            grad_hidden,
            back_inputs,
            logit_low,
            hidden_in,
            projected,
            queries,
            keys,
            values,
            attended,
            middle,
            attention_low,
            gain_rows,
            turns,
            router_low,
            spread_back,
            lower,
        )
        grad_hidden, weight_grad, gain_grads = results[:3]
        gain_parts[4 * layer_index : 4 * layer_index + 4] = list(gain_grads[:4])
        if layer_index > 0:
            sent_back = results[3]
            piece_parts[layer_index][:1], sent_back = tie(piece_parts[layer_index][:1], sent_back)
        attention_parts[layer_index] = weight_grad
        if not fits_sum:
            attention_parts[layer_index] = lax.psum_scatter(
                weight_grad, AXES, scatter_dimension=0, tiled=True
            ).astype(jnp.float32)

    log_norm_own, loss_own = own_stats[:, 0], own_stats[:, 1]
    spread_stats = jnp.concatenate([log_norm_own, loss_own]).reshape(1, 2 * own_count)
    stats_all = send_all(jnp.broadcast_to(spread_stats, (devices_all, 2 * own_count)))
    log_norm = stats_all[:, :own_count].reshape(position_count)
    loss_value = jnp.sum(stats_all[:, own_count:]) / position_count
    grad_logits = (
        jnp.exp(logits - log_norm[:, None]) * (1.0 + teacher_mass)[:, None] - marked
    ) / position_count
    table_grad = jnp.einsum(
        "pv,pd->vd",
        grad_logits.astype(jnp.bfloat16),
        all_rows,
        preferred_element_type=jnp.float32,
    )

    sending = (
        grad_hidden.astype(jnp.bfloat16)
        .reshape(seq_len, devices_all, column_count)
        .transpose(1, 0, 2)
        .reshape(devices_all, seq_len * column_count)
    )
    small_grads = jnp.concatenate(
        [jnp.stack(gain_parts, axis=1)] + [part[:, group_back] for part in router_parts], axis=1
    ).astype(jnp.bfloat16)
    arrived_grads = send_all(
        jnp.concatenate(
            [sending, small_grads.reshape(devices_all, column_count * small_count)], axis=1
        )
    )
    if fits_sum:
        attention_parts = list(owner_sums(attention_parts[::-1], 2048))[::-1]
    grad_pieces, arrived_grads, attention_parts = lax.optimization_barrier(
        (grad_pieces, arrived_grads, attention_parts)
    )
    late = range(turns_all)
    piece_parts[0] = piece_parts[0] + return_expert_grads(grad_pieces, row_groups, late)
    embedding_next = embedding_update_of(
        order,
        arrived_grads[:, : seq_len * column_count],
        embedding.T,
        embedding_mean.T,
        embedding_square.T,
    )
    piece_parts[0], embedding_next = tie(piece_parts[0], embedding_next)
    up_parts, down_parts = [], []
    for parts in piece_parts:
        piece_grad = scatter_sum(parts)
        up_parts.append(piece_grad[:, : 2 * F])
        down_parts.append(
            piece_grad[:, 2 * F :]
            .reshape(piece_rows, F // piece_rows, piece_rows)
            .transpose(1, 0, 2)
            .reshape(F, piece_rows)
        )
    small_total = jnp.sum(
        arrived_grads[:, seq_len * column_count :].astype(jnp.float32), axis=0
    ).reshape(column_count, small_count)
    gains_grad = small_total[:, :gain_count].T
    router_grad = (
        small_total[:, gain_count:]
        .reshape(column_count, layer_count, experts_all)
        .transpose(1, 0, 2)
    )
    attention_grad = jnp.stack(attention_parts)
    upward_grad = jnp.stack(up_parts)[None]
    downward_grad = jnp.stack(down_parts)[None]
    embedding_mean_next, embedding_square_next, embedding_update = [
        part.T for part in embedding_next
    ]
    attention_mean_next, attention_square_next, attention_update = adam_step(
        attention, attention_mean, attention_square, attention_grad
    )
    router_mean_next, router_square_next, router_update = adam_step(
        router, router_mean, router_square, router_grad
    )
    gains_mean_next, gains_square_next, gains_update = adam_step(
        norm_gains, gains_mean, gains_square, gains_grad
    )
    upward_mean_next, upward_square_next, upward_update = adam_step(
        expert_up, upward_mean, upward_square, upward_grad
    )
    downward_mean_next, downward_square_next, downward_update = adam_step(
        expert_down, downward_mean, downward_square, downward_grad
    )
    table_mean_next, table_square_next, table_update = adam_step(
        output_table, table_mean, table_square, table_grad
    )
    return (
        loss_value,
        embedding_mean_next,
        embedding_square_next,
        embedding_update,
        attention_mean_next,
        attention_square_next,
        attention_update,
        router_mean_next,
        router_square_next,
        router_update,
        gains_mean_next,
        gains_square_next,
        gains_update,
        upward_mean_next,
        upward_square_next,
        upward_update,
        downward_mean_next,
        downward_square_next,
        downward_update,
        table_mean_next,
        table_square_next,
        table_update,
    )


def solution(mesh):
    expert_count, shard_count = mesh.devices.shape
    mesh = Mesh(
        mesh.devices.reshape(PLANES, expert_count // PLANES, shard_count // 4, 2, 2), AXES
    )
    return jax.shard_map(
        shards,
        mesh=mesh,
        in_specs=(
            P(),
            P(AXES),
            P(AXES, None),
            P(AXES),
            P(),
            P(),
            P(None, AXES),
            P(None, AXES),
            P(None, AXES),
            P(None, AXES, None),
            P(None, AXES, None),
            P(None, AXES, None),
            P(None, AXES, None),
            P(None, AXES, None),
            P(None, AXES, None),
            P(None, AXES),
            P(None, AXES),
            P(None, AXES),
            P(("z", "x"), None, ("h", "y", "c"), None),
            P(("z", "x"), None, ("h", "y", "c"), None),
            P(("z", "x"), None, ("h", "y", "c"), None),
            P(("z", "x"), None, None, ("h", "y", "c")),
            P(("z", "x"), None, None, ("h", "y", "c")),
            P(("z", "x"), None, None, ("h", "y", "c")),
            P(AXES, None),
            P(AXES, None),
            P(AXES, None),
        ),
        out_specs=(
            P(),
            P(None, AXES),
            P(None, AXES),
            P(None, AXES),
            P(None, AXES, None),
            P(None, AXES, None),
            P(None, AXES, None),
            P(None, AXES, None),
            P(None, AXES, None),
            P(None, AXES, None),
            P(None, AXES),
            P(None, AXES),
            P(None, AXES),
            P(("z", "x"), None, ("h", "y", "c"), None),
            P(("z", "x"), None, ("h", "y", "c"), None),
            P(("z", "x"), None, ("h", "y", "c"), None),
            P(("z", "x"), None, None, ("h", "y", "c")),
            P(("z", "x"), None, None, ("h", "y", "c")),
            P(("z", "x"), None, None, ("h", "y", "c")),
            P(AXES, None),
            P(AXES, None),
            P(AXES, None),
        ),
        check_vma=False,
    )
```
